256 devices in a mesh: dp: 4 (over y), expert: 8 (over z), tensor: 8 (over x, core).
Axes of the slice: x: 4, y: 4, z: 8, core: 2. Of those that a mesh axis runs over, the one named last changes fastest.
Arguments:
- grad_out: bfloat16 [4096, 6144], P(('dp', 'expert')), may hold values from -1.5 to 1.5
- routes: int32 [4096, 2], P(('dp', 'expert')), may hold values from 0 to 7, as said below
- combine: bfloat16 [4096, 2], P(('dp', 'expert')), may hold values from 0.099609375 to 0.8984375
- saved_hidden: bfloat16 [4, 8, 384, 12288], P(None, 'expert', None, ('dp', 'tensor')), may hold values from -6 to 6
- down_weight: bfloat16 [8, 12288, 6144], P('expert', ('dp', 'tensor')), may hold values from -0.0546875 to 0.0546875
Outputs:
- grad_hidden: bfloat16 [4, 8, 384, 12288], P(None, 'expert', None, ('dp', 'tensor'))
- grad_down: bfloat16 [8, 12288, 6144], P('expert', ('dp', 'tensor'))
- grad_combine: float32 [4096, 2], P(('dp', 'expert'))
The draws below stay inside these ranges and needn't reach their ends.
Inputs may be any that keep to these rules, and one draw needn't show every extreme that they name: `routes`: the two experts of a token differ. Among the 128 tokens of one group no expert is named more than 48 times, and in every replica one expert is named exactly 48 times by the tokens of each of its groups.
All inputs are finite; a program needn't handle non-finite values.
Results may differ from the reference program's by a relative error of at most 0.0049.
Values may be sent and summed in bfloat16 or wider, within the bound.
No kernel may reach another device: no remote copies, remote signals or barrier semaphores. Data moves between devices by JAX's collectives and lax.ppermute only.
A program may use at most 192 MiB of HBM per device.

```python
import jax
import jax.numpy as jnp
from jax import lax

D = 6144
FFW = 12288
TOK_DEV = 128
MOST = 48
EXPERTS = 8
CAPR = 384
TOKENS = 4096
N_DP = 4
N_EXPERT = 8


def draw_routes(key, part):
    key = jax.random.fold_in(key, 17)
    key_list = jax.random.split(key, 5)
    blocks = TOKENS // TOK_DEV
    others = EXPERTS - 1
    hot_replica = jax.random.randint(key_list[0], (N_DP,), 0, EXPERTS)
    hot_expert = jnp.repeat(hot_replica, blocks // N_DP)
    orders = jax.vmap(lambda sub: jax.random.permutation(sub, others))(jax.random.split(key_list[1], blocks)).astype(jnp.int32)
    offset = jax.random.randint(key_list[2], (blocks, 1), 0, others)
    places = jax.vmap(lambda sub: jax.random.permutation(sub, TOK_DEV))(jax.random.split(key_list[3], blocks)).astype(jnp.int32)
    flip_bits = jax.random.randint(key_list[4], (blocks, TOK_DEV), 0, 2)
    position = jnp.arange(TOK_DEV, dtype=jnp.int32)[None, :]
    is_hot = position < MOST
    first_index = 2 * (position - MOST)
    second_index = jnp.where(is_hot, 2 * (TOK_DEV - MOST) + position, first_index + 1)

    def expert_of(index):
        index = jnp.broadcast_to(index, (blocks, TOK_DEV))
        chosen = jnp.take_along_axis(orders, (index + offset) % others, axis=1)
        return chosen + (chosen >= hot_expert[:, None]).astype(jnp.int32)
    pick_one = jnp.where(is_hot, hot_expert[:, None], expert_of(jnp.maximum(first_index, 0)))
    pick_two = expert_of(second_index)
    pick_one = jnp.take_along_axis(pick_one, places, axis=1)
    pick_two = jnp.take_along_axis(pick_two, places, axis=1)
    leading = jnp.where(flip_bits == 1, pick_two, pick_one)
    trailing = jnp.where(flip_bits == 1, pick_one, pick_two)
    return jnp.stack([leading, trailing], axis=-1).reshape(TOKENS, 2).astype(jnp.int32)


def block_levels(stream_key, extent, shards, low, top_value):
    gain, own = 1.0, jax.random.fold_in(stream_key, 6)
    for dim, shards_of in shards:
        heights = jnp.exp(jax.random.uniform(jax.random.fold_in(own, dim), (shards_of,), jnp.float32, low / len(shards), top_value / len(shards)))
        gain = gain * jnp.repeat(heights, extent[dim] // shards_of).reshape([-1 if axis == dim else 1 for axis in range(len(extent))])
    return gain


def gaussian(stream_key, shape, spread, limit, cuts=(), kind=jnp.bfloat16):
    drawn = jax.random.normal(stream_key, shape, jnp.float32) * spread
    if len(cuts) > 0:
        drawn = block_levels(stream_key, shape, cuts, -0.22, 0.18) * drawn
    return jnp.clip(drawn, min=-limit, max=limit).astype(kind)


def setup_inputs(seed: int = 0) -> dict:
    streams_of = jax.random.split(jax.random.key(seed), 6)
    grad_out = gaussian(streams_of[0], (TOKENS, D), 0.25, 1.5, ((0, 32),))
    routes = draw_routes(jax.random.fold_in(streams_of[5], 71), 0)
    combine = jnp.clip(0.099609375 + 0.7988281 * jax.random.uniform(streams_of[2], (TOKENS, 2), jnp.float32) ** block_levels(streams_of[2], (TOKENS, 2), ((0, 32),), -0.2, 0.2), 0.099609375, 0.8984375).astype(jnp.bfloat16)
    saved_hidden = gaussian(streams_of[3], (N_DP, EXPERTS, CAPR, FFW), 1.0, 6.0, ((1, 8), (3, 32)))
    down_weight = gaussian(streams_of[4], (EXPERTS, FFW, D), FFW ** -0.5, 0.0546875, ((0, 8), (1, 32)))
    return dict(grad_out=grad_out, routes=routes, combine=combine, saved_hidden=saved_hidden, down_weight=down_weight)


def slot_index(routes):
    per_group = routes.reshape(N_DP, N_EXPERT, TOK_DEV, 2)
    expert_ids = jnp.arange(EXPERTS, dtype=jnp.int32)
    hit_table = jnp.sum((per_group[..., None] == expert_ids).astype(jnp.int32), axis=3)
    before = (jnp.cumsum(hit_table, axis=2) - hit_table).astype(jnp.int32)
    ranking = jnp.take_along_axis(before, per_group, axis=3).astype(jnp.int32)
    replica = jnp.arange(N_DP, dtype=jnp.int32)[:, None, None, None]
    source = jnp.arange(N_EXPERT, dtype=jnp.int32)[None, :, None, None]
    target = (replica * EXPERTS + per_group) * CAPR + source * MOST + ranking
    return target.reshape(TOKENS, 2).astype(jnp.int32)


def reference(grad_out, routes, combine, saved_hidden, down_weight):
    target = slot_index(routes)
    slot_count = N_DP * EXPERTS * CAPR
    flat_target = target.reshape(-1)
    copies = jnp.broadcast_to(grad_out[:, None, :], (TOKENS, 2, D)).reshape(TOKENS * 2, D)
    slot_rows = jnp.zeros((slot_count, D), grad_out.dtype).at[flat_target].set(copies)
    slot_weights = jnp.zeros((slot_count,), jnp.float32).at[flat_target].set(combine.reshape(-1).astype(jnp.float32))
    slot_rows = slot_rows.reshape(N_DP, EXPERTS, CAPR, D).transpose(1, 0, 2, 3)
    slot_weights = slot_weights.reshape(N_DP, EXPERTS, CAPR).transpose(1, 0, 2)
    hidden = saved_hidden.transpose(1, 0, 2, 3)

    def per_expert(inputs):
        weight, rows_e, weights_e, hidden_e = inputs

        def per_replica(running, pieces):
            rows_p, weights_p, hidden_p = pieces
            update = jnp.dot(rows_p, weight.T, preferred_element_type=jnp.float32)
            scaling = weights_p[:, None]
            grad_rows = (scaling * update).astype(jnp.bfloat16)
            partial_value = jnp.sum(hidden_p.astype(jnp.float32) * update, axis=1)
            weighted = (scaling * hidden_p.astype(jnp.float32)).astype(jnp.bfloat16)
            running = running + jnp.dot(weighted.T, rows_p, preferred_element_type=jnp.float32)
            return running, (grad_rows, partial_value)

        zero_sum = jnp.zeros((FFW, D), jnp.float32)
        summed, (grad_slots, partials) = lax.scan(per_replica, zero_sum, (rows_e, weights_e, hidden_e))
        return summed.astype(jnp.bfloat16), grad_slots, partials

    grad_down, grad_slots, partials = lax.map(per_expert, (down_weight, slot_rows, slot_weights, hidden))
    grad_hidden = grad_slots.transpose(1, 0, 2, 3)
    grad_combine = partials.transpose(1, 0, 2).reshape(-1)[target]
    return grad_hidden, grad_down, grad_combine
```

```python
import jax
import jax.numpy as jnp
from jax import lax
from jax.experimental import pallas as pl
from jax.experimental.pallas import tpu as pltpu
from jax.sharding import PartitionSpec as P

F32, BF16 = jnp.float32, jnp.bfloat16
VMEM_LIMIT = 56 * 1024 * 1024


def slots_of(routes, most):
    tokens = routes.shape[0]
    lanes = lax.broadcasted_iota(jnp.int32, (tokens, 128), 1)
    hits = [routes[:, k : k + 1] == lanes for k in range(2)]
    counts = sum(h.astype(F32) for h in hits).astype(BF16)
    row = lax.broadcasted_iota(jnp.int32, (tokens, tokens), 0)
    col = lax.broadcasted_iota(jnp.int32, (tokens, tokens), 1)
    before = jnp.dot((col < row).astype(F32).astype(BF16), counts, preferred_element_type=F32)
    ranks = [jnp.sum(jnp.where(h, before, 0.0), axis=1, keepdims=True) for h in hits]
    return [
        routes[:, k : k + 1].astype(F32) * float(most) + ranks[k] for k in range(2)
    ]


def pick_kernel(place, routes, combine, grad, out, target):
    slots = out.shape[0]
    tokens = routes.shape[0]
    where = slots_of(routes[...], slots // 8)
    lane = lax.broadcasted_iota(jnp.int32, (tokens, slots), 1).astype(F32)
    weights = combine[...].astype(F32)
    picker = sum(
        jnp.where(where[k] == lane, weights[:, k : k + 1], 0.0) for k in range(2)
    ).astype(BF16)
    rows = lax.dot_general(
        picker, grad[...], (((0,), (0,)), ((), ())), preferred_element_type=F32
    )
    out[...] = rows.astype(BF16)
    target[...] = jnp.concatenate(where, axis=1)


def pick(routes, combine, grad_out, place, n_place, slots):
    tokens, width = grad_out.shape
    cols = width // n_place
    return pl.pallas_call(
        pick_kernel,
        grid_spec=pltpu.PrefetchScalarGridSpec(
            num_scalar_prefetch=1,
            grid=(1,),
            in_specs=[
                pl.BlockSpec((tokens, 2), lambda i, t: (0, 0)),
                pl.BlockSpec((tokens, 2), lambda i, t: (0, 0)),
                pl.BlockSpec((tokens, cols), lambda i, t: (0, t[0])),
            ],
            out_specs=[
                pl.BlockSpec((slots, cols), lambda i, t: (0, 0)),
                pl.BlockSpec((tokens, 2), lambda i, t: (0, 0)),
            ],
        ),
        out_shape=[
            jax.ShapeDtypeStruct((slots, cols), BF16),
            jax.ShapeDtypeStruct((tokens, 2), F32),
        ],
        cost_estimate=pl.CostEstimate(
            flops=2 * tokens * slots * cols, bytes_accessed=4 * slots * cols, transcendentals=0
        ),
    )(place, routes, combine, grad_out)


def update_kernel(first, second, weight, hidden, grad_hidden, partial, acc):
    t = pl.program_id(0)
    n_rep = hidden.shape[0]
    half = first.shape[2]
    capacity = hidden.shape[1]

    @pl.when(t == 0)
    def _():
        acc[...] = jnp.zeros_like(acc)

    for h, ref in enumerate((first, second)):
        for p in range(n_rep):
            acc[p, h * half : (h + 1) * half, :] += lax.dot_general(
                ref[p, 0], weight[...], (((1,), (1,)), ((), ())), preferred_element_type=F32
            )

    @pl.when(t == pl.num_programs(0) - 1)
    def _():
        for p in range(n_rep):
            whole = acc[p]
            grad_hidden[p] = whole.astype(BF16)
            prod = whole * hidden[p].astype(F32)
            folded = sum(prod[:, i : i + 128] for i in range(0, prod.shape[1], 128))
            partial[p : p + 1, :] = jnp.sum(folded.T, axis=0, keepdims=True)


def update(first, second, weight, hidden):
    n_rep, n_place, half, cols = first.shape
    units, width = weight.shape
    capacity = hidden.shape[1]
    block = pl.BlockSpec((n_rep, 1, half, cols), lambda t: (0, t, 0, 0))
    return pl.pallas_call(
        update_kernel,
        grid=(n_place,),
        in_specs=[
            block,
            block,
            pl.BlockSpec((units, cols), lambda t: (0, t)),
            pl.BlockSpec((n_rep, capacity, units), lambda t: (0, 0, 0)),
        ],
        out_specs=[
            pl.BlockSpec((n_rep, capacity, units), lambda t: (0, 0, 0)),
            pl.BlockSpec((n_rep, capacity), lambda t: (0, 0)),
        ],
        out_shape=[
            jax.ShapeDtypeStruct((n_rep, capacity, units), BF16),
            jax.ShapeDtypeStruct((n_rep, capacity), F32),
        ],
        scratch_shapes=[pltpu.VMEM((n_rep, capacity, units), F32)],
        compiler_params=pltpu.CompilerParams(vmem_limit_bytes=VMEM_LIMIT),
        cost_estimate=pl.CostEstimate(
            flops=2 * n_rep * capacity * units * width,
            bytes_accessed=2 * (n_rep * capacity * (width + 2 * units) + units * width),
            transcendentals=0,
        ),
    )(first, second, weight, hidden)


def down_kernel(first, second, turned, out):
    n_rep, _, half, cols = first.shape
    total = None
    for h, ref in enumerate((first, second)):
        for p in range(n_rep):
            term = jnp.dot(
                turned[2 * p + h], ref[p, 0], preferred_element_type=F32
            )
            total = term if total is None else total + term
    out[...] = total.astype(BF16)


def down(first, second, turned):
    n_rep, n_place, half, cols = first.shape
    units = turned.shape[1]
    block = pl.BlockSpec((n_rep, 1, half, cols), lambda t: (0, t, 0, 0))
    return pl.pallas_call(
        down_kernel,
        grid=(n_place,),
        in_specs=[block, block, pl.BlockSpec(turned.shape, lambda t: (0, 0, 0))],
        out_specs=pl.BlockSpec((units, cols), lambda t: (0, t)),
        out_shape=jax.ShapeDtypeStruct((units, n_place * cols), BF16),
        compiler_params=pltpu.CompilerParams(vmem_limit_bytes=VMEM_LIMIT),
        cost_estimate=pl.CostEstimate(
            flops=4 * n_rep * half * units * n_place * cols,
            bytes_accessed=4 * (n_rep * half + units) * n_place * cols,
            transcendentals=0,
        ),
    )(first, second, turned)


def per_device(grad_out, routes, combine, saved_hidden, down_weight):
    n_expert = lax.axis_size("expert")
    n_tensor = lax.axis_size("tensor")
    n_replica = lax.axis_size("dp")
    capacity = saved_hidden.shape[2]
    units = saved_hidden.shape[3]
    most = capacity // n_expert
    half = capacity // 2
    cols = grad_out.shape[1] // n_tensor
    place = lax.axis_index("tensor").astype(jnp.int32).reshape(1)
    rows, target = pick(routes, combine, grad_out, place, n_tensor, capacity)
    got = lax.all_to_all(
        rows.reshape(n_expert, most, cols), "expert", split_axis=0, concat_axis=0, tiled=True
    ).reshape(capacity, cols)
    first, second = (
        lax.all_gather(part, ("dp", "tensor"), axis=0).reshape(n_replica, n_tensor, half, cols)
        for part in (got[:half], got[half:])
    )
    hidden = saved_hidden[:, 0]
    turned = hidden.reshape(2 * n_replica, half, units).transpose(0, 2, 1)
    grad_hidden, partial = update(first, second, down_weight[0], hidden)
    grad_down = down(first, second, turned)
    spread = jnp.broadcast_to(
        partial.reshape(n_replica, n_expert, 1, most), (n_replica, n_expert, n_tensor, most)
    ).reshape(-1, 1, most)
    returned = lax.all_to_all(
        spread, ("dp", "expert", "tensor"), split_axis=0, concat_axis=0, tiled=True
    )
    sums = jnp.sum(returned.reshape(n_replica, n_expert, n_tensor, most), axis=(0, 2)).reshape(-1)
    slot = jnp.arange(capacity, dtype=jnp.int32).astype(F32)
    chosen = target[None] == slot[:, None, None]
    grad_combine = jnp.sum(jnp.where(chosen, sums[:, None, None], 0.0), axis=0) / combine.astype(F32)
    return grad_hidden[:, None], grad_down[None], grad_combine


def solution(mesh):
    return jax.shard_map(
        per_device,
        mesh=mesh,
        in_specs=(
            P(("dp", "expert"), None),
            P(("dp", "expert"), None),
            P(("dp", "expert"), None),
            P(None, "expert", None, ("dp", "tensor")),
            P("expert", ("dp", "tensor"), None),
        ),
        out_specs=(
            P(None, "expert", None, ("dp", "tensor")),
            P("expert", ("dp", "tensor"), None),
            P(("dp", "expert"), None),
        ),
        check_vma=False,
    )
```

```python
import jax
import jax.numpy as jnp
from jax import lax
from jax.experimental import pallas as pl
from jax.experimental.pallas import tpu as pltpu
from jax.sharding import PartitionSpec as P

F32, BF16 = jnp.float32, jnp.bfloat16
VMEM_LIMIT = 56 * 1024 * 1024


def slots_of(routes, most):
    tokens = routes.shape[0]
    lanes = lax.broadcasted_iota(jnp.int32, (tokens, 128), 1)
    hits = [routes[:, k : k + 1] == lanes for k in range(2)]
    counts = sum(h.astype(F32) for h in hits).astype(BF16)
    row = lax.broadcasted_iota(jnp.int32, (tokens, tokens), 0)
    col = lax.broadcasted_iota(jnp.int32, (tokens, tokens), 1)
    before = jnp.dot((col < row).astype(F32).astype(BF16), counts, preferred_element_type=F32)
    ranks = [jnp.sum(jnp.where(h, before, 0.0), axis=1, keepdims=True) for h in hits]
    return [
        routes[:, k : k + 1].astype(F32) * float(most) + ranks[k] for k in range(2)
    ]


def pick_kernel(where_cols, routes, combine, grad_a, grad_b, out, target):
    slots = out.shape[0]
    tokens = routes.shape[0]
    where = slots_of(routes[...], slots // 8)
    lane = lax.broadcasted_iota(jnp.int32, (tokens, slots), 1).astype(F32)
    weights = combine[...].astype(F32)
    picker = sum(
        jnp.where(where[k] == lane, weights[:, k : k + 1], 0.0) for k in range(2)
    ).astype(BF16)
    cols = grad_a.shape[1]
    for i, grad in enumerate((grad_a, grad_b)):
        rows = lax.dot_general(
            picker, grad[...], (((0,), (0,)), ((), ())), preferred_element_type=F32
        )
        out[:, i * cols : (i + 1) * cols] = rows.astype(BF16)
    target[...] = jnp.concatenate(where, axis=1)


def pick(routes, combine, grad_out, blocks, cols, slots):
    tokens = grad_out.shape[0]
    return pl.pallas_call(
        pick_kernel,
        grid_spec=pltpu.PrefetchScalarGridSpec(
            num_scalar_prefetch=1,
            grid=(1,),
            in_specs=[
                pl.BlockSpec((tokens, 2), lambda i, t: (0, 0)),
                pl.BlockSpec((tokens, 2), lambda i, t: (0, 0)),
                pl.BlockSpec((tokens, cols), lambda i, t: (0, t[0])),
                pl.BlockSpec((tokens, cols), lambda i, t: (0, t[1])),
            ],
            out_specs=[
                pl.BlockSpec((slots, 2 * cols), lambda i, t: (0, 0)),
                pl.BlockSpec((tokens, 2), lambda i, t: (0, 0)),
            ],
        ),
        out_shape=[
            jax.ShapeDtypeStruct((slots, 2 * cols), BF16),
            jax.ShapeDtypeStruct((tokens, 2), F32),
        ],
        cost_estimate=pl.CostEstimate(
            flops=4 * tokens * slots * cols, bytes_accessed=8 * slots * cols, transcendentals=0
        ),
    )(blocks, routes, combine, grad_out, grad_out)


ANY = pl.BlockSpec(memory_space=pl.ANY)
VMEM = pl.BlockSpec(memory_space=pltpu.VMEM)


def like(*arrays):
    return [jax.ShapeDtypeStruct(a.shape, a.dtype) for a in arrays]


def fence(*arrays):
    return pl.pallas_call(
        lambda *refs: None,
        out_shape=like(*arrays),
        in_specs=[ANY] * len(arrays),
        out_specs=[ANY] * len(arrays),
        input_output_aliases={i: i for i in range(len(arrays))},
        compiler_params=pltpu.CompilerParams(has_side_effects=True),
    )(*arrays)


def halves(left, right, down, up):
    def kernel(*refs):
        for i in range(4):
            refs[4 + i][...] = refs[i][...]

    rows, cols = left.shape
    lower = pl.BlockSpec((rows // 2, cols), lambda i: (0, 0))
    upper = pl.BlockSpec((rows // 2, cols), lambda i: (1, 0))
    return pl.pallas_call(
        kernel,
        grid=(1,),
        in_specs=[lower, upper, lower, upper],
        out_specs=[lower] * 4,
        out_shape=[jax.ShapeDtypeStruct((rows // 2, cols), left.dtype)] * 4,
    )(left, right, down, up)


def pairs(own, prev, after, low, high):
    return [(own, prev), (after, low, high)]


def stack(a_parts, b_parts):
    def kernel(*refs):
        ins, outs = refs[:10], refs[10:]
        for kind in range(2):
            own, prev, after, low, high = ins[5 * kind : 5 * kind + 5]
            rows = own.shape[0]
            for copy in range(2):
                first, second = outs[4 * copy + 2 * kind : 4 * copy + 2 * kind + 2]
                first[0] = own[...]
                first[1] = prev[...]
                second[0] = after[...]
                second[1, : rows // 2] = low[...]
                second[1, rows // 2 :] = high[...]

    rows, cols = a_parts[0].shape
    return pl.pallas_call(
        kernel,
        in_specs=[VMEM] * 10,
        out_specs=[VMEM] * 8,
        out_shape=[jax.ShapeDtypeStruct((2, rows, cols), BF16)] * 8,
        compiler_params=pltpu.CompilerParams(vmem_limit_bytes=VMEM_LIMIT),
    )(*a_parts, *b_parts)


NT = (((1,), (1,)), ((), ()))


def load(refs, bufs, sems):
    copies = [
        pltpu.make_async_copy(ref, buf, sems.at[i]) for i, (ref, buf) in enumerate(zip(refs, bufs))
    ]
    for c in copies:
        c.start()
    return copies


def step_cost(flops, arrays):
    return pl.CostEstimate(
        flops=flops,
        bytes_accessed=sum(a.size * a.dtype.itemsize for a in arrays),
        transcendentals=0,
    )


def absorb(acc, a_groups, b_groups, weight, turned, split):
    n_a, n_b = len(a_groups), len(b_groups)
    a_offs = [g[0] for g in a_groups]
    b_offs = [g[0] for g in b_groups]
    arrays = [r for g in (*a_groups, *b_groups) for r in g[1:]]
    n = len(arrays)
    fresh = acc is None
    with_down = turned is not None
    extra = [weight] + ([turned] if with_down else []) + ([] if fresh else [acc])
    rows, cols = arrays[0].shape[1:]
    both = weight.shape[2]
    units = both // 2
    acc_shape = (4, rows, both)

    def kernel(*refs):
        ins = refs[: n + len(extra)]
        n_out = (2 if split else 1) + (2 if with_down else 0)
        outs = refs[n + len(extra) : n + len(extra) + n_out]
        scratch = refs[n + len(extra) + n_out :]
        sems = scratch[-1]
        bufs = scratch[:-1]
        copies = load(ins, bufs[: len(ins)], sems)
        w = bufs[n]
        total = bufs[len(ins)] if fresh else bufs[len(ins) - 1]
        copies[n].wait()
        if not fresh:
            copies[-1].wait()
        seen = [not fresh] * 4

        def add(j, term):
            total[j] = total[j] + term if seen[j] else term
            seen[j] = True

        for g in range(n_a):
            term = None
            for k in range(4):
                if k % 2 == 0:
                    copies[2 * g + k // 2].wait()
                part = lax.dot_general(
                    bufs[2 * g + k // 2][k % 2], w[k, 0], NT, preferred_element_type=F32
                )
                term = part if term is None else term + part
            add(a_offs[g], term)
        if with_down:
            copies[n + 1].wait()
        for g in range(n_b):
            base = 2 * (n_a + g)
            down = None
            for k in range(4):
                if k % 2 == 0:
                    copies[base + k // 2].wait()
                block = bufs[base + k // 2][k % 2]
                add(k, lax.dot_general(block, w[b_offs[g], 1], NT, preferred_element_type=F32))
                if with_down:
                    part = jnp.dot(bufs[n + 1][k], block, preferred_element_type=F32)
                    down = part if down is None else down + part
            if with_down:
                outs[-2][g] = down[:units].astype(BF16)
                outs[-1][g] = down[units:].astype(BF16)
        if split:
            for j in range(4):
                outs[0][j] = total[j, :, :units]
                outs[1][j] = total[j, :, units:]
        else:
            outs[0][...] = total[...]

    out_shape = (
        [jax.ShapeDtypeStruct((4, rows, units), F32)] * 2
        if split
        else [jax.ShapeDtypeStruct(acc_shape, F32)]
    )
    if with_down:
        out_shape += [jax.ShapeDtypeStruct((n_b, units, cols), BF16)] * 2
    operands = arrays + extra
    scratch = [pltpu.VMEM(a.shape, a.dtype) for a in operands]
    if fresh:
        scratch.append(pltpu.VMEM(acc_shape, F32))
    scratch.append(pltpu.SemaphoreType.DMA((len(operands),)))
    flops = 2 * rows * cols * both * 4 * (n_a + n_b * (2 if with_down else 1))
    return pl.pallas_call(
        kernel,
        in_specs=[ANY] * len(operands),
        out_specs=[VMEM] * len(out_shape),
        out_shape=out_shape,
        scratch_shapes=scratch,
        compiler_params=pltpu.CompilerParams(vmem_limit_bytes=VMEM_LIMIT),
        cost_estimate=step_cost(flops, operands),
    )(*operands)


def down(a_groups, b_pair, turned):
    arrays = [r for g in a_groups for r in g] + list(b_pair)
    n = len(arrays)
    both, rows = turned.shape[1:]
    units = both // 2
    cols = arrays[0].shape[2]

    def kernel(*refs):
        ins, (own, other) = refs[: n + 1], refs[n + 1 : n + 3]
        bufs, sems = refs[n + 3 : -1], refs[-1]
        copies = load(ins, bufs, sems)
        for c in copies:
            c.wait()
        t = bufs[n]
        for k in range(5):
            total = None
            for j in range(4):
                block = bufs[2 * j + k // 2][k % 2] if k < 4 else bufs[n - 2 + j // 2][j % 2]
                part = jnp.dot(t[j], block, preferred_element_type=F32)
                total = part if total is None else total + part
            own[k] = total[:units].astype(BF16)
            other[k] = total[units:].astype(BF16)

    operands = arrays + [turned]
    return pl.pallas_call(
        kernel,
        in_specs=[ANY] * (n + 1),
        out_specs=[VMEM] * 2,
        out_shape=[jax.ShapeDtypeStruct((5, units, cols), BF16)] * 2,
        scratch_shapes=[pltpu.VMEM(a.shape, a.dtype) for a in operands]
        + [pltpu.SemaphoreType.DMA((n + 1,))],
        compiler_params=pltpu.CompilerParams(vmem_limit_bytes=VMEM_LIMIT),
        cost_estimate=step_cost(2 * 4 * rows * both * cols * 5, operands),
    )(*operands)


def finish_kernel(reps, own, other, hidden, grad_hidden, partial):
    whole = own[0] + other[0]
    grad_hidden[0] = whole.astype(BF16)
    prod = whole * hidden[0].astype(F32)
    folded = sum(prod[:, i : i + 128] for i in range(0, prod.shape[1], 128))
    partial[0] = jnp.sum(folded.T, axis=0, keepdims=True)


def finish(reps, own, other, hidden):
    n_rep, rows, units = own.shape
    here = pl.BlockSpec((1, rows, units), lambda i, r: (i, 0, 0))
    there = pl.BlockSpec((1, rows, units), lambda i, r: (r[i], 0, 0))
    return pl.pallas_call(
        finish_kernel,
        grid_spec=pltpu.PrefetchScalarGridSpec(
            num_scalar_prefetch=1,
            grid=(n_rep,),
            in_specs=[here, here, there],
            out_specs=[there, pl.BlockSpec((1, 1, rows), lambda i, r: (r[i], 0, 0))],
        ),
        out_shape=[
            jax.ShapeDtypeStruct((n_rep, rows, units), BF16),
            jax.ShapeDtypeStruct((n_rep, 1, rows), F32),
        ],
        cost_estimate=step_cost(0, (own, other, hidden, hidden)),
    )(reps, own, other, hidden)


def gather_down(places, blocks):
    sizes = [b.shape[0] for b in blocks]
    count = sum(sizes)
    units, cols = blocks[0].shape[1:]

    def kernel(place, *refs):
        ins, out = refs[: len(blocks)], refs[len(blocks)]
        bufs, in_sems, out_sems = refs[len(blocks) + 1 :]
        copies = []
        for ref, size in zip(ins, sizes):
            for k in range(size):
                i = len(copies)
                copies.append(pltpu.make_async_copy(ref.at[k], bufs.at[i], in_sems.at[i]))
                copies[-1].start()
        stores = []
        for i in range(count):
            copies[i].wait()
            at = pl.ds(pl.multiple_of(place[i] * cols, 128), cols)
            stores.append(pltpu.make_async_copy(bufs.at[i], out.at[:, at], out_sems.at[i]))
            stores[-1].start()
        for s in stores:
            s.wait()

    return pl.pallas_call(
        kernel,
        in_specs=[pl.BlockSpec(memory_space=pltpu.SMEM)] + [ANY] * len(blocks),
        out_specs=ANY,
        out_shape=jax.ShapeDtypeStruct((units, count * cols), BF16),
        scratch_shapes=[
            pltpu.VMEM((count, units, cols), BF16),
            pltpu.SemaphoreType.DMA((count,)),
            pltpu.SemaphoreType.DMA((count,)),
        ],
        compiler_params=pltpu.CompilerParams(vmem_limit_bytes=VMEM_LIMIT),
        cost_estimate=step_cost(0, (*blocks, *blocks)),
    )(places, *blocks)


OFFSETS = (0, -1, 1, 2)


def per_device(grad_out, routes, combine, saved_hidden, down_weight):
    n_expert = lax.axis_size("expert")
    n_tensor = lax.axis_size("tensor")
    n_rep = lax.axis_size("dp")
    n_x = n_tensor // 2
    capacity = saved_hidden.shape[2]
    units = saved_hidden.shape[3]
    most = capacity // n_expert
    cols = grad_out.shape[1] // (2 * n_tensor)
    tensor = lax.axis_index("tensor").astype(jnp.int32)
    rep = lax.axis_index("dp").astype(jnp.int32)
    x, core = tensor // 2, tensor % 2
    xs = [(x + o + n_x) % n_x for o in OFFSETS]
    reps = [(rep + o + n_rep) % n_rep for o in OFFSETS]

    def along_x(v, by):
        return lax.ppermute(
            v, "tensor", [(t, (t // 2 + by) % n_x * 2 + t % 2) for t in range(n_tensor)]
        )

    def along_y(v, by):
        return lax.ppermute(v, "dp", [(p, (p + by) % n_rep) for p in range(n_rep)])

    def to_core(v):
        return lax.ppermute(v, "tensor", [(t, t ^ 1) for t in range(n_tensor)])

    rows, target = pick(
        routes, combine, grad_out, jnp.stack([4 * x + core, 4 * x + 2 + core]), cols, capacity
    )
    got = lax.all_to_all(
        rows.reshape(n_expert, most, 2 * cols), "expert", split_axis=0, concat_axis=0, tiled=True
    ).reshape(capacity, 2 * cols)

    hidden = saved_hidden[:, 0]
    table = down_weight[0].reshape(units, n_x, 2, 2, cols)

    def weights_of(c):
        at_core = lax.dynamic_index_in_dim(table, c, 3, keepdims=False)
        turned = [lax.dynamic_index_in_dim(at_core, i, 1, keepdims=False) for i in xs]
        return jnp.stack(turned).transpose(0, 2, 1, 3)

    weight = jnp.concatenate([weights_of(core), to_core(weights_of(1 - core))], axis=2)
    turned = jnp.stack([lax.dynamic_index_in_dim(hidden, r, 0, keepdims=False) for r in reps])
    turned = turned.transpose(0, 2, 1)
    turned = jnp.concatenate([turned, to_core(turned)], axis=1)

    a, b = got[:, :cols], got[:, cols:]
    al, ar = along_x(a, 1), along_x(a, -1)
    bd, bu = along_y(b, 1), along_y(b, -1)
    hl, hr, hd, hu = halves(al, ar, bd, bu)
    a_low, a_high = along_x(hl, 1), along_x(hr, -1)
    b_low, b_high = along_y(hd, 1), along_y(hu, -1)
    a1, a2, b1, b2, a1s, a2s, b1s, b2s = stack(
        (a, al, ar, a_low, a_high), (b, bd, bu, b_low, b_high)
    )
    first = along_y(a1, 1), along_y(a2, -1), along_x(b1, 1), along_x(b2, -1)
    d1, u2, l1, r2, a1s, a2s, b1s, b2s = fence(*first, a1s, a2s, b1s, b2s)
    acc, g0, g0c = absorb(None, [(0, a1, a2)], [(0, b1, b2)], weight, turned, False)
    second = along_y(a2s, 1), along_y(a1s, -1), along_x(b2s, 1), along_x(b1s, -1)
    d1, u2, l1, r2, d2, u1, l2, r1 = fence(d1, u2, l1, r2, *second)
    acc, g1, g1c = absorb(
        acc, [(1, d1, d2), (2, u1, u2)], [(1, l1, l2), (2, r1, r2)], weight, turned, False
    )
    o1, o2, q1, q2 = along_y(d1, 1), along_y(u2, -1), along_x(l1, 1), along_x(r2, -1)
    own, other = absorb(acc, [(3, o1, o2)], [(3, q1, q2)], weight, None, True)
    rep_ids = jnp.stack(reps)
    grad_hidden, partial = finish(rep_ids, own, to_core(other), hidden)
    g2, g2c = down([(a1, a2), (d1, d2), (u1, u2), (o1, o2)], (q1, q2), turned)
    spread = jnp.broadcast_to(
        partial.reshape(n_rep, n_expert, 1, most), (n_rep, n_expert, n_tensor, most)
    ).reshape(-1, 1, most)
    returned = lax.all_to_all(
        spread, ("dp", "expert", "tensor"), split_axis=0, concat_axis=0, tiled=True
    )
    order = [4 * xs[k] + 2 for k in range(4)] + [4 * xs[k] for k in range(4)] + [4 * xs[3] + 2]
    order = jnp.stack(order[:3] + order[4:])
    places = jnp.concatenate([order + core, order + 1 - core])
    grad_down = gather_down(places, [g0, g1, g2, to_core(g0c), to_core(g1c), to_core(g2c)])
    sums = jnp.sum(returned.reshape(n_rep, n_expert, n_tensor, most), axis=(0, 2)).reshape(-1)
    slot = jnp.arange(capacity, dtype=jnp.int32).astype(F32)
    chosen = target[None] == slot[:, None, None]
    grad_combine = jnp.sum(jnp.where(chosen, sums[:, None, None], 0.0), axis=0) / combine.astype(F32)
    return grad_hidden[:, None], grad_down[None], grad_combine


def solution(mesh):
    return jax.shard_map(
        per_device,
        mesh=mesh,
        in_specs=(
            P(("dp", "expert"), None),
            P(("dp", "expert"), None),
            P(("dp", "expert"), None),
            P(None, "expert", None, ("dp", "tensor")),
            P("expert", ("dp", "tensor"), None),
        ),
        out_specs=(
            P(None, "expert", None, ("dp", "tensor")),
            P("expert", ("dp", "tensor"), None),
            P(("dp", "expert"), None),
        ),
        check_vma=False,
    )
```

```python
import jax
import jax.numpy as jnp
from jax import lax
from jax.experimental import pallas as pl
from jax.experimental.pallas import tpu as pltpu
from jax.sharding import PartitionSpec as P

F32, BF16 = jnp.float32, jnp.bfloat16
LIMIT = pltpu.CompilerParams(vmem_limit_bytes=60 * 1024 * 1024)
ANY = pl.BlockSpec(memory_space=pl.ANY)
VMEM = pl.BlockSpec(memory_space=pltpu.VMEM)
NT = (((1,), (1,)), ((), ()))
OFFSETS = (0, -1, 1, 2)


def like(*arrays):
    return [jax.ShapeDtypeStruct(a.shape, a.dtype) for a in arrays]


def cost(flops, arrays):
    return pl.CostEstimate(
        flops=flops,
        bytes_accessed=sum(a.size * a.dtype.itemsize for a in arrays),
        transcendentals=0,
    )


def ring_place(axis, by, cores):
    return lax.rem(lax.axis_index(axis) // cores + (OFFSETS[by] + 4), 4)


def column_place(k, kind, core):
    return 4 * ring_place("tensor", k, 2) + 2 * kind + core


def this_core():
    return lax.rem(lax.axis_index("tensor"), 2)


def columns(ref, place, cols):
    return ref.at[:, pl.ds(pl.multiple_of(place * cols, 128), cols)]


def pick(routes, combine, grad_out, cols, slots, most):
    tokens = grad_out.shape[0]

    def kernel(routes, combine, grad, out, target, rows, sems):
        copies = [
            pltpu.make_async_copy(
                columns(grad, column_place(0, kind, this_core()), cols), rows.at[kind], sems.at[kind]
            )
            for kind in range(2)
        ]
        for c in copies:
            c.start()
        expert = lax.broadcasted_iota(jnp.int32, (8, tokens), 0)
        named = [routes[k : k + 1, :] for k in range(2)]
        hits = [(n == expert).astype(F32) for n in named]
        earlier = lax.broadcasted_iota(jnp.int32, (tokens, tokens), 0)
        later = lax.broadcasted_iota(jnp.int32, (tokens, tokens), 1)
        before = jnp.dot(
            (hits[0] + hits[1]).astype(BF16),
            (earlier < later).astype(F32).astype(BF16),
            preferred_element_type=F32,
        )
        slot = lax.broadcasted_iota(jnp.int32, (slots, tokens), 0).astype(F32)
        picker = None
        for k in range(2):
            rank = jnp.sum(hits[k] * before, axis=0, keepdims=True)
            where = named[k].astype(F32) * float(most) + rank
            target[k : k + 1, :] = where
            term = jnp.where(where == slot, combine[k : k + 1, :].astype(F32), 0.0)
            picker = term if picker is None else picker + term
        picker = picker.astype(BF16)
        for kind in range(2):
            copies[kind].wait()
            found = jnp.dot(picker, rows[kind], preferred_element_type=F32)
            out[:, kind * cols : (kind + 1) * cols] = found.astype(BF16)

    return pl.pallas_call(
        kernel,
        in_specs=[VMEM, VMEM, ANY],
        out_specs=[VMEM, VMEM],
        out_shape=[
            jax.ShapeDtypeStruct((slots, 2 * cols), BF16),
            jax.ShapeDtypeStruct((2, tokens), F32),
        ],
        scratch_shapes=[pltpu.VMEM((2, tokens, cols), BF16), pltpu.SemaphoreType.DMA((2,))],
        compiler_params=LIMIT,
        cost_estimate=pl.CostEstimate(
            flops=4 * tokens * slots * cols, bytes_accessed=8 * slots * cols, transcendentals=0
        ),
    )(routes, combine, grad_out)


def prepare(weight, hidden, cols):
    units = weight.shape[0]
    n_rep, slots, _ = hidden.shape

    def kernel(weight, hidden, sent, turned, held, sems):
        copies = [
            pltpu.make_async_copy(hidden.at[ring_place("dp", j, 1)], held.at[j], sems.at[j])
            for j in range(4)
        ]
        blocks = [
            pltpu.make_async_copy(
                columns(weight, column_place(i // 2, i % 2, 1 - this_core()), cols),
                sent.at[i],
                sems.at[4 + i],
            )
            for i in range(8)
        ]
        for c in copies + blocks:
            c.start()
        for j in range(4):
            copies[j].wait()
            turned[j] = held[j].astype(F32).T.astype(BF16)
        for c in blocks:
            c.wait()

    return pl.pallas_call(
        kernel,
        in_specs=[ANY, ANY],
        out_specs=[VMEM, VMEM],
        out_shape=[
            jax.ShapeDtypeStruct((8, units, cols), BF16),
            jax.ShapeDtypeStruct((4, units, slots), BF16),
        ],
        scratch_shapes=[pltpu.VMEM((4, slots, units), BF16), pltpu.SemaphoreType.DMA((12,))],
        compiler_params=LIMIT,
        cost_estimate=cost(0, (weight, hidden, hidden)),
    )(weight, hidden)


def fence(*arrays):
    return pl.pallas_call(
        lambda *refs: None,
        out_shape=like(*arrays),
        in_specs=[ANY] * len(arrays),
        out_specs=[ANY] * len(arrays),
        input_output_aliases={i: i for i in range(len(arrays))},
        compiler_params=pltpu.CompilerParams(
            has_side_effects=True, vmem_limit_bytes=60 * 1024 * 1024
        ),
    )(*arrays)


def halves(left, right, down, up):
    def kernel(*refs):
        for i in range(4):
            refs[4 + i][...] = refs[i][...]

    rows, cols = left.shape
    lower = pl.BlockSpec((rows // 2, cols), lambda i: (0, 0))
    upper = pl.BlockSpec((rows // 2, cols), lambda i: (1, 0))
    return pl.pallas_call(
        kernel,
        grid=(1,),
        in_specs=[lower, upper, lower, upper],
        out_specs=[lower] * 4,
        out_shape=[jax.ShapeDtypeStruct((rows // 2, cols), left.dtype)] * 4,
        compiler_params=LIMIT,
    )(left, right, down, up)


def stack(a_parts, b_parts):
    rows, cols = a_parts[0].shape

    def kernel(*refs):
        ins, outs, sems = refs[:10], refs[10:14], refs[14]
        copies = []
        for kind in range(2):
            own, prev, after, low, high = ins[5 * kind : 5 * kind + 5]
            first, second = outs[2 * kind : 2 * kind + 2]
            for src, dst in (
                (own, first.at[0]),
                (prev, first.at[1]),
                (after, second.at[0]),
                (low, second.at[1, : rows // 2]),
                (high, second.at[1, rows // 2 :]),
            ):
                copies.append(pltpu.make_async_copy(src, dst, sems.at[len(copies)]))
                copies[-1].start()
        for c in copies:
            c.wait()

    return pl.pallas_call(
        kernel,
        in_specs=[ANY] * 10,
        out_specs=[VMEM] * 4,
        out_shape=[jax.ShapeDtypeStruct((2, rows, cols), BF16)] * 4,
        scratch_shapes=[pltpu.SemaphoreType.DMA((10,))],
        compiler_params=LIMIT,
    )(*a_parts, *b_parts)


def absorb(weight, sent, acc, parts, sides=(0, 1), turned=None, downs=(), again=False, kind=F32):
    arrays = [p[3] for p in parts]
    used = [p for p in parts if p[1] is not None and p[2] is not None and not p[4:]]
    keys = []
    for what, off, pair, *_ in used:
        for key in [(2 * pair, 0), (2 * pair + 1, 0)] if what == 0 else [(off, 1)]:
            if key not in keys:
                keys.append(key)
    n, m, s = len(arrays), len(keys), len(sides)
    rows, cols = arrays[0].shape[1:]
    units = weight.shape[0]
    acc = list(acc) if acc is not None else []
    turned = list(turned) if turned is not None else []
    operands = arrays + [weight, sent] + turned + acc
    n_out = s + (2 if downs else 0) + (n if again else 0)

    def kernel(*refs):
        ins, w_ref, s_ref = refs[:n], refs[n], refs[n + 1]
        t_refs = refs[n + 2 : n + 2 + len(turned)]
        acc_refs = refs[n + 2 + len(turned) : len(operands)]
        outs = refs[len(operands) : len(operands) + n_out]
        bufs = refs[len(operands) + n_out : len(operands) + n_out + n]
        wbuf, *rest = refs[len(operands) + n_out + n :]
        sems = rest[-1]
        totals = outs[:s]
        started = []

        def start(src, dst):
            copy = pltpu.make_async_copy(src, dst, sems.at[len(started)])
            copy.start()
            started.append(copy)
            return copy

        w_copies = {}
        part_copies = [None] * n
        for i, (what, off, pair, *_) in enumerate(parts):
            part_copies[i] = start(ins[i], bufs[i])
            if parts[i] not in used:
                continue
            for key in [(2 * pair, 0), (2 * pair + 1, 0)] if what == 0 else [(off, 1)]:
                if key in w_copies:
                    continue
                at = keys.index(key)
                w_copies[key] = []
                for where, side in enumerate(sides):
                    src = (
                        columns(w_ref, column_place(key[0], key[1], this_core()), cols)
                        if side == 0
                        else s_ref.at[2 * key[0] + key[1]]
                    )
                    dst = wbuf.at[at, pl.ds(where * units, units)]
                    w_copies[key].append(start(src, dst))
        t_copies = [
            start(ref, rest[0].at[:, pl.ds(i * units, units)]) for i, ref in enumerate(t_refs)
        ]
        acc_copies = [start(ref, total) for ref, total in zip(acc_refs, totals)]
        seen = [bool(acc)] * 4

        def w(key):
            for c in w_copies[key]:
                c.wait()
            w_copies[key] = []
            return wbuf[keys.index(key)]

        def add(j, term):
            while acc_copies:
                acc_copies.pop(0).wait()
            for where in range(s):
                mine = term[:, where * units : (where + 1) * units]
                totals[where][j] = (totals[where][j] + mine if seen[j] else mine).astype(kind)
            seen[j] = True

        stores = []
        for i, part in enumerate(parts):
            part_copies[i].wait()
            if again:
                stores.append(start(bufs[i], outs[n_out - n + i]))
            if part not in used:
                continue
            what, off, pair = part[:3]
            terms = []
            for k in range(2):
                key = (2 * pair + k, 0) if what == 0 else (off, 1)
                terms.append(lax.dot_general(bufs[i][k], w(key), NT, preferred_element_type=F32))
            if what == 0:
                add(off, terms[0] + terms[1])
            else:
                for k in range(2):
                    add(2 * pair + k, terms[k])
        for c in t_copies:
            c.wait()
        for g, off in enumerate(downs):
            down = None
            for i, part in enumerate(parts):
                if part[0] == 1 and part[1] == off:
                    for k in range(2):
                        term = jnp.dot(
                            rest[0][2 * part[2] + k], bufs[i][k], preferred_element_type=F32
                        )
                        down = term if down is None else down + term
            for side in range(2):
                outs[s + side][g] = down[side * units : (side + 1) * units].astype(BF16)
        for c in stores:
            c.wait()

    out_shape = [jax.ShapeDtypeStruct((4, rows, units), kind)] * s
    out_specs = [VMEM] * s
    if downs:
        out_shape += [jax.ShapeDtypeStruct((len(downs), units, cols), BF16)] * 2
        out_specs += [VMEM] * 2
    if again:
        out_shape += like(*arrays)
        out_specs += [ANY] * n
    scratch = [pltpu.VMEM(a.shape, a.dtype) for a in arrays]
    scratch.append(pltpu.VMEM((m, s * units, cols), BF16))
    if turned:
        scratch.append(pltpu.VMEM((4, 2 * units, rows), BF16))
    scratch.append(pltpu.SemaphoreType.DMA((2 * n + 2 * m + 4,)))
    flops = 4 * rows * cols * units * (s * len(used) + 2 * 2 * len(downs))
    return pl.pallas_call(
        kernel,
        in_specs=[ANY] * len(operands),
        out_specs=out_specs,
        out_shape=out_shape,
        scratch_shapes=scratch,
        compiler_params=LIMIT,
        cost_estimate=cost(flops, operands),
    )(*operands)


def down(a_groups, b_pair, turned):
    arrays = [r for g in a_groups for r in g] + list(b_pair)
    n = len(arrays)
    units, rows = turned[0].shape[1:]
    cols = arrays[0].shape[2]

    def kernel(*refs):
        ins, (own, other) = refs[: n + 2], refs[n + 2 : n + 4]
        bufs, t, sems = refs[n + 4 : n + 4 + n], refs[-2], refs[-1]
        t_copies = [
            pltpu.make_async_copy(ins[n + i], t.at[:, pl.ds(i * units, units)], sems.at[n + i])
            for i in range(2)
        ]
        copies = [pltpu.make_async_copy(ins[i], bufs[i], sems.at[i]) for i in range(n)]
        order = [2 * j for j in range(4)] + [2 * j + 1 for j in range(4)] + [8, 9]
        for c in t_copies + [copies[i] for i in order]:
            c.start()
        for c in t_copies:
            c.wait()
        for k in range(5):
            total = None
            for j in range(4):
                i, member = (2 * j + k // 2, k % 2) if k < 4 else (8 + j // 2, j % 2)
                if copies[i] is not None:
                    copies[i].wait()
                    copies[i] = None
                part = jnp.dot(t[j], bufs[i][member], preferred_element_type=F32)
                total = part if total is None else total + part
            own[k] = total[:units].astype(BF16)
            other[k] = total[units:].astype(BF16)

    operands = arrays + list(turned)
    return pl.pallas_call(
        kernel,
        in_specs=[ANY] * (n + 2),
        out_specs=[VMEM] * 2,
        out_shape=[jax.ShapeDtypeStruct((5, units, cols), BF16)] * 2,
        scratch_shapes=[pltpu.VMEM(a.shape, a.dtype) for a in arrays]
        + [pltpu.VMEM((4, 2 * units, rows), BF16), pltpu.SemaphoreType.DMA((n + 2,))],
        compiler_params=LIMIT,
        cost_estimate=cost(2 * 4 * rows * 2 * units * cols * 5, operands),
    )(*operands)


def finish(own, before, after, hidden):
    n_rep, rows, units = own.shape

    def kernel(own, before, after, hidden, grad_hidden, partial, *scratch):
        bufs, rounded, in_sems, out_sems = scratch[:4], scratch[4], scratch[5], scratch[6]
        loads, stores = [], []
        for j in range(4):
            place = ring_place("dp", j, 1)
            for i, src in enumerate((own.at[j], before.at[j], after.at[j], hidden.at[place])):
                loads.append(pltpu.make_async_copy(src, bufs[i].at[j], in_sems.at[4 * j + i]))
                loads[-1].start()
        for j in range(4):
            place = ring_place("dp", j, 1)
            for i in range(4):
                loads[4 * j + i].wait()
            whole = bufs[0][j] + bufs[1][j] + bufs[2][j].astype(F32)
            rounded[j] = whole.astype(BF16)
            stores.append(
                pltpu.make_async_copy(rounded.at[j], grad_hidden.at[place], out_sems.at[j])
            )
            stores[-1].start()
            prod = whole * bufs[3][j].astype(F32)
            folded = sum(prod[:, i : i + 128] for i in range(0, units, 128))
            partial[pl.ds(place, 1), :] = jnp.sum(folded.T, axis=0, keepdims=True)
        for c in stores:
            c.wait()

    operands = (own, before, after, hidden)
    return pl.pallas_call(
        kernel,
        in_specs=[ANY] * 4,
        out_specs=[ANY, VMEM],
        out_shape=[
            jax.ShapeDtypeStruct((n_rep, rows, units), BF16),
            jax.ShapeDtypeStruct((n_rep, rows), F32),
        ],
        scratch_shapes=[pltpu.VMEM(a.shape, a.dtype) for a in operands]
        + [
            pltpu.VMEM((n_rep, rows, units), BF16),
            pltpu.SemaphoreType.DMA((16,)),
            pltpu.SemaphoreType.DMA((4,)),
        ],
        compiler_params=LIMIT,
        cost_estimate=cost(0, operands),
    )(*operands)


def gather_down(base, width, pieces):
    blocks = [p[0] for p in pieces]
    count = sum(len(p[2]) for p in pieces)
    units, cols = blocks[0].shape[1:]
    given = [] if base is None else [base]

    def kernel(*refs):
        ins, out = refs[: len(blocks)], refs[len(blocks) + len(given)]
        bufs, in_sems, out_sems = refs[len(blocks) + len(given) + 1 :]
        copies, stores, places = [], [], []
        for ref, (_, crossed, keys) in zip(ins, pieces):
            core = 1 - this_core() if crossed else this_core()
            for k, key in enumerate(keys):
                i = len(copies)
                places.append(column_place(key[0], key[1], core))
                copies.append(pltpu.make_async_copy(ref.at[k], bufs.at[i], in_sems.at[i]))
                copies[-1].start()
        for i in range(count):
            copies[i].wait()
            stores.append(
                pltpu.make_async_copy(bufs.at[i], columns(out, places[i], cols), out_sems.at[i])
            )
            stores[-1].start()
        for c in stores:
            c.wait()

    return pl.pallas_call(
        kernel,
        in_specs=[ANY] * (len(blocks) + len(given)),
        out_specs=ANY,
        out_shape=jax.ShapeDtypeStruct((units, width), BF16),
        input_output_aliases={len(blocks): 0} if given else {},
        scratch_shapes=[
            pltpu.VMEM((count, units, cols), BF16),
            pltpu.SemaphoreType.DMA((count,)),
            pltpu.SemaphoreType.DMA((count,)),
        ],
        compiler_params=LIMIT,
        cost_estimate=cost(0, (*blocks, *blocks)),
    )(*blocks, *given)


def per_device(grad_out, routes, combine, saved_hidden, down_weight):
    n_expert = lax.axis_size("expert")
    n_tensor = lax.axis_size("tensor")
    n_rep = lax.axis_size("dp")
    n_x = n_tensor // 2
    capacity = saved_hidden.shape[2]
    width = grad_out.shape[1]
    most = capacity // n_expert
    cols = width // (2 * n_tensor)
    weight, hidden = down_weight[0], saved_hidden[:, 0]

    def along_x(v, by):
        return lax.ppermute(
            v, "tensor", [(t, (t // 2 + by) % n_x * 2 + t % 2) for t in range(n_tensor)]
        )

    def along_y(v, by):
        return lax.ppermute(v, "dp", [(p, (p + by) % n_rep) for p in range(n_rep)])

    def to_core(v):
        return lax.ppermute(v, "tensor", [(t, t ^ 1) for t in range(n_tensor)])

    rows, target = pick(routes.T, combine.T, grad_out, cols, capacity, most)
    got = lax.all_to_all(
        rows.reshape(n_expert, most, 2 * cols), "expert", split_axis=0, concat_axis=0, tiled=True
    ).reshape(capacity, 2 * cols)
    sent, turned = prepare(weight, hidden, cols)
    sent, turned = to_core(sent), (turned, to_core(turned))
    got, sent, *turned = fence(got, sent, *turned)

    a, b = got[:, :cols], got[:, cols:]
    al, ar = along_x(a, 1), along_x(a, -1)
    bd, bu = along_y(b, 1), along_y(b, -1)
    hl, hr, hd, hu = halves(al, ar, bd, bu)
    a_low, a_high = along_x(hl, 1), along_x(hr, -1)
    b_low, b_high = along_y(hd, 1), along_y(hu, -1)
    a1, a2, b1, b2 = stack((a, al, ar, a_low, a_high), (b, bd, bu, b_low, b_high))
    first = along_y(a1, 1), along_y(a2, -1), along_x(b1, 1), along_x(b2, -1)
    own, other, g0, g0c, a1s, a2s, b1s, b2s = absorb(
        weight,
        sent,
        None,
        [(0, 0, 0, a1), (0, 0, 1, a2), (1, 0, 0, b1), (1, 0, 1, b2)],
        turned=turned,
        downs=(0,),
        again=True,
    )
    d1, u2, l1, r2, a1s, a2s, b1s, b2s = fence(*first, a1s, a2s, b1s, b2s)
    second = along_y(a2s, 1), along_y(a1s, -1), along_x(b2s, 1), along_x(b1s, -1)
    own, other = absorb(
        weight,
        sent,
        (own, other),
        [(0, 1, 0, d1), (0, 2, 1, u2), (1, 1, 0, l1), (1, 2, 1, r2)],
    )
    d1, u2, l1, r2, d2, u1, l2, r1, own, other = fence(d1, u2, l1, r2, *second, own, other)
    o1, o2, q1, q2 = along_y(d1, 1), along_y(u2, -1), along_x(l1, 1), along_x(r2, -1)
    own, other, g1, g1c = absorb(
        weight,
        sent,
        (own, other),
        [
            (0, 1, 1, d2),
            (0, 2, 0, u1),
            (1, 1, 1, l2),
            (1, 2, 0, r1),
            (1, 1, 0, l1, "down"),
            (1, 2, 1, r2, "down"),
        ],
        turned=turned,
        downs=(1, 2),
    )
    before = to_core(other)
    grad_down = gather_down(
        None,
        width,
        [
            (g0, False, [(0, 1)]),
            (g1, False, [(1, 1), (2, 1)]),
            (to_core(g0c), True, [(0, 1)]),
            (to_core(g1c), True, [(1, 1), (2, 1)]),
        ],
    )
    last = [(0, 3, 0, o1), (0, 3, 1, o2), (1, 3, 0, q1), (1, 3, 1, q2)]
    (other,) = absorb(weight, sent, None, last, sides=(1,))
    after = to_core(other)
    (own,) = absorb(weight, sent, (own,), last, sides=(0,))
    grad_hidden, partial = finish(own, before, after, hidden)
    g2, g2c = down([(a1, a2), (d1, d2), (u1, u2), (o1, o2)], (q1, q2), turned)
    spread = jnp.broadcast_to(
        partial.reshape(n_rep, n_expert, 1, most), (n_rep, n_expert, n_tensor, most)
    ).reshape(-1, 1, most)
    returned = lax.all_to_all(
        spread, ("dp", "expert", "tensor"), split_axis=0, concat_axis=0, tiled=True
    )
    at = [(0, 0), (1, 0), (2, 0), (3, 0), (3, 1)]
    grad_down = gather_down(grad_down, width, [(g2, False, at), (to_core(g2c), True, at)])
    sums = jnp.sum(returned.reshape(n_rep, n_expert, n_tensor, most), axis=(0, 2)).reshape(-1)
    slot = jnp.arange(capacity, dtype=jnp.int32).astype(F32)
    chosen = target[:, None] == slot[None, :, None]
    grad_combine = jnp.sum(jnp.where(chosen, sums[None, :, None], 0.0), axis=1) / combine.T.astype(F32)
    return grad_hidden[:, None], grad_down[None], grad_combine.T


def solution(mesh):
    return jax.shard_map(
        per_device,
        mesh=mesh,
        in_specs=(
            P(("dp", "expert"), None),
            P(("dp", "expert"), None),
            P(("dp", "expert"), None),
            P(None, "expert", None, ("dp", "tensor")),
            P("expert", ("dp", "tensor"), None),
        ),
        out_specs=(
            P(None, "expert", None, ("dp", "tensor")),
            P("expert", ("dp", "tensor"), None),
            P(("dp", "expert"), None),
        ),
        check_vma=False,
    )
```

```python
import jax
import jax.numpy as jnp
from jax import lax
from jax.experimental import pallas as pl
from jax.experimental.pallas import tpu as pltpu
from jax.sharding import PartitionSpec as P

F32, BF16 = jnp.float32, jnp.bfloat16
LIMIT = pltpu.CompilerParams(vmem_limit_bytes=28 * 1024 * 1024)
SMALL = pltpu.CompilerParams(vmem_limit_bytes=12 * 1024 * 1024)
LARGE = pltpu.CompilerParams(vmem_limit_bytes=60 * 1024 * 1024)
ANY = pl.BlockSpec(memory_space=pl.ANY)
VMEM = pl.BlockSpec(memory_space=pltpu.VMEM)
HBM = pl.BlockSpec(memory_space=pltpu.HBM)
NT = (((1,), (1,)), ((), ()))
OFFSETS = (0, -1, 1, 2)


def like(*arrays):
    return [jax.ShapeDtypeStruct(a.shape, a.dtype) for a in arrays]


def cost(flops, arrays):
    return pl.CostEstimate(
        flops=flops,
        bytes_accessed=sum(a.size * a.dtype.itemsize for a in arrays),
        transcendentals=0,
    )


def ring_place(axis, by, cores):
    return lax.rem(lax.axis_index(axis) // cores + (OFFSETS[by] + 4), 4)


def column_place(k, kind, core):
    return 4 * ring_place("tensor", k, 2) + 2 * kind + core


def this_core():
    return lax.rem(lax.axis_index("tensor"), 2)


def columns(ref, place, cols):
    return ref.at[:, pl.ds(pl.multiple_of(place * cols, 128), cols)]


def pick(routes, combine, grad_out, cols, slots, most):
    tokens = grad_out.shape[0]

    def kernel(routes, combine, grad, out, target, rows, sems):
        copies = [
            pltpu.make_async_copy(
                columns(grad, column_place(0, kind, this_core()), cols), rows.at[kind], sems.at[kind]
            )
            for kind in range(2)
        ]
        for c in copies:
            c.start()
        expert = lax.broadcasted_iota(jnp.int32, (8, tokens), 0)
        named = [routes[k : k + 1, :] for k in range(2)]
        hits = [(n == expert).astype(F32) for n in named]
        earlier = lax.broadcasted_iota(jnp.int32, (tokens, tokens), 0)
        later = lax.broadcasted_iota(jnp.int32, (tokens, tokens), 1)
        before = jnp.dot(
            (hits[0] + hits[1]).astype(BF16),
            (earlier < later).astype(F32).astype(BF16),
            preferred_element_type=F32,
        )
        slot = lax.broadcasted_iota(jnp.int32, (slots, tokens), 0).astype(F32)
        picker = None
        for k in range(2):
            rank = jnp.sum(hits[k] * before, axis=0, keepdims=True)
            where = named[k].astype(F32) * float(most) + rank
            target[k : k + 1, :] = where
            term = jnp.where(where == slot, combine[k : k + 1, :].astype(F32), 0.0)
            picker = term if picker is None else picker + term
        picker = picker.astype(BF16)
        for kind in range(2):
            copies[kind].wait()
            found = jnp.dot(picker, rows[kind], preferred_element_type=F32)
            out[:, kind * cols : (kind + 1) * cols] = found.astype(BF16)

    return pl.pallas_call(
        kernel,
        in_specs=[VMEM, VMEM, HBM],
        out_specs=[VMEM, VMEM],
        out_shape=[
            jax.ShapeDtypeStruct((slots, 2 * cols), BF16),
            jax.ShapeDtypeStruct((2, tokens), F32),
        ],
        scratch_shapes=[pltpu.VMEM((2, tokens, cols), BF16), pltpu.SemaphoreType.DMA((2,))],
        compiler_params=LARGE,
        cost_estimate=pl.CostEstimate(
            flops=4 * tokens * slots * cols, bytes_accessed=8 * slots * cols, transcendentals=0
        ),
    )(routes, combine, grad_out)


def turn(hidden, crossed):
    n_rep, slots, units = hidden.shape

    def kernel(hidden, crossed, turned, held, sems):
        copies = []
        for j in range(4):
            for i, ref in enumerate((hidden, crossed)):
                copies.append(
                    pltpu.make_async_copy(
                        ref.at[ring_place("dp", j, 1)], held.at[j, i], sems.at[2 * j + i]
                    )
                )
                copies[-1].start()
        for j in range(4):
            for i in range(2):
                copies[2 * j + i].wait()
                turned[j, i * units : (i + 1) * units] = held[j, i].astype(F32).T.astype(BF16)

    return pl.pallas_call(
        kernel,
        in_specs=[HBM, HBM],
        out_specs=VMEM,
        out_shape=jax.ShapeDtypeStruct((4, 2 * units, slots), BF16),
        scratch_shapes=[pltpu.VMEM((4, 2, slots, units), BF16), pltpu.SemaphoreType.DMA((8,))],
        compiler_params=SMALL,
        cost_estimate=cost(0, (hidden, hidden, hidden, hidden)),
    )(hidden, crossed)


def fence(*arrays):
    return pl.pallas_call(
        lambda *refs: None,
        out_shape=like(*arrays),
        in_specs=[ANY] * len(arrays),
        out_specs=[ANY] * len(arrays),
        input_output_aliases={i: i for i in range(len(arrays))},
        compiler_params=pltpu.CompilerParams(
            has_side_effects=True, vmem_limit_bytes=1024 * 1024
        ),
    )(*arrays)


def settled(*arrays):
    def kernel(*refs):
        refs[-1][...] = jnp.zeros_like(refs[-1])

    n = len(arrays)
    return pl.pallas_call(
        kernel,
        out_shape=like(*arrays) + [jax.ShapeDtypeStruct((8, 128), F32)],
        in_specs=[HBM] * n,
        out_specs=[HBM] * n + [VMEM],
        input_output_aliases={i: i for i in range(n)},
        compiler_params=pltpu.CompilerParams(vmem_limit_bytes=1024 * 1024),
    )(*arrays)


def halves(left, right, down, up):
    def kernel(*refs):
        for i in range(4):
            refs[4 + i][...] = refs[i][...]

    rows, cols = left.shape
    lower = pl.BlockSpec((rows // 2, cols), lambda i: (0, 0))
    upper = pl.BlockSpec((rows // 2, cols), lambda i: (1, 0))
    return pl.pallas_call(
        kernel,
        grid=(1,),
        in_specs=[lower, upper, lower, upper],
        out_specs=[lower] * 4,
        out_shape=[jax.ShapeDtypeStruct((rows // 2, cols), left.dtype)] * 4,
        compiler_params=SMALL,
    )(left, right, down, up)


def stack(a_parts, b_parts, token):
    rows, cols = a_parts[0].shape

    def kernel(*refs):
        ins, outs, sems = refs[:10], refs[11:19], refs[19]
        copies = []
        for twice in range(2):
            for kind in range(2):
                own, prev, after, low, high = ins[5 * kind : 5 * kind + 5]
                first, second = outs[4 * twice + 2 * kind : 4 * twice + 2 * kind + 2]
                for src, dst in (
                    (own, first.at[0]),
                    (prev, first.at[1]),
                    (after, second.at[0]),
                    (low, second.at[1, : rows // 2]),
                    (high, second.at[1, rows // 2 :]),
                ):
                    copies.append(pltpu.make_async_copy(src, dst, sems.at[len(copies)]))
                    copies[-1].start()
        for c in copies:
            c.wait()

    return pl.pallas_call(
        kernel,
        in_specs=[ANY] * 11,
        out_specs=[VMEM] * 8,
        out_shape=[jax.ShapeDtypeStruct((2, rows, cols), BF16)] * 8,
        scratch_shapes=[pltpu.SemaphoreType.DMA((20,))],
        compiler_params=SMALL,
    )(*a_parts, *b_parts, token)


def absorb(weight, sent, before, parts, sides=(0, 1), crossed=False, turned=None, downs=(), kinds=(F32, F32), hidden=None):
    arrays = [p[3] for p in parts]
    used = [i for i, p in enumerate(parts) if p[4]]

    def keys_of(i):
        what, off, pair = parts[i][:3]
        return [(2 * pair, 0), (2 * pair + 1, 0)] if what == 0 else [(off, 1)] * 2

    keys = sorted({key for i in used for key in keys_of(i)})
    n, m, s = len(arrays), len(keys), len(sides)
    rows, cols = arrays[0].shape[1:]
    units = weight.shape[0]
    olds = [a for side in before for a in side]
    n_old = [len(side) for side in before]
    turned = [] if turned is None else [turned]
    last = [] if hidden is None else [hidden]
    operands = arrays + [weight, sent] + turned + olds + last
    n_sum = 2 if last else s
    n_out = n_sum + (2 if downs else 0)

    def kernel(*refs):
        refs = list(refs)

        def take(count):
            taken = refs[:count]
            del refs[:count]
            return taken

        bufs, (w_ref, s_ref) = take(n), take(2)
        t, held, hid_ref = take(len(turned)), take(len(olds)), take(len(last))
        outs, (wbuf,) = take(n_out), take(1)
        hid, rounded = take(2) if last else (None, None)
        (sems,) = take(1)
        started = []

        def start(src, dst):
            copy = pltpu.make_async_copy(src, dst, sems.at[len(started)])
            copy.start()
            started.append(copy)
            return copy

        waiting = {}

        def ready(*what):
            for c in waiting[what]:
                c.wait()
            waiting[what] = []

        def of(j):
            return [
                (i, k, key)
                for i in used
                for k, key in enumerate(keys_of(i))
                if (parts[i][1] if parts[i][0] == 0 else 2 * parts[i][2] + k) == j
            ]

        core = 1 - this_core() if crossed else this_core()
        for j in range(4):
            for _, _, key in of(j):
                if ("w", key) in waiting:
                    continue
                waiting["w", key] = [
                    start(
                        columns(s_ref if side else w_ref, column_place(key[0], key[1], core), cols),
                        wbuf.at[keys.index(key), pl.ds(where * units, units)],
                    )
                    for where, side in enumerate(sides)
                ]
            if last:
                waiting["h", j] = [start(hid_ref[0].at[ring_place("dp", j, 1)], hid.at[j])]
        stores = []
        for g, off in enumerate(downs):
            down = None
            for i, part in enumerate(parts):
                if part[0] == 1 and part[1] == off:
                    for k in range(2):
                        term = jnp.dot(
                            t[0][2 * part[2] + k], bufs[i][k], preferred_element_type=F32
                        )
                        down = term if down is None else down + term
            for side in range(2):
                outs[n_sum + side][g] = down[side * units : (side + 1) * units].astype(BF16)
        for j in range(4):
            total = None
            for i, k, key in of(j):
                ready("w", key)
                term = lax.dot_general(
                    bufs[i][k], wbuf[keys.index(key)], NT, preferred_element_type=F32
                )
                total = term if total is None else total + term
            at = 0
            for where in range(s):
                mine = None if total is None else total[:, where * units : (where + 1) * units]
                for h in held[at : at + (n_old[where] if n_old else 0)]:
                    old = h[j].astype(F32)
                    mine = old if mine is None else mine + old
                at += n_old[where] if n_old else 0
                if last:
                    ready("h", j)
                    place = ring_place("dp", j, 1)
                    rounded[j] = mine.astype(BF16)
                    stores.append(start(rounded.at[j], outs[0].at[place]))
                    prod = mine * hid[j].astype(F32)
                    folded = sum(prod[:, c : c + 128] for c in range(0, units, 128))
                    outs[1][pl.ds(place, 1), :] = jnp.sum(folded.T, axis=0, keepdims=True)
                else:
                    outs[where][j] = mine.astype(kinds[where])
        for c in stores:
            c.wait()

    if last:
        out_shape = [
            jax.ShapeDtypeStruct((4, rows, units), BF16),
            jax.ShapeDtypeStruct((4, rows), F32),
        ]
        out_specs = [HBM, VMEM]
    else:
        out_shape = [jax.ShapeDtypeStruct((4, rows, units), kinds[i]) for i in range(s)]
        out_specs = [VMEM] * s
    if downs:
        out_shape += [jax.ShapeDtypeStruct((len(downs), units, cols), BF16)] * 2
        out_specs = out_specs + [VMEM] * 2
    scratch = [pltpu.VMEM((m, s * units, cols), BF16)]
    if last:
        scratch += [pltpu.VMEM((4, rows, units), BF16)] * 2
    scratch.append(pltpu.SemaphoreType.DMA((s * m + 8,)))
    flops = 4 * rows * cols * units * (s * len(used) + 2 * 2 * len(downs))
    return pl.pallas_call(
        kernel,
        in_specs=[VMEM] * n + [HBM] * 2 + [VMEM] * (len(turned) + len(olds)) + [HBM] * len(last),
        out_specs=out_specs,
        out_shape=out_shape,
        scratch_shapes=scratch,
        compiler_params=LIMIT,
        cost_estimate=cost(flops, operands),
    )(*operands)


def first_down(pair, turned):
    both, rows = turned.shape[1:]
    units, cols = both // 2, pair[0].shape[2]

    def kernel(first, second, t, own, other):
        total = None
        for j in range(4):
            part = jnp.dot(t[j], (first, second)[j // 2][j % 2], preferred_element_type=F32)
            total = part if total is None else total + part
        own[0] = total[:units].astype(BF16)
        other[0] = total[units:].astype(BF16)

    return pl.pallas_call(
        kernel,
        in_specs=[VMEM] * 3,
        out_specs=[VMEM] * 2,
        out_shape=[jax.ShapeDtypeStruct((1, units, cols), BF16)] * 2,
        compiler_params=SMALL,
        cost_estimate=cost(8 * rows * both * cols, (*pair, turned)),
    )(*pair, turned)


def early_down(groups, turned):
    both, rows = turned.shape[1:]
    cols = groups[0][0].shape[2]
    arrays = [r for g in groups for r in g]

    def kernel(*refs):
        ins, t, sums = refs[:-2], refs[-2], refs[-1]
        for k in range(4):
            total = None
            for j in range(len(groups)):
                part = jnp.dot(t[j], ins[2 * j + k // 2][k % 2], preferred_element_type=F32)
                total = part if total is None else total + part
            sums[k] = total

    return pl.pallas_call(
        kernel,
        in_specs=[VMEM] * (len(arrays) + 1),
        out_specs=VMEM,
        out_shape=jax.ShapeDtypeStruct((4, both, cols), F32),
        compiler_params=LIMIT,
        cost_estimate=cost(8 * len(groups) * rows * both * cols, (*arrays, turned)),
    )(*arrays, turned)


def last_down(sums, a_pair, b_pair, turned, base, after):
    both, rows = turned.shape[1:]
    units = both // 2
    cols = a_pair[0].shape[2]
    keys = [(0, 0), (1, 0), (2, 0), (3, 0), (3, 1)]

    def kernel(sums, a1, a2, b1, b2, t, _, after, out, other, own, sems):
        stores = []
        for k in range(5):
            if k < 4:
                total = sums[k] + jnp.dot(
                    t[3], (a1, a2)[k // 2][k % 2], preferred_element_type=F32
                )
            else:
                total = None
                for j in range(4):
                    part = jnp.dot(t[j], (b1, b2)[j // 2][j % 2], preferred_element_type=F32)
                    total = part if total is None else total + part
            other[k] = total[units:].astype(BF16)
            own[k] = total[:units].astype(BF16)
            to = columns(out, column_place(keys[k][0], keys[k][1], this_core()), cols)
            stores.append(pltpu.make_async_copy(own.at[k], to, sems.at[k]))
            stores[-1].start()
        for c in stores:
            c.wait()

    operands = [sums, *a_pair, *b_pair, turned, base, after]
    return pl.pallas_call(
        kernel,
        in_specs=[VMEM] * 6 + [HBM, ANY],
        out_specs=[HBM, VMEM],
        out_shape=like(base) + [jax.ShapeDtypeStruct((5, units, cols), BF16)],
        input_output_aliases={6: 0},
        scratch_shapes=[pltpu.VMEM((5, units, cols), BF16), pltpu.SemaphoreType.DMA((5,))],
        compiler_params=LIMIT,
        cost_estimate=cost(16 * rows * both * cols, operands[:6]),
    )(*operands)


def gather_down(base, width, pieces):
    blocks = [p[0] for p in pieces]
    count = sum(len(p[2]) for p in pieces)
    units, cols = blocks[0].shape[1:]
    given = [] if base is None else [base]

    def kernel(*refs):
        ins, out = refs[: len(blocks)], refs[len(blocks) + len(given)]
        bufs, in_sems, out_sems = refs[len(blocks) + len(given) + 1 :]
        copies, stores, places = [], [], []
        for ref, (_, crossed, keys) in zip(ins, pieces):
            core = 1 - this_core() if crossed else this_core()
            for k, key in enumerate(keys):
                i = len(copies)
                places.append(column_place(key[0], key[1], core))
                copies.append(pltpu.make_async_copy(ref.at[k], bufs.at[i], in_sems.at[i]))
                copies[-1].start()
        for i in range(count):
            copies[i].wait()
            stores.append(
                pltpu.make_async_copy(bufs.at[i], columns(out, places[i], cols), out_sems.at[i])
            )
            stores[-1].start()
        for c in stores:
            c.wait()

    return pl.pallas_call(
        kernel,
        in_specs=[ANY] * len(blocks) + [HBM] * len(given),
        out_specs=HBM,
        out_shape=jax.ShapeDtypeStruct((units, width), BF16),
        input_output_aliases={len(blocks): 0} if given else {},
        scratch_shapes=[
            pltpu.VMEM((count, units, cols), BF16),
            pltpu.SemaphoreType.DMA((count,)),
            pltpu.SemaphoreType.DMA((count,)),
        ],
        compiler_params=SMALL,
        cost_estimate=cost(0, (*blocks, *blocks)),
    )(*blocks, *given)


def per_device(grad_out, routes, combine, saved_hidden, down_weight):
    n_expert = lax.axis_size("expert")
    n_tensor = lax.axis_size("tensor")
    n_rep = lax.axis_size("dp")
    n_x = n_tensor // 2
    capacity = saved_hidden.shape[2]
    width = grad_out.shape[1]
    most = capacity // n_expert
    cols = width // (2 * n_tensor)
    weight, hidden = down_weight[0], saved_hidden[:, 0]

    def along_x(v, by):
        return lax.ppermute(
            v, "tensor", [(t, (t // 2 + by) % n_x * 2 + t % 2) for t in range(n_tensor)]
        )

    def along_y(v, by):
        return lax.ppermute(v, "dp", [(p, (p + by) % n_rep) for p in range(n_rep)])

    def to_core(v):
        return lax.ppermute(v, "tensor", [(t, t ^ 1) for t in range(n_tensor)])

    sent, crossed = to_core(weight), to_core(hidden)
    rows, target = pick(routes.T, combine.T, grad_out, cols, capacity, most)
    got = lax.all_to_all(
        rows.reshape(n_expert, most, 2 * cols), "expert", split_axis=0, concat_axis=0, tiled=True
    ).reshape(capacity, 2 * cols)
    sent, crossed, token = settled(sent, crossed)
    got, _ = fence(got, token)

    a, b = got[:, :cols], got[:, cols:]
    al, ar = along_x(a, 1), along_x(a, -1)
    bd, bu = along_y(b, 1), along_y(b, -1)
    hl, hr, hd, hu = halves(al, ar, bd, bu)
    a_low, a_high = along_x(hl, 1), along_x(hr, -1)
    b_low, b_high = along_y(hd, 1), along_y(hu, -1)
    a1, a2, b1, b2, a1s, a2s, b1s, b2s = stack(
        (a, al, ar, a_low, a_high), (b, bd, bu, b_low, b_high), token
    )
    d1, u2, l1, r2 = along_y(a1, 1), along_y(a2, -1), along_x(b1, 1), along_x(b2, -1)
    turned = turn(hidden, crossed)
    g0, g0c = first_down((b1, b2), turned)
    d1, a2s = fence(d1, a2s)
    u2, a1s = fence(u2, a1s)
    l1, b2s = fence(l1, b2s)
    r2, b1s, g0, g0c = fence(r2, b1s, g0, g0c)
    second = along_y(a2s, 1), along_y(a1s, -1), along_x(b2s, 1), along_x(b1s, -1)
    own, other = absorb(
        weight,
        sent,
        (),
        [
            (0, 0, 0, a1, True),
            (0, 0, 1, a2, True),
            (1, 0, 0, b1, True),
            (1, 0, 1, b2, True),
            (0, 1, 0, d1, True),
            (0, 2, 1, u2, True),
            (1, 1, 0, l1, True),
            (1, 2, 1, r2, True),
        ],
    )
    d1, u2, l1, r2, d2, u1, l2, r1, own, other = fence(
        d1, u2, l1, r2, *second, own, other
    )
    o1, o2, q1, q2 = along_y(d1, 1), along_y(u2, -1), along_x(l1, 1), along_x(r2, -1)
    own, other, g1, g1c = absorb(
        weight,
        sent,
        ((own,), (other,)),
        [
            (0, 1, 1, d2, True),
            (0, 2, 0, u1, True),
            (1, 1, 1, l2, True),
            (1, 2, 0, r1, True),
            (1, 1, 0, l1, False),
            (1, 2, 1, r2, False),
        ],
        turned=turned,
        downs=(1, 2),
        kinds=(F32, BF16),
    )
    sums = early_down([(a1, a2), (d1, d2), (u1, u2)], turned)
    other, g0c, g1c, q2, sums = fence(other, g0c, g1c, q2, sums)
    grad_down = gather_down(
        None,
        width,
        [
            (g0, False, [(0, 1)]),
            (g1, False, [(1, 1), (2, 1)]),
            (to_core(g0c), True, [(0, 1)]),
            (to_core(g1c), True, [(1, 1), (2, 1)]),
        ],
    )
    last = [(0, 3, 0, o1, True), (0, 3, 1, o2, True), (1, 3, 0, q1, True), (1, 3, 1, q2, True)]
    crossing = [(*part[:3], to_core(part[3]), True) for part in last]
    (own,) = absorb(weight, sent, ((own,),), last, sides=(0,))
    grad_hidden, partial = absorb(
        weight, sent, ((own, to_core(other)),), crossing, sides=(0,), crossed=True, hidden=hidden
    )
    grad_down, g2c = last_down(
        sums, (o1, o2), (q1, q2), turned, grad_down, partial
    )
    partial = partial + to_core(partial)
    partial = partial + along_x(partial, 1) + along_x(partial, -1) + along_x(partial, 2)
    partial, g2c = fence(partial, g2c)
    returned = lax.all_to_all(
        partial.reshape(n_rep * n_expert, 1, most),
        ("dp", "expert"),
        split_axis=0,
        concat_axis=0,
        tiled=True,
    )
    at = [(0, 0), (1, 0), (2, 0), (3, 0), (3, 1)]
    grad_down = gather_down(grad_down, width, [(to_core(g2c), True, at)])
    returned, grad_down = fence(returned, grad_down)
    whole = jnp.sum(returned.reshape(n_rep, capacity), axis=0)
    slot = jnp.arange(capacity, dtype=jnp.int32).astype(F32)
    chosen = target[:, None] == slot[None, :, None]
    grad_combine = jnp.sum(jnp.where(chosen, whole[None, :, None], 0.0), axis=1) / combine.T.astype(F32)
    return grad_hidden[:, None], grad_down[None], grad_combine.T


def solution(mesh):
    return jax.shard_map(
        per_device,
        mesh=mesh,
        in_specs=(
            P(("dp", "expert"), None),
            P(("dp", "expert"), None),
            P(("dp", "expert"), None),
            P(None, "expert", None, ("dp", "tensor")),
            P("expert", ("dp", "tensor"), None),
        ),
        out_specs=(
            P(None, "expert", None, ("dp", "tensor")),
            P("expert", ("dp", "tensor"), None),
            P(("dp", "expert"), None),
        ),
        check_vma=False,
    )
```

```python
import jax
import jax.numpy as jnp
from jax import lax
from jax.experimental import pallas as pl
from jax.experimental.pallas import tpu as pltpu
from jax.sharding import Mesh
from jax.sharding import PartitionSpec as P

F32, BF16 = jnp.float32, jnp.bfloat16
LIMIT = pltpu.CompilerParams(vmem_limit_bytes=28 * 1024 * 1024)
SMALL = pltpu.CompilerParams(vmem_limit_bytes=12 * 1024 * 1024)
LARGE = pltpu.CompilerParams(vmem_limit_bytes=60 * 1024 * 1024)
ANY = pl.BlockSpec(memory_space=pl.ANY)
VMEM = pl.BlockSpec(memory_space=pltpu.VMEM)
HBM = pl.BlockSpec(memory_space=pltpu.HBM)
NT = (((1,), (1,)), ((), ()))
OFFSETS = (0, -1, 1, 2)


def like(*arrays):
    return [jax.ShapeDtypeStruct(a.shape, a.dtype) for a in arrays]


def cost(flops, arrays):
    return pl.CostEstimate(
        flops=flops,
        bytes_accessed=sum(a.size * a.dtype.itemsize for a in arrays),
        transcendentals=0,
    )


def ring_place(axis, by):
    return lax.rem(lax.axis_index(axis) + (OFFSETS[by] + 4), 4)


def column_place(k, kind, core):
    return 4 * ring_place("x", k) + 2 * kind + core


def this_core():
    return lax.axis_index("core")


def columns(ref, place, cols):
    return ref.at[:, pl.ds(pl.multiple_of(place * cols, 128), cols)]


def pick(routes, combine, grad_out, cols, slots, most):
    tokens = grad_out.shape[0]

    def kernel(routes, combine, grad, out, target, rows, sems):
        copies = [
            pltpu.make_async_copy(
                columns(grad, column_place(0, kind, this_core()), cols), rows.at[kind], sems.at[kind]
            )
            for kind in range(2)
        ]
        for c in copies:
            c.start()
        expert = lax.broadcasted_iota(jnp.int32, (8, tokens), 0)
        named = [routes[k : k + 1, :] for k in range(2)]
        hits = [(n == expert).astype(F32) for n in named]
        earlier = lax.broadcasted_iota(jnp.int32, (tokens, tokens), 0)
        later = lax.broadcasted_iota(jnp.int32, (tokens, tokens), 1)
        before = jnp.dot(
            (hits[0] + hits[1]).astype(BF16),
            (earlier < later).astype(F32).astype(BF16),
            preferred_element_type=F32,
        )
        slot = lax.broadcasted_iota(jnp.int32, (slots, tokens), 0).astype(F32)
        picker = None
        for k in range(2):
            rank = jnp.sum(hits[k] * before, axis=0, keepdims=True)
            where = named[k].astype(F32) * float(most) + rank
            target[k : k + 1, :] = where
            term = jnp.where(where == slot, combine[k : k + 1, :].astype(F32), 0.0)
            picker = term if picker is None else picker + term
        picker = picker.astype(BF16)
        for kind in range(2):
            copies[kind].wait()
            found = jnp.dot(picker, rows[kind], preferred_element_type=F32)
            out[:, kind * cols : (kind + 1) * cols] = found.astype(BF16)

    return pl.pallas_call(
        kernel,
        in_specs=[VMEM, VMEM, HBM],
        out_specs=[VMEM, VMEM],
        out_shape=[
            jax.ShapeDtypeStruct((slots, 2 * cols), BF16),
            jax.ShapeDtypeStruct((2, tokens), F32),
        ],
        scratch_shapes=[pltpu.VMEM((2, tokens, cols), BF16), pltpu.SemaphoreType.DMA((2,))],
        compiler_params=LARGE,
        cost_estimate=pl.CostEstimate(
            flops=4 * tokens * slots * cols, bytes_accessed=8 * slots * cols, transcendentals=0
        ),
    )(routes, combine, grad_out)


def turn(hidden, crossed):
    n_rep, slots, units = hidden.shape

    def kernel(hidden, crossed, turned, held, sems):
        copies = []
        for j in range(4):
            for i, ref in enumerate((hidden, crossed)):
                copies.append(
                    pltpu.make_async_copy(
                        ref.at[ring_place("dp", j)], held.at[j, i], sems.at[2 * j + i]
                    )
                )
                copies[-1].start()
        for j in range(4):
            for i in range(2):
                copies[2 * j + i].wait()
                turned[j, i * units : (i + 1) * units] = held[j, i].astype(F32).T.astype(BF16)

    return pl.pallas_call(
        kernel,
        in_specs=[HBM, HBM],
        out_specs=VMEM,
        out_shape=jax.ShapeDtypeStruct((4, 2 * units, slots), BF16),
        scratch_shapes=[pltpu.VMEM((4, 2, slots, units), BF16), pltpu.SemaphoreType.DMA((8,))],
        compiler_params=SMALL,
        cost_estimate=cost(0, (hidden, hidden, hidden, hidden)),
    )(hidden, crossed)


def fence(*arrays):
    return pl.pallas_call(
        lambda *refs: None,
        out_shape=like(*arrays),
        in_specs=[ANY] * len(arrays),
        out_specs=[ANY] * len(arrays),
        input_output_aliases={i: i for i in range(len(arrays))},
        compiler_params=pltpu.CompilerParams(
            has_side_effects=True, vmem_limit_bytes=1024 * 1024
        ),
    )(*arrays)


def settled(*arrays):
    def kernel(*refs):
        refs[-1][...] = jnp.zeros_like(refs[-1])

    n = len(arrays)
    return pl.pallas_call(
        kernel,
        out_shape=like(*arrays) + [jax.ShapeDtypeStruct((8, 128), F32)],
        in_specs=[HBM] * n,
        out_specs=[HBM] * n + [VMEM],
        input_output_aliases={i: i for i in range(n)},
        compiler_params=pltpu.CompilerParams(vmem_limit_bytes=1024 * 1024),
    )(*arrays)


def stack(copies, *pairs, after=()):
    rows, cols = pairs[0][0].shape
    ins = [a for pair in pairs for a in pair]
    n = len(pairs)

    def kernel(*refs):
        outs, sems = refs[2 * n + len(after) : -1], refs[-1]
        started = []
        for i in range(n):
            for out in outs[i * copies : (i + 1) * copies]:
                for k in range(2):
                    started.append(
                        pltpu.make_async_copy(refs[2 * i + k], out.at[k], sems.at[len(started)])
                    )
                    started[-1].start()
        for c in started:
            c.wait()

    return pl.pallas_call(
        kernel,
        in_specs=[ANY] * (2 * n + len(after)),
        out_specs=[VMEM] * (n * copies),
        out_shape=[jax.ShapeDtypeStruct((2, rows, cols), BF16)] * (n * copies),
        scratch_shapes=[pltpu.SemaphoreType.DMA((2 * n * copies,))],
        compiler_params=SMALL,
    )(*ins, *after)


def absorb(weight, sent, before, parts, sides=(0, 1), crossed=False, turned=None, downs=(), kinds=(F32, F32), hidden=None, after=None):
    arrays = [p[3] for p in parts]
    used = [i for i, p in enumerate(parts) if p[4]]

    def keys_of(i):
        what, off, pair = parts[i][:3]
        return [(2 * pair, 0), (2 * pair + 1, 0)] if what == 0 else [(off, 1)] * 2

    keys = sorted({key for i in used for key in keys_of(i)})
    n, m, s = len(arrays), len(keys), len(sides)
    rows, cols = arrays[0].shape[1:]
    units = weight.shape[0]
    olds = [a for side in before for a in side]
    n_old = [len(side) for side in before]
    turned = [] if turned is None else [turned]
    last = [] if hidden is None else [hidden]
    extra = [] if after is None else [after]
    operands = arrays + [weight, sent] + turned + olds + last + extra
    n_sum = 2 if last else s
    n_out = n_sum + (2 if downs else 0)

    def kernel(*refs):
        refs = list(refs)

        def take(count):
            taken = refs[:count]
            del refs[:count]
            return taken

        bufs, (w_ref, s_ref) = take(n), take(2)
        t, held, hid_ref = take(len(turned)), take(len(olds)), take(len(last))
        take(len(extra))
        outs, (wbuf,) = take(n_out), take(1)
        hid, rounded = take(2) if last else (None, None)
        (sems,) = take(1)
        started = []

        def start(src, dst):
            copy = pltpu.make_async_copy(src, dst, sems.at[len(started)])
            copy.start()
            started.append(copy)
            return copy

        waiting = {}

        def ready(*what):
            for c in waiting[what]:
                c.wait()
            waiting[what] = []

        def of(j):
            return [
                (i, k, key)
                for i in used
                for k, key in enumerate(keys_of(i))
                if (parts[i][1] if parts[i][0] == 0 else 2 * parts[i][2] + k) == j
            ]

        core = 1 - this_core() if crossed else this_core()
        for j in range(4):
            for _, _, key in of(j):
                if ("w", key) in waiting:
                    continue
                waiting["w", key] = [
                    start(
                        columns(s_ref if side else w_ref, column_place(key[0], key[1], core), cols),
                        wbuf.at[keys.index(key), pl.ds(where * units, units)],
                    )
                    for where, side in enumerate(sides)
                ]
            if last:
                waiting["h", j] = [start(hid_ref[0].at[ring_place("dp", j)], hid.at[j])]
        stores = []
        for g, off in enumerate(downs):
            down = None
            for i, part in enumerate(parts):
                if part[0] == 1 and part[1] == off:
                    for k in range(2):
                        term = jnp.dot(
                            t[0][2 * part[2] + k], bufs[i][k], preferred_element_type=F32
                        )
                        down = term if down is None else down + term
            for side in range(2):
                outs[n_sum + side][g] = down[side * units : (side + 1) * units].astype(BF16)
        for j in range(4):
            total = None
            for i, k, key in of(j):
                ready("w", key)
                term = lax.dot_general(
                    bufs[i][k], wbuf[keys.index(key)], NT, preferred_element_type=F32
                )
                total = term if total is None else total + term
            at = 0
            for where in range(s):
                mine = None if total is None else total[:, where * units : (where + 1) * units]
                for h in held[at : at + (n_old[where] if n_old else 0)]:
                    old = h[j].astype(F32)
                    mine = old if mine is None else mine + old
                at += n_old[where] if n_old else 0
                if last:
                    ready("h", j)
                    place = ring_place("dp", j)
                    rounded[j] = mine.astype(BF16)
                    stores.append(start(rounded.at[j], outs[0].at[place]))
                    prod = mine * hid[j].astype(F32)
                    folded = sum(prod[:, c : c + 128] for c in range(0, units, 128))
                    outs[1][pl.ds(place, 1), :] = jnp.sum(folded.T, axis=0, keepdims=True)
                else:
                    outs[where][j] = mine.astype(kinds[where])
        for c in stores:
            c.wait()

    if last:
        out_shape = [
            jax.ShapeDtypeStruct((4, rows, units), BF16),
            jax.ShapeDtypeStruct((4, rows), F32),
        ]
        out_specs = [HBM, VMEM]
    else:
        out_shape = [jax.ShapeDtypeStruct((4, rows, units), kinds[i]) for i in range(s)]
        out_specs = [VMEM] * s
    if downs:
        out_shape += [jax.ShapeDtypeStruct((len(downs), units, cols), BF16)] * 2
        out_specs = out_specs + [VMEM] * 2
    scratch = [pltpu.VMEM((m, s * units, cols), BF16)]
    if last:
        scratch += [pltpu.VMEM((4, rows, units), BF16)] * 2
    scratch.append(pltpu.SemaphoreType.DMA((s * m + 8,)))
    flops = 4 * rows * cols * units * (s * len(used) + 2 * 2 * len(downs))
    return pl.pallas_call(
        kernel,
        in_specs=[VMEM] * n + [HBM] * 2 + [VMEM] * (len(turned) + len(olds)) + [HBM] * len(last) + [ANY] * len(extra),
        out_specs=out_specs,
        out_shape=out_shape,
        scratch_shapes=scratch,
        compiler_params=LIMIT,
        cost_estimate=cost(flops, operands),
    )(*operands)


def first_down(pair, turned):
    both, rows = turned.shape[1:]
    units, cols = both // 2, pair[0].shape[2]

    def kernel(first, second, t, own, other):
        total = None
        for j in range(4):
            part = jnp.dot(t[j], (first, second)[j // 2][j % 2], preferred_element_type=F32)
            total = part if total is None else total + part
        own[0] = total[:units].astype(BF16)
        other[0] = total[units:].astype(BF16)

    return pl.pallas_call(
        kernel,
        in_specs=[VMEM] * 3,
        out_specs=[VMEM] * 2,
        out_shape=[jax.ShapeDtypeStruct((1, units, cols), BF16)] * 2,
        compiler_params=SMALL,
        cost_estimate=cost(8 * rows * both * cols, (*pair, turned)),
    )(*pair, turned)


def early_down(groups, turned):
    both, rows = turned.shape[1:]
    cols = groups[0][0].shape[2]
    arrays = [r for g in groups for r in g]

    def kernel(*refs):
        ins, t, sums = refs[:-2], refs[-2], refs[-1]
        for k in range(4):
            total = None
            for j in range(len(groups)):
                part = jnp.dot(t[j], ins[2 * j + k // 2][k % 2], preferred_element_type=F32)
                total = part if total is None else total + part
            sums[k] = total

    return pl.pallas_call(
        kernel,
        in_specs=[VMEM] * (len(arrays) + 1),
        out_specs=VMEM,
        out_shape=jax.ShapeDtypeStruct((4, both, cols), F32),
        compiler_params=LIMIT,
        cost_estimate=cost(8 * len(groups) * rows * both * cols, (*arrays, turned)),
    )(*arrays, turned)


def last_down(sums, a_pair, b_pair, turned, after):
    both, rows = turned.shape[1:]
    units = both // 2
    cols = a_pair[0].shape[2]

    def kernel(sums, a1, a2, b1, b2, t, _, own, other):
        for k in range(5):
            if k < 4:
                total = sums[k] + jnp.dot(
                    t[3], (a1, a2)[k // 2][k % 2], preferred_element_type=F32
                )
            else:
                total = None
                for j in range(4):
                    part = jnp.dot(t[j], (b1, b2)[j // 2][j % 2], preferred_element_type=F32)
                    total = part if total is None else total + part
            other[k] = total[units:].astype(BF16)
            own[k] = total[:units].astype(BF16)

    operands = [sums, *a_pair, *b_pair, turned, after]
    return pl.pallas_call(
        kernel,
        in_specs=[VMEM] * 6 + [ANY],
        out_specs=[VMEM] * 2,
        out_shape=[jax.ShapeDtypeStruct((5, units, cols), BF16)] * 2,
        compiler_params=LIMIT,
        cost_estimate=cost(16 * rows * both * cols, operands),
    )(*operands)


def gather_down(width, pieces):
    blocks = [p[0] for p in pieces]
    count = sum(len(p[2]) for p in pieces)
    units, cols = blocks[0].shape[1:]

    def kernel(*refs):
        ins, out = refs[: len(blocks)], refs[len(blocks)]
        bufs, in_sems, out_sems = refs[len(blocks) + 1 :]
        copies, stores, places = [], [], []
        for ref, (_, crossed, keys) in zip(ins, pieces):
            core = 1 - this_core() if crossed else this_core()
            for k, key in enumerate(keys):
                i = len(copies)
                places.append(column_place(key[0], key[1], core))
                copies.append(pltpu.make_async_copy(ref.at[k], bufs.at[i], in_sems.at[i]))
                copies[-1].start()
        for i in range(count):
            copies[i].wait()
            stores.append(
                pltpu.make_async_copy(bufs.at[i], columns(out, places[i], cols), out_sems.at[i])
            )
            stores[-1].start()
        for c in stores:
            c.wait()

    return pl.pallas_call(
        kernel,
        in_specs=[ANY] * len(blocks),
        out_specs=HBM,
        out_shape=jax.ShapeDtypeStruct((units, width), BF16),
        scratch_shapes=[
            pltpu.VMEM((count, units, cols), BF16),
            pltpu.SemaphoreType.DMA((count,)),
            pltpu.SemaphoreType.DMA((count,)),
        ],
        compiler_params=SMALL,
        cost_estimate=cost(0, (*blocks, *blocks)),
    )(*blocks)


def per_device(grad_out, routes, combine, saved_hidden, down_weight):
    n_expert = lax.axis_size("expert")
    n_rep = lax.axis_size("dp")
    n_x = lax.axis_size("x")
    capacity = saved_hidden.shape[2]
    width = grad_out.shape[1]
    most = capacity // n_expert
    cols = width // (4 * n_x)
    weight, hidden = down_weight[0], saved_hidden[:, 0]

    def along_x(v, by):
        return lax.ppermute(v, "x", [(i, (i + by) % n_x) for i in range(n_x)])

    def along_y(v, by):
        return lax.ppermute(v, "dp", [(p, (p + by) % n_rep) for p in range(n_rep)])

    def to_core(v):
        return lax.ppermute(v, "core", [(0, 1), (1, 0)])

    sent, crossed = to_core(weight), to_core(hidden)
    rows, target = pick(routes.T, combine.T, grad_out, cols, capacity, most)
    got = lax.all_to_all(
        rows.reshape(n_expert, most, 2 * cols), "expert", split_axis=0, concat_axis=0, tiled=True
    ).reshape(capacity, 2 * cols)
    sent, crossed, token = settled(sent, crossed)
    got, _ = fence(got, token)

    a, b = got[:, :cols], got[:, cols:]
    al, ar = along_x(a, 1), along_x(a, -1)
    bd, bu = along_y(b, 1), along_y(b, -1)
    a_far, b_far = along_x(al, 1), along_y(bd, 1)
    a1, a1p, b1, b1p = stack(2, (a, al), (b, bd), after=(ar, bu))
    u1, r1 = along_y(a1, -1), along_x(b1, -1)
    b_far, a1p = fence(b_far, a1p)
    a_far, b1p = fence(a_far, b1p)
    d1, l1 = along_y(a1p, 1), along_x(b1p, 1)
    a2, a2p, a2m, b2, b2p, b2m = stack(3, (ar, a_far), (bu, b_far))
    turned = turn(hidden, crossed)
    g0, g0c = first_down((b1, b2), turned)
    r1, b2m = fence(r1, b2m)
    u1, a2m = fence(u1, a2m)
    l1, b2p = fence(l1, b2p)
    d1, a2p, g0, g0c = fence(d1, a2p, g0, g0c)
    d2, u2, l2, r2 = along_y(a2p, 1), along_y(a2m, -1), along_x(b2p, 1), along_x(b2m, -1)
    own, other = absorb(
        weight,
        sent,
        (),
        [
            (0, 0, 0, a1, True),
            (0, 0, 1, a2, True),
            (1, 0, 0, b1, True),
            (1, 0, 1, b2, True),
            (0, 1, 0, d1, True),
            (0, 2, 0, u1, True),
            (1, 1, 0, l1, True),
            (1, 2, 0, r1, True),
        ],
    )
    r1, r2, own = fence(r1, r2, own)
    u1, u2, own = fence(u1, u2, own)
    l1, l2, own = fence(l1, l2, own)
    d1, d2, own, other = fence(d1, d2, own, other)
    o1, o2, q1, q2 = along_y(d1, 1), along_y(u2, -1), along_x(l1, 1), along_x(r2, -1)
    own, other, g1, g1c = absorb(
        weight,
        sent,
        ((own,), (other,)),
        [
            (0, 1, 1, d2, True),
            (0, 2, 1, u2, True),
            (1, 1, 1, l2, True),
            (1, 2, 1, r2, True),
            (1, 1, 0, l1, False),
            (1, 2, 0, r1, False),
        ],
        turned=turned,
        downs=(1, 2),
        kinds=(F32, BF16),
    )
    sums = early_down([(a1, a2), (d1, d2), (u1, u2)], turned)
    other, o1, o2, q1, q2, sums = fence(other, o1, o2, q1, q2, sums)
    before = to_core(other)
    last = [(0, 3, 0, o1, True), (0, 3, 1, o2, True), (1, 3, 0, q1, True), (1, 3, 1, q2, True)]
    crossing = [(*part[:3], to_core(part[3]), True) for part in last]
    g2, g2c = last_down(sums, (o1, o2), (q1, q2), turned, before)
    (own,) = absorb(weight, sent, ((own, before),), last, sides=(0,))
    grad_hidden, partial = absorb(
        weight, sent, ((own,),), crossing, sides=(0,), crossed=True, hidden=hidden, after=g2
    )
    partial, g0c, g1c, g2c = fence(partial, g0c, g1c, g2c)
    spread = jnp.broadcast_to(
        partial.reshape(n_rep, n_expert, 1, most), (n_rep, n_expert, 2 * n_x, most)
    )
    returned = lax.all_to_all(
        spread.reshape(-1, 1, most),
        ("dp", "expert", "x", "core"),
        split_axis=0,
        concat_axis=0,
        tiled=True,
    )
    first, later, final = [(0, 1)], [(1, 1), (2, 1)], [(0, 0), (1, 0), (2, 0), (3, 0), (3, 1)]
    grad_down = gather_down(
        width,
        [
            (g0, False, first),
            (g1, False, later),
            (g2, False, final),
            (to_core(g0c), True, first),
            (to_core(g1c), True, later),
            (to_core(g2c), True, final),
        ],
    )
    returned, grad_down = fence(returned, grad_down)
    whole = jnp.sum(returned.reshape(n_rep, n_expert, 2 * n_x, most), axis=(0, 2)).reshape(-1)
    slot = jnp.arange(capacity, dtype=jnp.int32).astype(F32)
    chosen = target[:, None] == slot[None, :, None]
    grad_combine = jnp.sum(jnp.where(chosen, whole[None, :, None], 0.0), axis=1) / combine.T.astype(F32)
    return grad_hidden[:, None], grad_down[None], grad_combine.T


def solution(mesh):
    n_dp, n_expert, n_tensor = mesh.devices.shape
    split = Mesh(
        mesh.devices.reshape(n_dp, n_expert, n_tensor // 2, 2), ("dp", "expert", "x", "core")
    )
    return jax.shard_map(
        per_device,
        mesh=split,
        in_specs=(
            P(("dp", "expert"), None),
            P(("dp", "expert"), None),
            P(("dp", "expert"), None),
            P(None, "expert", None, ("dp", "x", "core")),
            P("expert", ("dp", "x", "core"), None),
        ),
        out_specs=(
            P(None, "expert", None, ("dp", "x", "core")),
            P("expert", ("dp", "x", "core"), None),
            P(("dp", "expert"), None),
        ),
        check_vma=False,
    )
```

```python
import jax
import jax.numpy as jnp
from jax import lax
from jax.experimental import pallas as pl
from jax.experimental.pallas import tpu as pltpu
from jax.sharding import Mesh
from jax.sharding import PartitionSpec as P

F32, BF16 = jnp.float32, jnp.bfloat16
LIMIT = pltpu.CompilerParams(vmem_limit_bytes=28 * 1024 * 1024)
SMALL = pltpu.CompilerParams(vmem_limit_bytes=12 * 1024 * 1024)
LARGE = pltpu.CompilerParams(vmem_limit_bytes=60 * 1024 * 1024)
ANY = pl.BlockSpec(memory_space=pl.ANY)
VMEM = pl.BlockSpec(memory_space=pltpu.VMEM)
HBM = pl.BlockSpec(memory_space=pltpu.HBM)
NT = (((1,), (1,)), ((), ()))
OFFSETS = (0, -1, 1, 2)


def like(*arrays):
    return [jax.ShapeDtypeStruct(a.shape, a.dtype) for a in arrays]


def cost(flops, arrays):
    return pl.CostEstimate(
        flops=flops,
        bytes_accessed=sum(a.size * a.dtype.itemsize for a in arrays),
        transcendentals=0,
    )


def ring_place(axis, by):
    return lax.rem(lax.axis_index(axis) + (OFFSETS[by] + 4), 4)


def column_place(k, kind, core):
    return 4 * ring_place("x", k) + 2 * kind + core


def this_core():
    return lax.axis_index("core")


def columns(ref, place, cols):
    return ref.at[:, pl.ds(pl.multiple_of(place * cols, 128), cols)]


def pick(routes, combine, grad_out, cols, slots, most):
    tokens = grad_out.shape[0]

    def kernel(routes, combine, grad, out, target, rows, sems):
        copies = [
            pltpu.make_async_copy(
                columns(grad, column_place(0, kind, this_core()), cols), rows.at[kind], sems.at[kind]
            )
            for kind in range(2)
        ]
        for c in copies:
            c.start()
        expert = lax.broadcasted_iota(jnp.int32, (8, tokens), 0)
        named = [routes[k : k + 1, :] for k in range(2)]
        hits = [(n == expert).astype(F32) for n in named]
        earlier = lax.broadcasted_iota(jnp.int32, (tokens, tokens), 0)
        later = lax.broadcasted_iota(jnp.int32, (tokens, tokens), 1)
        before = jnp.dot(
            (hits[0] + hits[1]).astype(BF16),
            (earlier < later).astype(F32).astype(BF16),
            preferred_element_type=F32,
        )
        slot = lax.broadcasted_iota(jnp.int32, (slots, tokens), 0).astype(F32)
        picker = None
        for k in range(2):
            rank = jnp.sum(hits[k] * before, axis=0, keepdims=True)
            where = named[k].astype(F32) * float(most) + rank
            target[k : k + 1, :] = where
            term = jnp.where(where == slot, combine[k : k + 1, :].astype(F32), 0.0)
            picker = term if picker is None else picker + term
        picker = picker.astype(BF16)
        for kind in range(2):
            copies[kind].wait()
            found = jnp.dot(picker, rows[kind], preferred_element_type=F32)
            out[:, kind * cols : (kind + 1) * cols] = found.astype(BF16)

    return pl.pallas_call(
        kernel,
        in_specs=[VMEM, VMEM, HBM],
        out_specs=[VMEM, VMEM],
        out_shape=[
            jax.ShapeDtypeStruct((slots, 2 * cols), BF16),
            jax.ShapeDtypeStruct((2, tokens), F32),
        ],
        scratch_shapes=[pltpu.VMEM((2, tokens, cols), BF16), pltpu.SemaphoreType.DMA((2,))],
        compiler_params=LARGE,
        cost_estimate=pl.CostEstimate(
            flops=4 * tokens * slots * cols, bytes_accessed=8 * slots * cols, transcendentals=0
        ),
    )(routes, combine, grad_out)


def turn(hidden, crossed):
    n_rep, slots, units = hidden.shape

    def kernel(hidden, crossed, turned, held, sems):
        copies = []
        for j in range(4):
            for i, ref in enumerate((hidden, crossed)):
                copies.append(
                    pltpu.make_async_copy(
                        ref.at[ring_place("dp", j)], held.at[j, i], sems.at[2 * j + i]
                    )
                )
                copies[-1].start()
        for j in range(4):
            for i in range(2):
                copies[2 * j + i].wait()
                turned[j, i * units : (i + 1) * units] = held[j, i].astype(F32).T.astype(BF16)

    return pl.pallas_call(
        kernel,
        in_specs=[HBM, HBM],
        out_specs=VMEM,
        out_shape=jax.ShapeDtypeStruct((4, 2 * units, slots), BF16),
        scratch_shapes=[pltpu.VMEM((4, 2, slots, units), BF16), pltpu.SemaphoreType.DMA((8,))],
        compiler_params=SMALL,
        cost_estimate=cost(0, (hidden, hidden, hidden, hidden)),
    )(hidden, crossed)


LAST_KEYS = ((0, 0), (1, 0), (2, 0), (3, 0), (3, 1))


def fetch(weight, sent, hidden, cols):
    units = weight.shape[0]

    def kernel(weight, sent, hidden, own, crossed, held, sems):
        copies = []

        def start(src, dst):
            copies.append(pltpu.make_async_copy(src, dst, sems.at[len(copies)]))
            copies[-1].start()

        for k in range(4):
            for kind in range(2):
                place = column_place(k, kind, this_core())
                for side, ref in enumerate((weight, sent)):
                    to = own.at[2 * k + kind, pl.ds(side * units, units)]
                    start(columns(ref, place, cols), to)
        for i, (k, kind) in enumerate(LAST_KEYS):
            start(columns(weight, column_place(k, kind, 1 - this_core()), cols), crossed.at[i])
        for j in range(4):
            start(hidden.at[ring_place("dp", j)], held.at[j])
        for c in copies:
            c.wait()

    return pl.pallas_call(
        kernel,
        in_specs=[HBM] * 3,
        out_specs=[VMEM] * 3,
        out_shape=[
            jax.ShapeDtypeStruct((8, 2 * units, cols), BF16),
            jax.ShapeDtypeStruct((5, units, cols), BF16),
            jax.ShapeDtypeStruct(hidden.shape, BF16),
        ],
        scratch_shapes=[pltpu.SemaphoreType.DMA((25,))],
        compiler_params=SMALL,
        cost_estimate=cost(0, (weight, weight, hidden)),
    )(weight, sent, hidden)


def fence(*arrays):
    return pl.pallas_call(
        lambda *refs: None,
        out_shape=like(*arrays),
        in_specs=[ANY] * len(arrays),
        out_specs=[ANY] * len(arrays),
        input_output_aliases={i: i for i in range(len(arrays))},
        compiler_params=pltpu.CompilerParams(
            has_side_effects=True, vmem_limit_bytes=1024 * 1024
        ),
    )(*arrays)


def settled(*arrays, place=ANY):
    def kernel(*refs):
        refs[-1][...] = jnp.zeros_like(refs[-1])

    n = len(arrays)
    return pl.pallas_call(
        kernel,
        out_shape=like(*arrays) + [jax.ShapeDtypeStruct((8, 128), F32)],
        in_specs=[place] * n,
        out_specs=[place] * n + [VMEM],
        input_output_aliases={i: i for i in range(n)},
        compiler_params=pltpu.CompilerParams(vmem_limit_bytes=1024 * 1024),
    )(*arrays)


def stack(copies, *pairs, after=()):
    rows, cols = pairs[0][0].shape
    ins = [a for pair in pairs for a in pair]
    n = len(pairs)

    def kernel(*refs):
        outs, sems = refs[2 * n + len(after) : -1], refs[-1]
        started = []
        for i in range(n):
            for out in outs[i * copies : (i + 1) * copies]:
                for k in range(2):
                    started.append(
                        pltpu.make_async_copy(refs[2 * i + k], out.at[k], sems.at[len(started)])
                    )
                    started[-1].start()
        for c in started:
            c.wait()

    return pl.pallas_call(
        kernel,
        in_specs=[ANY] * (2 * n + len(after)),
        out_specs=[VMEM] * (n * copies),
        out_shape=[jax.ShapeDtypeStruct((2, rows, cols), BF16)] * (n * copies),
        scratch_shapes=[pltpu.SemaphoreType.DMA((2 * n * copies,))],
        compiler_params=SMALL,
    )(*ins, *after)


def absorb(weight, before, parts, sides=(0, 1), crossed=False, turned=None, downs=(), kinds=(F32, F32), hidden=None, after=None):
    arrays = [p[3] for p in parts]
    used = [i for i, p in enumerate(parts) if p[4]]

    def keys_of(i):
        what, off, pair = parts[i][:3]
        return [(2 * pair, 0), (2 * pair + 1, 0)] if what == 0 else [(off, 1)] * 2

    def block(ref, key):
        if crossed:
            return ref[LAST_KEYS.index(key)]
        return ref[2 * key[0] + key[1], sides[0] * units : (sides[-1] + 1) * units]

    n, s = len(arrays), len(sides)
    rows, cols = arrays[0].shape[1:]
    units = rows
    olds = [a for side in before for a in side]
    n_old = [len(side) for side in before]
    turned = [] if turned is None else [turned]
    last = [] if hidden is None else [hidden]
    extra = [] if after is None else [after]
    operands = arrays + [weight] + turned + olds + last + extra
    n_sum = 2 if last else s
    n_out = n_sum + (2 if downs else 0)

    def kernel(*refs):
        refs = list(refs)

        def take(count):
            taken = refs[:count]
            del refs[:count]
            return taken

        bufs, (w_ref,) = take(n), take(1)
        t, held, hid_ref = take(len(turned)), take(len(olds)), take(len(last))
        take(len(extra))
        outs = take(n_out)
        rounded, sems = take(2) if last else (None, None)
        started = []

        def start(src, dst):
            copy = pltpu.make_async_copy(src, dst, sems.at[len(started)])
            copy.start()
            started.append(copy)
            return copy

        def of(j):
            return [
                (i, k, key)
                for i in used
                for k, key in enumerate(keys_of(i))
                if (parts[i][1] if parts[i][0] == 0 else 2 * parts[i][2] + k) == j
            ]

        stores = []
        for g, off in enumerate(downs):
            down = None
            for i, part in enumerate(parts):
                if part[0] == 1 and part[1] == off:
                    for k in range(2):
                        term = jnp.dot(
                            t[0][2 * part[2] + k], bufs[i][k], preferred_element_type=F32
                        )
                        down = term if down is None else down + term
            for side in range(2):
                outs[n_sum + side][g] = down[side * units : (side + 1) * units].astype(BF16)
        for j in range(4):
            total = None
            for i, k, key in of(j):
                term = lax.dot_general(
                    bufs[i][k], block(w_ref, key), NT, preferred_element_type=F32
                )
                total = term if total is None else total + term
            at = 0
            for where in range(s):
                mine = None if total is None else total[:, where * units : (where + 1) * units]
                for h in held[at : at + (n_old[where] if n_old else 0)]:
                    old = h[j].astype(F32)
                    mine = old if mine is None else mine + old
                at += n_old[where] if n_old else 0
                if last:
                    place = ring_place("dp", j)
                    rounded[j] = mine.astype(BF16)
                    stores.append(start(rounded.at[j], outs[0].at[place]))
                    prod = mine * hid_ref[0][j].astype(F32)
                    folded = sum(prod[:, c : c + 128] for c in range(0, units, 128))
                    row = jnp.sum(folded.T, axis=0, keepdims=True)
                    for q in range(8):
                        piece = row[:, q * (rows // 8) : (q + 1) * (rows // 8)]
                        outs[1][place, q] = jnp.broadcast_to(piece, (8, rows // 8))
                else:
                    outs[where][j] = mine.astype(kinds[where])
        for c in stores:
            c.wait()

    if last:
        out_shape = [
            jax.ShapeDtypeStruct((4, rows, units), BF16),
            jax.ShapeDtypeStruct((4, 8, 8, rows // 8), F32),
        ]
        out_specs = [HBM, VMEM]
    else:
        out_shape = [jax.ShapeDtypeStruct((4, rows, units), kinds[i]) for i in range(s)]
        out_specs = [VMEM] * s
    if downs:
        out_shape += [jax.ShapeDtypeStruct((len(downs), units, cols), BF16)] * 2
        out_specs = out_specs + [VMEM] * 2
    scratch = [pltpu.VMEM((4, rows, units), BF16), pltpu.SemaphoreType.DMA((4,))] if last else []
    flops = 4 * rows * cols * units * (s * len(used) + 2 * 2 * len(downs))
    return pl.pallas_call(
        kernel,
        in_specs=[VMEM] * (len(operands) - len(extra)) + [ANY] * len(extra),
        out_specs=out_specs,
        out_shape=out_shape,
        scratch_shapes=scratch,
        compiler_params=LIMIT,
        cost_estimate=cost(flops, operands),
    )(*operands)


def first_down(pair, turned):
    both, rows = turned.shape[1:]
    units, cols = both // 2, pair[0].shape[2]

    def kernel(first, second, t, own, other):
        total = None
        for j in range(4):
            part = jnp.dot(t[j], (first, second)[j // 2][j % 2], preferred_element_type=F32)
            total = part if total is None else total + part
        own[0] = total[:units].astype(BF16)
        other[0] = total[units:].astype(BF16)

    return pl.pallas_call(
        kernel,
        in_specs=[VMEM] * 3,
        out_specs=[VMEM] * 2,
        out_shape=[jax.ShapeDtypeStruct((1, units, cols), BF16)] * 2,
        compiler_params=SMALL,
        cost_estimate=cost(8 * rows * both * cols, (*pair, turned)),
    )(*pair, turned)


def early_down(groups, turned):
    both, rows = turned.shape[1:]
    cols = groups[0][0].shape[2]
    arrays = [r for g in groups for r in g]

    def kernel(*refs):
        ins, t, sums = refs[:-2], refs[-2], refs[-1]
        for k in range(4):
            total = None
            for j in range(len(groups)):
                part = jnp.dot(t[j], ins[2 * j + k // 2][k % 2], preferred_element_type=F32)
                total = part if total is None else total + part
            sums[k] = total

    return pl.pallas_call(
        kernel,
        in_specs=[VMEM] * (len(arrays) + 1),
        out_specs=VMEM,
        out_shape=jax.ShapeDtypeStruct((4, both, cols), F32),
        compiler_params=LIMIT,
        cost_estimate=cost(8 * len(groups) * rows * both * cols, (*arrays, turned)),
    )(*arrays, turned)


def last_down(sums, a_pair, b_pair, turned, after):
    both, rows = turned.shape[1:]
    units = both // 2
    cols = a_pair[0].shape[2]

    def kernel(sums, a1, a2, b1, b2, t, _, own, other):
        for k in range(5):
            if k < 4:
                total = sums[k] + jnp.dot(
                    t[3], (a1, a2)[k // 2][k % 2], preferred_element_type=F32
                )
            else:
                total = None
                for j in range(4):
                    part = jnp.dot(t[j], (b1, b2)[j // 2][j % 2], preferred_element_type=F32)
                    total = part if total is None else total + part
            other[k] = total[units:].astype(BF16)
            own[k] = total[:units].astype(BF16)

    operands = [sums, *a_pair, *b_pair, turned, after]
    return pl.pallas_call(
        kernel,
        in_specs=[VMEM] * 6 + [ANY],
        out_specs=[VMEM] * 2,
        out_shape=[jax.ShapeDtypeStruct((5, units, cols), BF16)] * 2,
        compiler_params=LIMIT,
        cost_estimate=cost(16 * rows * both * cols, operands),
    )(*operands)


def gather_down(width, pieces):
    blocks = [p[0] for p in pieces]
    count = sum(len(p[2]) for p in pieces)
    units, cols = blocks[0].shape[1:]

    def kernel(*refs):
        ins, out = refs[: len(blocks)], refs[len(blocks)]
        bufs, in_sems, out_sems = refs[len(blocks) + 1 :]
        copies, stores, places = [], [], []
        for ref, (_, crossed, keys) in zip(ins, pieces):
            core = 1 - this_core() if crossed else this_core()
            for k, key in enumerate(keys):
                i = len(copies)
                places.append(column_place(key[0], key[1], core))
                copies.append(pltpu.make_async_copy(ref.at[k], bufs.at[i], in_sems.at[i]))
                copies[-1].start()
        for i in range(count):
            copies[i].wait()
            stores.append(
                pltpu.make_async_copy(bufs.at[i], columns(out, places[i], cols), out_sems.at[i])
            )
            stores[-1].start()
        for c in stores:
            c.wait()

    return pl.pallas_call(
        kernel,
        in_specs=[ANY] * len(blocks),
        out_specs=HBM,
        out_shape=jax.ShapeDtypeStruct((units, width), BF16),
        scratch_shapes=[
            pltpu.VMEM((count, units, cols), BF16),
            pltpu.SemaphoreType.DMA((count,)),
            pltpu.SemaphoreType.DMA((count,)),
        ],
        compiler_params=SMALL,
        cost_estimate=cost(0, (*blocks, *blocks)),
    )(*blocks)


def per_device(grad_out, routes, combine, saved_hidden, down_weight):
    n_expert = lax.axis_size("expert")
    n_rep = lax.axis_size("dp")
    n_x = lax.axis_size("x")
    capacity = saved_hidden.shape[2]
    width = grad_out.shape[1]
    most = capacity // n_expert
    cols = width // (4 * n_x)
    weight, hidden = down_weight[0], saved_hidden[:, 0]

    def along_x(v, by):
        return lax.ppermute(v, "x", [(i, (i + by) % n_x) for i in range(n_x)])

    def along_y(v, by):
        return lax.ppermute(v, "dp", [(p, (p + by) % n_rep) for p in range(n_rep)])

    def to_core(v):
        return lax.ppermute(v, "core", [(0, 1), (1, 0)])

    sent, crossed = to_core(weight), to_core(hidden)
    rows, target = pick(routes.T, combine.T, grad_out, cols, capacity, most)
    got = lax.all_to_all(
        rows.reshape(n_expert, most, 2 * cols), "expert", split_axis=0, concat_axis=0, tiled=True
    ).reshape(capacity, 2 * cols)
    sent, crossed, token = settled(sent, crossed, place=HBM)
    got, _ = fence(got, token)

    a, b = got[:, :cols], got[:, cols:]
    al, ar = along_x(a, 1), along_x(a, -1)
    bd, bu = along_y(b, 1), along_y(b, -1)
    a_far, b_far = along_x(al, 1), along_y(bd, 1)
    a1, a1p, b1, b1p = stack(2, (a, al), (b, bd), after=(ar, bu))
    a1, b1, token = settled(a1, b1)
    a1, b1, _ = fence(a1, b1, to_core(token))
    u1, r1 = along_y(a1, -1), along_x(b1, -1)
    b_far, a1p = fence(b_far, a1p)
    a_far, b1p = fence(a_far, b1p)
    d1, l1 = along_y(a1p, 1), along_x(b1p, 1)
    a2, a2p, a2m, b2, b2p, b2m = stack(3, (ar, a_far), (bu, b_far))
    turned = turn(hidden, crossed)
    blocks, crossed_blocks, held = fetch(weight, sent, hidden, cols)
    g0, g0c = first_down((b1, b2), turned)
    r1, b2m = fence(r1, b2m)
    u1, a2m = fence(u1, a2m)
    l1, b2p = fence(l1, b2p)
    d1, a2p, g0, g0c, blocks = fence(d1, a2p, g0, g0c, blocks)
    d2, u2, l2, r2 = along_y(a2p, 1), along_y(a2m, -1), along_x(b2p, 1), along_x(b2m, -1)
    own, other = absorb(
        blocks,
        (),
        [
            (0, 0, 0, a1, True),
            (0, 0, 1, a2, True),
            (1, 0, 0, b1, True),
            (1, 0, 1, b2, True),
            (0, 1, 0, d1, True),
            (0, 2, 0, u1, True),
            (1, 1, 0, l1, True),
            (1, 2, 0, r1, True),
        ],
    )
    r1, r2, own = fence(r1, r2, own)
    u1, u2, own = fence(u1, u2, own)
    l1, l2, own = fence(l1, l2, own)
    d1, d2, own, other = fence(d1, d2, own, other)
    o1, o2, q1, q2 = along_y(d1, 1), along_y(u2, -1), along_x(l1, 1), along_x(r2, -1)
    own, other, g1, g1c = absorb(
        blocks,
        ((own,), (other,)),
        [
            (0, 1, 1, d2, True),
            (0, 2, 1, u2, True),
            (1, 1, 1, l2, True),
            (1, 2, 1, r2, True),
            (1, 1, 0, l1, False),
            (1, 2, 0, r1, False),
        ],
        turned=turned,
        downs=(1, 2),
        kinds=(F32, BF16),
    )
    sums = early_down([(a1, a2), (d1, d2), (u1, u2)], turned)
    other, o1, o2, q1, q2, sums, token = settled(other, o1, o2, q1, q2, sums)
    before = to_core(other)
    last = [(0, 3, 0, o1, True), (0, 3, 1, o2, True), (1, 3, 0, q1, True), (1, 3, 1, q2, True)]
    crossing = [(*part[:3], to_core(part[3]), True) for part in last]
    g2, g2c = last_down(sums, (o1, o2), (q1, q2), turned, to_core(token))
    (own,) = absorb(blocks, ((own, before),), last, sides=(0,))
    grad_hidden, partial = absorb(
        crossed_blocks, ((own,),), crossing, sides=(0,), crossed=True, hidden=held, after=g2
    )
    partial, g0c, g1c, g2c = fence(partial, g0c, g1c, g2c)
    returned = lax.all_to_all(
        partial.reshape(-1, 1, most),
        ("dp", "expert", "x", "core"),
        split_axis=0,
        concat_axis=0,
        tiled=True,
    )
    first, later, final = [(0, 1)], [(1, 1), (2, 1)], [(0, 0), (1, 0), (2, 0), (3, 0), (3, 1)]
    grad_down = gather_down(
        width,
        [
            (g0, False, first),
            (g1, False, later),
            (g2, False, final),
            (to_core(g0c), True, first),
            (to_core(g1c), True, later),
            (to_core(g2c), True, final),
        ],
    )
    returned, grad_down = fence(returned, grad_down)
    whole = jnp.sum(returned.reshape(n_rep, n_expert, 2 * n_x, most), axis=(0, 2)).reshape(-1)
    slot = jnp.arange(capacity, dtype=jnp.int32).astype(F32)
    chosen = target[:, None] == slot[None, :, None]
    grad_combine = jnp.sum(jnp.where(chosen, whole[None, :, None], 0.0), axis=1) / combine.T.astype(F32)
    return grad_hidden[:, None], grad_down[None], grad_combine.T


def solution(mesh):
    n_dp, n_expert, n_tensor = mesh.devices.shape
    split = Mesh(
        mesh.devices.reshape(n_dp, n_expert, n_tensor // 2, 2), ("dp", "expert", "x", "core")
    )
    return jax.shard_map(
        per_device,
        mesh=split,
        in_specs=(
            P(("dp", "expert"), None),
            P(("dp", "expert"), None),
            P(("dp", "expert"), None),
            P(None, "expert", None, ("dp", "x", "core")),
            P("expert", ("dp", "x", "core"), None),
        ),
        out_specs=(
            P(None, "expert", None, ("dp", "x", "core")),
            P("expert", ("dp", "x", "core"), None),
            P(("dp", "expert"), None),
        ),
        check_vma=False,
    )
```

```python
import jax
import jax.numpy as jnp
from jax import lax
from jax.experimental import pallas as pl
from jax.experimental.pallas import tpu as pltpu
from jax.sharding import Mesh
from jax.sharding import PartitionSpec as P

F32, BF16 = jnp.float32, jnp.bfloat16
LIMIT = pltpu.CompilerParams(vmem_limit_bytes=28 * 1024 * 1024)
SMALL = pltpu.CompilerParams(vmem_limit_bytes=12 * 1024 * 1024)
LARGE = pltpu.CompilerParams(vmem_limit_bytes=60 * 1024 * 1024)
ANY = pl.BlockSpec(memory_space=pl.ANY)
VMEM = pl.BlockSpec(memory_space=pltpu.VMEM)
HBM = pl.BlockSpec(memory_space=pltpu.HBM)
NT = (((1,), (1,)), ((), ()))
OFFSETS = (0, -1, 1, 2)


def like(*arrays):
    return [jax.ShapeDtypeStruct(a.shape, a.dtype) for a in arrays]


def cost(flops, arrays):
    return pl.CostEstimate(
        flops=flops,
        bytes_accessed=sum(a.size * a.dtype.itemsize for a in arrays),
        transcendentals=0,
    )


def ring_place(axis, by):
    return lax.rem(lax.axis_index(axis) + (OFFSETS[by] + 4), 4)


def column_place(k, kind, core):
    return 4 * ring_place("x", k) + 2 * kind + core


def this_core():
    return lax.axis_index("core")


def columns(ref, place, cols):
    return ref.at[:, pl.ds(pl.multiple_of(place * cols, 128), cols)]


def pick(routes, combine, grad_out, cols, slots, most):
    tokens = grad_out.shape[0]

    def kernel(routes_ref, combine_ref, grad, out_ref, target, rows, routes, combine, out, sems):
        small = [
            pltpu.make_async_copy(routes_ref, routes, sems.at[2]),
            pltpu.make_async_copy(combine_ref, combine, sems.at[3]),
        ]
        for c in small:
            c.start()
        copies = [
            pltpu.make_async_copy(
                columns(grad, column_place(0, kind, this_core()), cols), rows.at[kind], sems.at[kind]
            )
            for kind in range(2)
        ]
        for c in copies:
            c.start()
        for c in small:
            c.wait()
        expert = lax.broadcasted_iota(jnp.int32, (8, tokens), 0)
        named = [routes[k : k + 1, :] for k in range(2)]
        hits = [(n == expert).astype(F32) for n in named]
        earlier = lax.broadcasted_iota(jnp.int32, (tokens, tokens), 0)
        later = lax.broadcasted_iota(jnp.int32, (tokens, tokens), 1)
        before = jnp.dot(
            (hits[0] + hits[1]).astype(BF16),
            (earlier < later).astype(F32).astype(BF16),
            preferred_element_type=F32,
        )
        slot = lax.broadcasted_iota(jnp.int32, (slots, tokens), 0).astype(F32)
        picker = None
        for k in range(2):
            rank = jnp.sum(hits[k] * before, axis=0, keepdims=True)
            where = named[k].astype(F32) * float(most) + rank
            target[k : k + 1, :] = where
            term = jnp.where(where == slot, combine[k : k + 1, :].astype(F32), 0.0)
            picker = term if picker is None else picker + term
        picker = picker.astype(BF16)
        stores = []
        for kind in range(2):
            copies[kind].wait()
            found = jnp.dot(picker, rows[kind], preferred_element_type=F32)
            out[kind] = found.astype(BF16)
            to = out_ref.at[:, pl.ds(kind * cols, cols)]
            stores.append(pltpu.make_async_copy(out.at[kind], to, sems.at[4 + kind]))
            stores[-1].start()
        for c in stores:
            c.wait()

    return pl.pallas_call(
        kernel,
        in_specs=[HBM, HBM, HBM],
        out_specs=[HBM, VMEM],
        out_shape=[
            jax.ShapeDtypeStruct((slots, 2 * cols), BF16),
            jax.ShapeDtypeStruct((2, tokens), F32),
        ],
        scratch_shapes=[
            pltpu.VMEM((2, tokens, cols), BF16),
            pltpu.VMEM(routes.shape, routes.dtype),
            pltpu.VMEM(combine.shape, combine.dtype),
            pltpu.VMEM((2, slots, cols), BF16),
            pltpu.SemaphoreType.DMA((6,)),
        ],
        compiler_params=LARGE,
        cost_estimate=pl.CostEstimate(
            flops=4 * tokens * slots * cols, bytes_accessed=8 * slots * cols, transcendentals=0
        ),
    )(routes, combine, grad_out)


def turn(hidden, crossed):
    n_rep, slots, units = hidden.shape

    def kernel(hidden, crossed, turned, held, sems):
        copies = []
        for j in range(4):
            for i, ref in enumerate((hidden, crossed)):
                copies.append(
                    pltpu.make_async_copy(
                        ref.at[ring_place("dp", j)], held.at[j, i], sems.at[2 * j + i]
                    )
                )
                copies[-1].start()
        for j in range(4):
            for i in range(2):
                copies[2 * j + i].wait()
                turned[j, i * units : (i + 1) * units] = held[j, i].astype(F32).T.astype(BF16)

    return pl.pallas_call(
        kernel,
        in_specs=[HBM, HBM],
        out_specs=VMEM,
        out_shape=jax.ShapeDtypeStruct((4, 2 * units, slots), BF16),
        scratch_shapes=[pltpu.VMEM((4, 2, slots, units), BF16), pltpu.SemaphoreType.DMA((8,))],
        compiler_params=SMALL,
        cost_estimate=cost(0, (hidden, hidden, hidden, hidden)),
    )(hidden, crossed)


LAST_KEYS = ((0, 0), (1, 0), (2, 0), (3, 0), (3, 1))


def fetch(weight, sent, hidden, cols):
    units = weight.shape[0]

    def kernel(weight, sent, hidden, own, crossed, held, sems):
        copies = []

        def start(src, dst):
            copies.append(pltpu.make_async_copy(src, dst, sems.at[len(copies)]))
            copies[-1].start()

        for k in range(4):
            for kind in range(2):
                place = column_place(k, kind, this_core())
                for side, ref in enumerate((weight, sent)):
                    to = own.at[2 * k + kind, pl.ds(side * units, units)]
                    start(columns(ref, place, cols), to)
        for i, (k, kind) in enumerate(LAST_KEYS):
            start(columns(weight, column_place(k, kind, 1 - this_core()), cols), crossed.at[i])
        for j in range(4):
            start(hidden.at[ring_place("dp", j)], held.at[j])
        for c in copies:
            c.wait()

    return pl.pallas_call(
        kernel,
        in_specs=[HBM] * 3,
        out_specs=[VMEM] * 3,
        out_shape=[
            jax.ShapeDtypeStruct((8, 2 * units, cols), BF16),
            jax.ShapeDtypeStruct((5, units, cols), BF16),
            jax.ShapeDtypeStruct(hidden.shape, BF16),
        ],
        scratch_shapes=[pltpu.SemaphoreType.DMA((25,))],
        compiler_params=SMALL,
        cost_estimate=cost(0, (weight, weight, hidden)),
    )(weight, sent, hidden)


def fence(*arrays):
    return pl.pallas_call(
        lambda *refs: None,
        out_shape=like(*arrays),
        in_specs=[ANY] * len(arrays),
        out_specs=[ANY] * len(arrays),
        input_output_aliases={i: i for i in range(len(arrays))},
        compiler_params=pltpu.CompilerParams(
            has_side_effects=True, vmem_limit_bytes=1024 * 1024
        ),
    )(*arrays)


def settled(*arrays, place=ANY):
    def kernel(*refs):
        refs[-1][...] = jnp.zeros_like(refs[-1])

    n = len(arrays)
    return pl.pallas_call(
        kernel,
        out_shape=like(*arrays) + [jax.ShapeDtypeStruct((8, 128), F32)],
        in_specs=[place] * n,
        out_specs=[place] * n + [VMEM],
        input_output_aliases={i: i for i in range(n)},
        compiler_params=pltpu.CompilerParams(vmem_limit_bytes=1024 * 1024),
    )(*arrays)


def arrived(*arrays):
    def kernel(*refs):
        refs[-1][...] = jnp.zeros_like(refs[-1])

    return pl.pallas_call(
        kernel,
        out_shape=jax.ShapeDtypeStruct((8, 128), F32),
        in_specs=[ANY] * len(arrays),
        out_specs=VMEM,
        compiler_params=pltpu.CompilerParams(vmem_limit_bytes=1024 * 1024),
    )(*arrays)


def stack(copies, *pairs, after=()):
    rows, cols = pairs[0][0].shape
    ins = [a for pair in pairs for a in pair]
    n = len(pairs)

    def kernel(*refs):
        outs, sems = refs[2 * n + len(after) : -1], refs[-1]
        started = []
        for i in range(n):
            for out in outs[i * copies : (i + 1) * copies]:
                for k in range(2):
                    started.append(
                        pltpu.make_async_copy(refs[2 * i + k], out.at[k], sems.at[len(started)])
                    )
                    started[-1].start()
        for c in started:
            c.wait()

    return pl.pallas_call(
        kernel,
        in_specs=[ANY] * (2 * n + len(after)),
        out_specs=[VMEM] * (n * copies),
        out_shape=[jax.ShapeDtypeStruct((2, rows, cols), BF16)] * (n * copies),
        scratch_shapes=[pltpu.SemaphoreType.DMA((2 * n * copies,))],
        compiler_params=SMALL,
    )(*ins, *after)


def absorb(weight, before, parts, sides=(0, 1), crossed=False, turned=None, downs=(), kinds=(F32, F32), hidden=None, after=None):
    arrays = [p[3] for p in parts]
    used = [i for i, p in enumerate(parts) if p[4]]

    def keys_of(i):
        what, off, pair = parts[i][:3]
        return [(2 * pair, 0), (2 * pair + 1, 0)] if what == 0 else [(off, 1)] * 2

    def block(ref, key):
        if crossed:
            return ref[LAST_KEYS.index(key)]
        return ref[2 * key[0] + key[1], sides[0] * units : (sides[-1] + 1) * units]

    n, s = len(arrays), len(sides)
    rows, cols = arrays[0].shape[1:]
    units = rows
    olds = [a for side in before for a in side]
    n_old = [len(side) for side in before]
    turned = [] if turned is None else [turned]
    last = [] if hidden is None else [hidden]
    extra = [] if after is None else [after]
    operands = arrays + [weight] + turned + olds + last + extra
    n_sum = 2 if last else s
    n_out = n_sum + (2 if downs else 0)

    def kernel(*refs):
        refs = list(refs)

        def take(count):
            taken = refs[:count]
            del refs[:count]
            return taken

        bufs, (w_ref,) = take(n), take(1)
        t, held, hid_ref = take(len(turned)), take(len(olds)), take(len(last))
        take(len(extra))
        outs = take(n_out)
        rounded, sems = take(2) if last else (None, None)
        started = []

        def start(src, dst):
            copy = pltpu.make_async_copy(src, dst, sems.at[len(started)])
            copy.start()
            started.append(copy)
            return copy

        def of(j):
            return [
                (i, k, key)
                for i in used
                for k, key in enumerate(keys_of(i))
                if (parts[i][1] if parts[i][0] == 0 else 2 * parts[i][2] + k) == j
            ]

        stores = []
        for g, off in enumerate(downs):
            down = None
            for i, part in enumerate(parts):
                if part[0] == 1 and part[1] == off:
                    for k in range(2):
                        term = jnp.dot(
                            t[0][2 * part[2] + k], bufs[i][k], preferred_element_type=F32
                        )
                        down = term if down is None else down + term
            for side in range(2):
                outs[n_sum + side][g] = down[side * units : (side + 1) * units].astype(BF16)
        for j in range(4):
            total = None
            for i, k, key in of(j):
                term = lax.dot_general(
                    bufs[i][k], block(w_ref, key), NT, preferred_element_type=F32
                )
                total = term if total is None else total + term
            at = 0
            for where in range(s):
                mine = None if total is None else total[:, where * units : (where + 1) * units]
                for h in held[at : at + (n_old[where] if n_old else 0)]:
                    old = h[j].astype(F32)
                    mine = old if mine is None else mine + old
                at += n_old[where] if n_old else 0
                if last:
                    place = ring_place("dp", j)
                    rounded[j] = mine.astype(BF16)
                    stores.append(start(rounded.at[j], outs[0].at[place]))
                    prod = mine * hid_ref[0][j].astype(F32)
                    folded = sum(prod[:, c : c + 128] for c in range(0, units, 128))
                    row = jnp.sum(folded.T, axis=0, keepdims=True)
                    for q in range(8):
                        piece = row[:, q * (rows // 8) : (q + 1) * (rows // 8)]
                        outs[1][place, q] = jnp.broadcast_to(piece, (8, rows // 8))
                else:
                    outs[where][j] = mine.astype(kinds[where])
        for c in stores:
            c.wait()

    if last:
        out_shape = [
            jax.ShapeDtypeStruct((4, rows, units), BF16),
            jax.ShapeDtypeStruct((4, 8, 8, rows // 8), F32),
        ]
        out_specs = [HBM, VMEM]
    else:
        out_shape = [jax.ShapeDtypeStruct((4, rows, units), kinds[i]) for i in range(s)]
        out_specs = [VMEM] * s
    if downs:
        out_shape += [jax.ShapeDtypeStruct((len(downs), units, cols), BF16)] * 2
        out_specs = out_specs + [VMEM] * 2
    scratch = [pltpu.VMEM((4, rows, units), BF16), pltpu.SemaphoreType.DMA((4,))] if last else []
    flops = 4 * rows * cols * units * (s * len(used) + 2 * 2 * len(downs))
    return pl.pallas_call(
        kernel,
        in_specs=[VMEM] * (len(operands) - len(extra)) + [ANY] * len(extra),
        out_specs=out_specs,
        out_shape=out_shape,
        scratch_shapes=scratch,
        compiler_params=LIMIT,
        cost_estimate=cost(flops, operands),
    )(*operands)


def first_down(pair, turned):
    both, rows = turned.shape[1:]
    units, cols = both // 2, pair[0].shape[2]

    def kernel(first, second, t, own, other):
        total = None
        for j in range(4):
            part = jnp.dot(t[j], (first, second)[j // 2][j % 2], preferred_element_type=F32)
            total = part if total is None else total + part
        own[0] = total[:units].astype(BF16)
        other[0] = total[units:].astype(BF16)

    return pl.pallas_call(
        kernel,
        in_specs=[VMEM] * 3,
        out_specs=[VMEM] * 2,
        out_shape=[jax.ShapeDtypeStruct((1, units, cols), BF16)] * 2,
        compiler_params=SMALL,
        cost_estimate=cost(8 * rows * both * cols, (*pair, turned)),
    )(*pair, turned)


def early_down(groups, turned):
    both, rows = turned.shape[1:]
    cols = groups[0][0].shape[2]
    arrays = [r for g in groups for r in g]

    def kernel(*refs):
        ins, t, sums = refs[:-2], refs[-2], refs[-1]
        for i in range(2):
            total = None
            for j in range(len(groups)):
                both_blocks = jnp.concatenate([ins[2 * j + i][0], ins[2 * j + i][1]], axis=1)
                part = jnp.dot(t[j], both_blocks, preferred_element_type=F32)
                total = part if total is None else total + part
            for k in range(2):
                sums[2 * i + k] = total[:, k * cols : (k + 1) * cols]

    return pl.pallas_call(
        kernel,
        in_specs=[VMEM] * (len(arrays) + 1),
        out_specs=VMEM,
        out_shape=jax.ShapeDtypeStruct((4, both, cols), F32),
        compiler_params=LIMIT,
        cost_estimate=cost(8 * len(groups) * rows * both * cols, (*arrays, turned)),
    )(*arrays, turned)


def last_down(sums, a_pair, b_pair, turned, after):
    both, rows = turned.shape[1:]
    units = both // 2
    cols = a_pair[0].shape[2]

    def kernel(sums, a1, a2, b1, b2, t, _, own, other):
        def put(k, total):
            other[k] = total[units:].astype(BF16)
            own[k] = total[:units].astype(BF16)

        for i, a in enumerate((a1, a2)):
            both_blocks = jnp.concatenate([a[0], a[1]], axis=1)
            part = jnp.dot(t[3], both_blocks, preferred_element_type=F32)
            for k in range(2):
                put(2 * i + k, sums[2 * i + k] + part[:, k * cols : (k + 1) * cols])
        total = None
        for i, b in enumerate((b1, b2)):
            turned_pair = jnp.concatenate([t[2 * i], t[2 * i + 1]], axis=1)
            part = jnp.dot(turned_pair, b[...].reshape(2 * rows, cols), preferred_element_type=F32)
            total = part if total is None else total + part
        put(4, total)

    operands = [sums, *a_pair, *b_pair, turned, after]
    return pl.pallas_call(
        kernel,
        in_specs=[VMEM] * 6 + [ANY],
        out_specs=[VMEM] * 2,
        out_shape=[jax.ShapeDtypeStruct((5, units, cols), BF16)] * 2,
        compiler_params=LIMIT,
        cost_estimate=cost(16 * rows * both * cols, operands),
    )(*operands)


def gather_down(width, pieces):
    blocks = [p[0] for p in pieces]
    count = sum(len(p[2]) for p in pieces)
    units, cols = blocks[0].shape[1:]

    def kernel(*refs):
        ins, out = refs[: len(blocks)], refs[len(blocks)]
        bufs, in_sems, out_sems = refs[len(blocks) + 1 :]
        copies, stores, places = [], [], []
        for ref, (_, crossed, keys) in zip(ins, pieces):
            core = 1 - this_core() if crossed else this_core()
            for k, key in enumerate(keys):
                i = len(copies)
                places.append(column_place(key[0], key[1], core))
                copies.append(pltpu.make_async_copy(ref.at[k], bufs.at[i], in_sems.at[i]))
                copies[-1].start()
        for i in range(count):
            copies[i].wait()
            stores.append(
                pltpu.make_async_copy(bufs.at[i], columns(out, places[i], cols), out_sems.at[i])
            )
            stores[-1].start()
        for c in stores:
            c.wait()

    return pl.pallas_call(
        kernel,
        in_specs=[ANY] * len(blocks),
        out_specs=HBM,
        out_shape=jax.ShapeDtypeStruct((units, width), BF16),
        scratch_shapes=[
            pltpu.VMEM((count, units, cols), BF16),
            pltpu.SemaphoreType.DMA((count,)),
            pltpu.SemaphoreType.DMA((count,)),
        ],
        compiler_params=SMALL,
        cost_estimate=cost(0, (*blocks, *blocks)),
    )(*blocks)


def per_device(grad_out, routes, combine, saved_hidden, down_weight):
    n_expert = lax.axis_size("expert")
    n_rep = lax.axis_size("dp")
    n_x = lax.axis_size("x")
    capacity = saved_hidden.shape[2]
    width = grad_out.shape[1]
    most = capacity // n_expert
    cols = width // (4 * n_x)
    weight, hidden = down_weight[0], saved_hidden[:, 0]

    def along_x(v, by):
        return lax.ppermute(v, "x", [(i, (i + by) % n_x) for i in range(n_x)])

    def along_y(v, by):
        return lax.ppermute(v, "dp", [(p, (p + by) % n_rep) for p in range(n_rep)])

    def to_core(v):
        return lax.ppermute(v, "core", [(0, 1), (1, 0)])

    sent, crossed = to_core(weight), to_core(hidden)
    rows, target = pick(routes.T, combine.T, grad_out, cols, capacity, most)
    got = lax.all_to_all(
        rows.reshape(n_expert, most, 2 * cols), "expert", split_axis=0, concat_axis=0, tiled=True
    ).reshape(capacity, 2 * cols)
    sent, crossed, token = settled(sent, crossed, place=HBM)
    got, _ = fence(got, token)

    a, b = got[:, :cols], got[:, cols:]
    al, ar = along_x(a, 1), along_x(a, -1)
    bd, bu = along_y(b, 1), along_y(b, -1)
    a_far, b_far = along_x(al, 1), along_y(bd, 1)
    met = to_core(arrived(al, bd))
    a1, a1p, b1, b1p = stack(2, (a, al), (b, bd), after=(ar, bu, met))
    u1, r1 = along_y(a1, -1), along_x(b1, -1)
    b_far, a1p = fence(b_far, a1p)
    a_far, b1p = fence(a_far, b1p)
    d1, l1 = along_y(a1p, 1), along_x(b1p, 1)
    a2, a2p, a2m, b2, b2p, b2m = stack(3, (ar, a_far), (bu, b_far))
    turned = turn(hidden, crossed)
    blocks, crossed_blocks, held = fetch(weight, sent, hidden, cols)
    g0, g0c = first_down((b1, b2), turned)
    r1, b2m = fence(r1, b2m)
    u1, a2m = fence(u1, a2m)
    l1, b2p = fence(l1, b2p)
    d1, a2p, g0, g0c, blocks = fence(d1, a2p, g0, g0c, blocks)
    d2, u2, l2, r2 = along_y(a2p, 1), along_y(a2m, -1), along_x(b2p, 1), along_x(b2m, -1)
    own, other = absorb(
        blocks,
        (),
        [
            (0, 0, 0, a1, True),
            (0, 0, 1, a2, True),
            (1, 0, 0, b1, True),
            (1, 0, 1, b2, True),
            (0, 1, 0, d1, True),
            (0, 2, 0, u1, True),
            (1, 1, 0, l1, True),
            (1, 2, 0, r1, True),
        ],
    )
    r1, r2, own = fence(r1, r2, own)
    u1, u2, own = fence(u1, u2, own)
    l1, l2, own = fence(l1, l2, own)
    d1, d2, own, other = fence(d1, d2, own, other)
    o1, o2, q1, q2 = along_y(d1, 1), along_y(u2, -1), along_x(l1, 1), along_x(r2, -1)
    own, other, g1, g1c = absorb(
        blocks,
        ((own,), (other,)),
        [
            (0, 1, 1, d2, True),
            (0, 2, 1, u2, True),
            (1, 1, 1, l2, True),
            (1, 2, 1, r2, True),
            (1, 1, 0, l1, False),
            (1, 2, 0, r1, False),
        ],
        turned=turned,
        downs=(1, 2),
        kinds=(F32, BF16),
    )
    sums = early_down([(a1, a2), (d1, d2), (u1, u2)], turned)
    other, o1, o2, q1, q2, sums, token = settled(other, o1, o2, q1, q2, sums)
    before = to_core(other)
    last = [(0, 3, 0, o1, True), (0, 3, 1, o2, True), (1, 3, 0, q1, True), (1, 3, 1, q2, True)]
    crossing = [(*part[:3], to_core(part[3]), True) for part in last]
    g2, g2c = last_down(sums, (o1, o2), (q1, q2), turned, to_core(token))
    (own,) = absorb(blocks, ((own, before),), last, sides=(0,))
    grad_hidden, partial = absorb(
        crossed_blocks, ((own,),), crossing, sides=(0,), crossed=True, hidden=held, after=g2
    )
    partial, g0c, g1c, g2c = fence(partial, g0c, g1c, g2c)
    returned = lax.all_to_all(
        partial.reshape(-1, 1, most),
        ("dp", "expert", "x", "core"),
        split_axis=0,
        concat_axis=0,
        tiled=True,
    )
    first, later, final = [(0, 1)], [(1, 1), (2, 1)], [(0, 0), (1, 0), (2, 0), (3, 0), (3, 1)]
    grad_down = gather_down(
        width,
        [
            (g0, False, first),
            (g1, False, later),
            (g2, False, final),
            (to_core(g0c), True, first),
            (to_core(g1c), True, later),
            (to_core(g2c), True, final),
        ],
    )
    returned, grad_down = fence(returned, grad_down)
    whole = jnp.sum(returned.reshape(n_rep, n_expert, 2 * n_x, most), axis=(0, 2)).reshape(-1)
    slot = jnp.arange(capacity, dtype=jnp.int32).astype(F32)
    chosen = target[:, None] == slot[None, :, None]
    grad_combine = jnp.sum(jnp.where(chosen, whole[None, :, None], 0.0), axis=1) / combine.T.astype(F32)
    return grad_hidden[:, None], grad_down[None], grad_combine.T


def solution(mesh):
    n_dp, n_expert, n_tensor = mesh.devices.shape
    split = Mesh(
        mesh.devices.reshape(n_dp, n_expert, n_tensor // 2, 2), ("dp", "expert", "x", "core")
    )
    return jax.shard_map(
        per_device,
        mesh=split,
        in_specs=(
            P(("dp", "expert"), None),
            P(("dp", "expert"), None),
            P(("dp", "expert"), None),
            P(None, "expert", None, ("dp", "x", "core")),
            P("expert", ("dp", "x", "core"), None),
        ),
        out_specs=(
            P(None, "expert", None, ("dp", "x", "core")),
            P("expert", ("dp", "x", "core"), None),
            P(("dp", "expert"), None),
        ),
        check_vma=False,
    )
```

```python
import jax
import jax.numpy as jnp
from jax import lax
from jax.experimental import pallas as pl
from jax.experimental.pallas import tpu as pltpu
from jax.sharding import Mesh
from jax.sharding import PartitionSpec as P

F32, BF16 = jnp.float32, jnp.bfloat16
LIMIT = pltpu.CompilerParams(vmem_limit_bytes=28 * 1024 * 1024)
SMALL = pltpu.CompilerParams(vmem_limit_bytes=12 * 1024 * 1024)
LARGE = pltpu.CompilerParams(vmem_limit_bytes=60 * 1024 * 1024)
ANY = pl.BlockSpec(memory_space=pl.ANY)
VMEM = pl.BlockSpec(memory_space=pltpu.VMEM)
HBM = pl.BlockSpec(memory_space=pltpu.HBM)
NT = (((1,), (1,)), ((), ()))
OFFSETS = (0, -1, 1, 2)


def like(*arrays):
    return [jax.ShapeDtypeStruct(a.shape, a.dtype) for a in arrays]


def cost(flops, arrays):
    return pl.CostEstimate(
        flops=flops,
        bytes_accessed=sum(a.size * a.dtype.itemsize for a in arrays),
        transcendentals=0,
    )


def ring_place(axis, by):
    return lax.rem(lax.axis_index(axis) + (OFFSETS[by] + 4), 4)


def column_place(k, kind, core):
    return 4 * ring_place("x", k) + 2 * kind + core


def this_core():
    return lax.axis_index("core")


def columns(ref, place, cols):
    return ref.at[:, pl.ds(pl.multiple_of(place * cols, 128), cols)]


def pick(routes, combine, grad_out, cols, slots, most):
    tokens = grad_out.shape[0]

    def kernel(routes_ref, combine_ref, grad, out_ref, target, rows, routes, combine, out, sems):
        small = [
            pltpu.make_async_copy(routes_ref, routes, sems.at[2]),
            pltpu.make_async_copy(combine_ref, combine, sems.at[3]),
        ]
        for c in small:
            c.start()
        copies = [
            pltpu.make_async_copy(
                columns(grad, column_place(0, kind, this_core()), cols), rows.at[kind], sems.at[kind]
            )
            for kind in range(2)
        ]
        for c in copies:
            c.start()
        for c in small:
            c.wait()
        expert = lax.broadcasted_iota(jnp.int32, (8, tokens), 0)
        named = [routes[k : k + 1, :] for k in range(2)]
        hits = [(n == expert).astype(F32) for n in named]
        earlier = lax.broadcasted_iota(jnp.int32, (tokens, tokens), 0)
        later = lax.broadcasted_iota(jnp.int32, (tokens, tokens), 1)
        before = jnp.dot(
            (hits[0] + hits[1]).astype(BF16),
            (earlier < later).astype(F32).astype(BF16),
            preferred_element_type=F32,
        )
        slot = lax.broadcasted_iota(jnp.int32, (slots, tokens), 0).astype(F32)
        picker = None
        for k in range(2):
            rank = jnp.sum(hits[k] * before, axis=0, keepdims=True)
            where = named[k].astype(F32) * float(most) + rank
            target[k : k + 1, :] = where
            term = jnp.where(where == slot, combine[k : k + 1, :].astype(F32), 0.0)
            picker = term if picker is None else picker + term
        picker = picker.astype(BF16)
        stores = []
        for kind in range(2):
            copies[kind].wait()
            found = jnp.dot(picker, rows[kind], preferred_element_type=F32)
            out[kind] = found.astype(BF16)
            to = out_ref.at[:, pl.ds(kind * cols, cols)]
            stores.append(pltpu.make_async_copy(out.at[kind], to, sems.at[4 + kind]))
            stores[-1].start()
        for c in stores:
            c.wait()

    return pl.pallas_call(
        kernel,
        in_specs=[HBM, HBM, HBM],
        out_specs=[HBM, VMEM],
        out_shape=[
            jax.ShapeDtypeStruct((slots, 2 * cols), BF16),
            jax.ShapeDtypeStruct((2, tokens), F32),
        ],
        scratch_shapes=[
            pltpu.VMEM((2, tokens, cols), BF16),
            pltpu.VMEM(routes.shape, routes.dtype),
            pltpu.VMEM(combine.shape, combine.dtype),
            pltpu.VMEM((2, slots, cols), BF16),
            pltpu.SemaphoreType.DMA((6,)),
        ],
        compiler_params=LARGE,
        cost_estimate=pl.CostEstimate(
            flops=4 * tokens * slots * cols, bytes_accessed=8 * slots * cols, transcendentals=0
        ),
    )(routes, combine, grad_out)


def turn(hidden, crossed):
    n_rep, slots, units = hidden.shape

    def kernel(hidden, crossed, turned, held, sems):
        copies = []
        for j in range(4):
            for i, ref in enumerate((hidden, crossed)):
                copies.append(
                    pltpu.make_async_copy(
                        ref.at[ring_place("dp", j)], held.at[j, i], sems.at[2 * j + i]
                    )
                )
                copies[-1].start()
        for j in range(4):
            for i in range(2):
                copies[2 * j + i].wait()
                turned[j, i * units : (i + 1) * units] = held[j, i].astype(F32).T.astype(BF16)

    return pl.pallas_call(
        kernel,
        in_specs=[HBM, HBM],
        out_specs=VMEM,
        out_shape=jax.ShapeDtypeStruct((4, 2 * units, slots), BF16),
        scratch_shapes=[pltpu.VMEM((4, 2, slots, units), BF16), pltpu.SemaphoreType.DMA((8,))],
        compiler_params=SMALL,
        cost_estimate=cost(0, (hidden, hidden, hidden, hidden)),
    )(hidden, crossed)


LAST_KEYS = ((0, 0), (1, 0), (2, 0), (3, 0), (3, 1))


def fetch(weight, sent, hidden, cols):
    units = weight.shape[0]

    def kernel(weight, sent, hidden, own, crossed, held, sems):
        copies = []

        def start(src, dst):
            copies.append(pltpu.make_async_copy(src, dst, sems.at[len(copies)]))
            copies[-1].start()

        for k in range(4):
            for kind in range(2):
                place = column_place(k, kind, this_core())
                for side, ref in enumerate((weight, sent)):
                    to = own.at[2 * k + kind, pl.ds(side * units, units)]
                    start(columns(ref, place, cols), to)
        for i, (k, kind) in enumerate(LAST_KEYS):
            start(columns(weight, column_place(k, kind, 1 - this_core()), cols), crossed.at[i])
        for j in range(4):
            start(hidden.at[ring_place("dp", j)], held.at[j])
        for c in copies:
            c.wait()

    return pl.pallas_call(
        kernel,
        in_specs=[HBM] * 3,
        out_specs=[VMEM] * 3,
        out_shape=[
            jax.ShapeDtypeStruct((8, 2 * units, cols), BF16),
            jax.ShapeDtypeStruct((5, units, cols), BF16),
            jax.ShapeDtypeStruct(hidden.shape, BF16),
        ],
        scratch_shapes=[pltpu.SemaphoreType.DMA((25,))],
        compiler_params=SMALL,
        cost_estimate=cost(0, (weight, weight, hidden)),
    )(weight, sent, hidden)


def fence(*arrays):
    return pl.pallas_call(
        lambda *refs: None,
        out_shape=like(*arrays),
        in_specs=[ANY] * len(arrays),
        out_specs=[ANY] * len(arrays),
        input_output_aliases={i: i for i in range(len(arrays))},
        compiler_params=pltpu.CompilerParams(
            has_side_effects=True, vmem_limit_bytes=1024 * 1024
        ),
    )(*arrays)


def settled(*arrays, place=ANY):
    def kernel(*refs):
        refs[-1][...] = jnp.zeros_like(refs[-1])

    n = len(arrays)
    return pl.pallas_call(
        kernel,
        out_shape=like(*arrays) + [jax.ShapeDtypeStruct((8, 128), F32)],
        in_specs=[place] * n,
        out_specs=[place] * n + [VMEM],
        input_output_aliases={i: i for i in range(n)},
        compiler_params=pltpu.CompilerParams(vmem_limit_bytes=1024 * 1024),
    )(*arrays)


def arrived(*arrays):
    def kernel(*refs):
        refs[-1][...] = jnp.zeros_like(refs[-1])

    return pl.pallas_call(
        kernel,
        out_shape=jax.ShapeDtypeStruct((8, 128), F32),
        in_specs=[ANY] * len(arrays),
        out_specs=VMEM,
        compiler_params=pltpu.CompilerParams(vmem_limit_bytes=1024 * 1024),
    )(*arrays)


def stack(copies, *pairs, after=()):
    rows, cols = pairs[0][0].shape
    ins = [a for pair in pairs for a in pair]
    n = len(pairs)

    def kernel(*refs):
        outs, sems = refs[2 * n + len(after) : -1], refs[-1]
        started = []
        for i in range(n):
            for out in outs[i * copies : (i + 1) * copies]:
                for k in range(2):
                    started.append(
                        pltpu.make_async_copy(refs[2 * i + k], out.at[k], sems.at[len(started)])
                    )
                    started[-1].start()
        for c in started:
            c.wait()

    return pl.pallas_call(
        kernel,
        in_specs=[ANY] * (2 * n + len(after)),
        out_specs=[VMEM] * (n * copies),
        out_shape=[jax.ShapeDtypeStruct((2, rows, cols), BF16)] * (n * copies),
        scratch_shapes=[pltpu.SemaphoreType.DMA((2 * n * copies,))],
        compiler_params=SMALL,
    )(*ins, *after)


def absorb(weight, before, parts, sides=(0, 1), crossed=False, turned=None, downs=(), kinds=(F32, F32), hidden=None, after=None):
    arrays = [p[3] for p in parts]
    used = [i for i, p in enumerate(parts) if p[4]]

    def keys_of(i):
        what, off, pair = parts[i][:3]
        return [(2 * pair, 0), (2 * pair + 1, 0)] if what == 0 else [(off, 1)] * 2

    def block(ref, key):
        if crossed:
            return ref[LAST_KEYS.index(key)]
        return ref[2 * key[0] + key[1], sides[0] * units : (sides[-1] + 1) * units]

    n, s = len(arrays), len(sides)
    rows, cols = arrays[0].shape[1:]
    units = rows
    olds = [a for side in before for a in side]
    n_old = [len(side) for side in before]
    turned = [] if turned is None else [turned]
    last = [] if hidden is None else [hidden]
    extra = [] if after is None else [after]
    operands = arrays + [weight] + turned + olds + last + extra
    n_sum = 2 if last else s
    n_out = n_sum + (2 if downs else 0)

    def kernel(*refs):
        refs = list(refs)

        def take(count):
            taken = refs[:count]
            del refs[:count]
            return taken

        bufs, (w_ref,) = take(n), take(1)
        t, held, hid_ref = take(len(turned)), take(len(olds)), take(len(last))
        take(len(extra))
        outs = take(n_out)
        rounded, sems = take(2) if last else (None, None)
        started = []

        def start(src, dst):
            copy = pltpu.make_async_copy(src, dst, sems.at[len(started)])
            copy.start()
            started.append(copy)
            return copy

        def of(j):
            return [
                (i, k, key)
                for i in used
                for k, key in enumerate(keys_of(i))
                if (parts[i][1] if parts[i][0] == 0 else 2 * parts[i][2] + k) == j
            ]

        stores = []
        for g, off in enumerate(downs):
            down = None
            for i, part in enumerate(parts):
                if part[0] == 1 and part[1] == off:
                    at = 2 * part[2]
                    term = jnp.dot(
                        jnp.concatenate([t[0][at], t[0][at + 1]], axis=1),
                        bufs[i][...].reshape(2 * rows, cols),
                        preferred_element_type=F32,
                    )
                    down = term if down is None else down + term
            for side in range(2):
                outs[n_sum + side][g] = down[side * units : (side + 1) * units].astype(BF16)
        for j in range(4):
            total = None
            for i, k, key in of(j):
                term = lax.dot_general(
                    bufs[i][k], block(w_ref, key), NT, preferred_element_type=F32
                )
                total = term if total is None else total + term
            at = 0
            for where in range(s):
                mine = None if total is None else total[:, where * units : (where + 1) * units]
                for h in held[at : at + (n_old[where] if n_old else 0)]:
                    old = h[j].astype(F32)
                    mine = old if mine is None else mine + old
                at += n_old[where] if n_old else 0
                if last:
                    place = ring_place("dp", j)
                    rounded[j] = mine.astype(BF16)
                    stores.append(start(rounded.at[j], outs[0].at[place]))
                    prod = mine * hid_ref[0][j].astype(F32)
                    folded = sum(prod[:, c : c + 128] for c in range(0, units, 128))
                    row = jnp.sum(folded.T, axis=0, keepdims=True)
                    for q in range(8):
                        piece = row[:, q * (rows // 8) : (q + 1) * (rows // 8)]
                        outs[1][place, q] = jnp.broadcast_to(piece, (8, rows // 8))
                else:
                    outs[where][j] = mine.astype(kinds[where])
        for c in stores:
            c.wait()

    if last:
        out_shape = [
            jax.ShapeDtypeStruct((4, rows, units), BF16),
            jax.ShapeDtypeStruct((4, 8, 8, rows // 8), F32),
        ]
        out_specs = [HBM, VMEM]
    else:
        out_shape = [jax.ShapeDtypeStruct((4, rows, units), kinds[i]) for i in range(s)]
        out_specs = [VMEM] * s
    if downs:
        out_shape += [jax.ShapeDtypeStruct((len(downs), units, cols), BF16)] * 2
        out_specs = out_specs + [VMEM] * 2
    scratch = [pltpu.VMEM((4, rows, units), BF16), pltpu.SemaphoreType.DMA((4,))] if last else []
    flops = 4 * rows * cols * units * (s * len(used) + 2 * 2 * len(downs))
    return pl.pallas_call(
        kernel,
        in_specs=[VMEM] * (len(operands) - len(extra)) + [ANY] * len(extra),
        out_specs=out_specs,
        out_shape=out_shape,
        scratch_shapes=scratch,
        compiler_params=LIMIT,
        cost_estimate=cost(flops, operands),
    )(*operands)


def first_down(pair, turned):
    both, rows = turned.shape[1:]
    units, cols = both // 2, pair[0].shape[2]

    def kernel(first, second, t, own, other):
        total = None
        for j in range(4):
            part = jnp.dot(t[j], (first, second)[j // 2][j % 2], preferred_element_type=F32)
            total = part if total is None else total + part
        own[0] = total[:units].astype(BF16)
        other[0] = total[units:].astype(BF16)

    return pl.pallas_call(
        kernel,
        in_specs=[VMEM] * 3,
        out_specs=[VMEM] * 2,
        out_shape=[jax.ShapeDtypeStruct((1, units, cols), BF16)] * 2,
        compiler_params=SMALL,
        cost_estimate=cost(8 * rows * both * cols, (*pair, turned)),
    )(*pair, turned)


def early_down(groups, turned):
    both, rows = turned.shape[1:]
    cols = groups[0][0].shape[2]
    arrays = [r for g in groups for r in g]

    def kernel(*refs):
        ins, t, sums = refs[:-2], refs[-2], refs[-1]
        for i in range(2):
            total = None
            for j in range(len(groups)):
                both_blocks = jnp.concatenate([ins[2 * j + i][0], ins[2 * j + i][1]], axis=1)
                part = jnp.dot(t[j], both_blocks, preferred_element_type=F32)
                total = part if total is None else total + part
            for k in range(2):
                sums[2 * i + k] = total[:, k * cols : (k + 1) * cols]

    return pl.pallas_call(
        kernel,
        in_specs=[VMEM] * (len(arrays) + 1),
        out_specs=VMEM,
        out_shape=jax.ShapeDtypeStruct((4, both, cols), F32),
        compiler_params=LIMIT,
        cost_estimate=cost(8 * len(groups) * rows * both * cols, (*arrays, turned)),
    )(*arrays, turned)


def last_down(sums, a_pair, b_pair, turned, early, after):
    both, rows = turned.shape[1:]
    units = both // 2
    cols = a_pair[0].shape[2]

    def kernel(sums, a1, a2, b1, b2, t, early1, early2, _, own, other):
        other[0] = early1[0]
        other[1:3] = early2[...]

        def put(k, total):
            other[3 + k] = total[units:].astype(BF16)
            own[k] = total[:units].astype(BF16)

        for i, a in enumerate((a1, a2)):
            both_blocks = jnp.concatenate([a[0], a[1]], axis=1)
            part = jnp.dot(t[3], both_blocks, preferred_element_type=F32)
            for k in range(2):
                put(2 * i + k, sums[2 * i + k] + part[:, k * cols : (k + 1) * cols])
        total = None
        for i, b in enumerate((b1, b2)):
            turned_pair = jnp.concatenate([t[2 * i], t[2 * i + 1]], axis=1)
            part = jnp.dot(turned_pair, b[...].reshape(2 * rows, cols), preferred_element_type=F32)
            total = part if total is None else total + part
        put(4, total)

    operands = [sums, *a_pair, *b_pair, turned, *early, after]
    return pl.pallas_call(
        kernel,
        in_specs=[VMEM] * 8 + [ANY],
        out_specs=[VMEM] * 2,
        out_shape=[jax.ShapeDtypeStruct((n, units, cols), BF16) for n in (5, 8)],
        compiler_params=LIMIT,
        cost_estimate=cost(16 * rows * both * cols, operands),
    )(*operands)


def gather_down(width, pieces):
    blocks = [p[0] for p in pieces]
    count = sum(len(p[2]) for p in pieces)
    units, cols = blocks[0].shape[1:]

    def kernel(*refs):
        ins, out = refs[: len(blocks)], refs[len(blocks)]
        bufs, in_sems, out_sems = refs[len(blocks) + 1 :]
        copies, stores, places = [], [], []
        for ref, (_, crossed, keys) in zip(ins, pieces):
            core = 1 - this_core() if crossed else this_core()
            for k, key in enumerate(keys):
                i = len(copies)
                places.append(column_place(key[0], key[1], core))
                copies.append(pltpu.make_async_copy(ref.at[k], bufs.at[i], in_sems.at[i]))
                copies[-1].start()
        for i in range(count):
            copies[i].wait()
            stores.append(
                pltpu.make_async_copy(bufs.at[i], columns(out, places[i], cols), out_sems.at[i])
            )
            stores[-1].start()
        for c in stores:
            c.wait()

    return pl.pallas_call(
        kernel,
        in_specs=[ANY] * len(blocks),
        out_specs=HBM,
        out_shape=jax.ShapeDtypeStruct((units, width), BF16),
        scratch_shapes=[
            pltpu.VMEM((count, units, cols), BF16),
            pltpu.SemaphoreType.DMA((count,)),
            pltpu.SemaphoreType.DMA((count,)),
        ],
        compiler_params=SMALL,
        cost_estimate=cost(0, (*blocks, *blocks)),
    )(*blocks)


def per_device(grad_out, routes, combine, saved_hidden, down_weight):
    n_expert = lax.axis_size("expert")
    n_rep = lax.axis_size("dp")
    n_x = lax.axis_size("x")
    capacity = saved_hidden.shape[2]
    width = grad_out.shape[1]
    most = capacity // n_expert
    cols = width // (4 * n_x)
    weight, hidden = down_weight[0], saved_hidden[:, 0]

    def along_x(v, by):
        return lax.ppermute(v, "x", [(i, (i + by) % n_x) for i in range(n_x)])

    def along_y(v, by):
        return lax.ppermute(v, "dp", [(p, (p + by) % n_rep) for p in range(n_rep)])

    def to_core(v):
        return lax.ppermute(v, "core", [(0, 1), (1, 0)])

    sent, crossed = to_core(weight), to_core(hidden)
    rows, target = pick(routes.T, combine.T, grad_out, cols, capacity, most)
    got = lax.all_to_all(
        rows.reshape(n_expert, most, 2 * cols), "expert", split_axis=0, concat_axis=0, tiled=True
    ).reshape(capacity, 2 * cols)
    sent, crossed, token = settled(sent, crossed, place=HBM)
    got, _ = fence(got, token)

    a, b = got[:, :cols], got[:, cols:]
    al, ar = along_x(a, 1), along_x(a, -1)
    bd, bu = along_y(b, 1), along_y(b, -1)
    a_far, b_far = along_x(al, 1), along_y(bd, 1)
    met = to_core(arrived(al, bd))
    a1, a1p, b1, b1p = stack(2, (a, al), (b, bd), after=(ar, bu, met))
    u1, r1 = along_y(a1, -1), along_x(b1, -1)
    b_far, a1p = fence(b_far, a1p)
    a_far, b1p = fence(a_far, b1p)
    d1, l1 = along_y(a1p, 1), along_x(b1p, 1)
    a2, a2p, a2m, b2, b2p, b2m = stack(3, (ar, a_far), (bu, b_far))
    turned = turn(hidden, crossed)
    blocks, crossed_blocks, held = fetch(weight, sent, hidden, cols)
    g0, g0c = first_down((b1, b2), turned)
    r1, b2m = fence(r1, b2m)
    u1, a2m = fence(u1, a2m)
    l1, b2p = fence(l1, b2p)
    d1, a2p, g0, g0c, blocks = fence(d1, a2p, g0, g0c, blocks)
    d2, u2, l2, r2 = along_y(a2p, 1), along_y(a2m, -1), along_x(b2p, 1), along_x(b2m, -1)
    own, other = absorb(
        blocks,
        (),
        [
            (0, 0, 0, a1, True),
            (0, 0, 1, a2, True),
            (1, 0, 0, b1, True),
            (1, 0, 1, b2, True),
            (0, 1, 0, d1, True),
            (0, 2, 0, u1, True),
            (1, 1, 0, l1, True),
            (1, 2, 0, r1, True),
        ],
    )
    r1, r2, own = fence(r1, r2, own)
    u1, u2, own = fence(u1, u2, own)
    l1, l2, own = fence(l1, l2, own)
    d1, d2, own, other = fence(d1, d2, own, other)
    o1, o2, q1, q2 = along_y(d1, 1), along_y(u2, -1), along_x(l1, 1), along_x(r2, -1)
    own, other, g1, g1c = absorb(
        blocks,
        ((own,), (other,)),
        [
            (0, 1, 1, d2, True),
            (0, 2, 1, u2, True),
            (1, 1, 1, l2, True),
            (1, 2, 1, r2, True),
            (1, 1, 0, l1, False),
            (1, 2, 0, r1, False),
        ],
        turned=turned,
        downs=(1, 2),
        kinds=(F32, BF16),
    )
    sums = early_down([(a1, a2), (d1, d2), (u1, u2)], turned)
    other, o1, o2, q1, q2, sums, token = settled(other, o1, o2, q1, q2, sums)
    before = to_core(other)
    last = [(0, 3, 0, o1, True), (0, 3, 1, o2, True), (1, 3, 0, q1, True), (1, 3, 1, q2, True)]
    crossing = [(*part[:3], to_core(part[3]), True) for part in last]
    g2, g2c = last_down(sums, (o1, o2), (q1, q2), turned, (g0c, g1c), to_core(token))
    (own,) = absorb(blocks, ((own, before),), last, sides=(0,))
    grad_hidden, partial = absorb(
        crossed_blocks, ((own,),), crossing, sides=(0,), crossed=True, hidden=held, after=g2
    )
    partial, g2c = fence(partial, g2c)
    returned = lax.all_to_all(
        partial.reshape(-1, 1, most),
        ("dp", "expert", "x", "core"),
        split_axis=0,
        concat_axis=0,
        tiled=True,
    )
    first, later, final = [(0, 1)], [(1, 1), (2, 1)], [(0, 0), (1, 0), (2, 0), (3, 0), (3, 1)]
    grad_down = gather_down(
        width,
        [
            (g0, False, first),
            (g1, False, later),
            (g2, False, final),
            (to_core(g2c), True, first + later + final),
        ],
    )
    returned, grad_down = fence(returned, grad_down)
    whole = jnp.sum(returned.reshape(n_rep, n_expert, 2 * n_x, most), axis=(0, 2)).reshape(-1)
    slot = jnp.arange(capacity, dtype=jnp.int32).astype(F32)
    chosen = target[:, None] == slot[None, :, None]
    grad_combine = jnp.sum(jnp.where(chosen, whole[None, :, None], 0.0), axis=1) / combine.T.astype(F32)
    return grad_hidden[:, None], grad_down[None], grad_combine.T


def solution(mesh):
    n_dp, n_expert, n_tensor = mesh.devices.shape
    split = Mesh(
        mesh.devices.reshape(n_dp, n_expert, n_tensor // 2, 2), ("dp", "expert", "x", "core")
    )
    return jax.shard_map(
        per_device,
        mesh=split,
        in_specs=(
            P(("dp", "expert"), None),
            P(("dp", "expert"), None),
            P(("dp", "expert"), None),
            P(None, "expert", None, ("dp", "x", "core")),
            P("expert", ("dp", "x", "core"), None),
        ),
        out_specs=(
            P(None, "expert", None, ("dp", "x", "core")),
            P("expert", ("dp", "x", "core"), None),
            P(("dp", "expert"), None),
        ),
        check_vma=False,
    )
```

```python
import jax
import jax.numpy as jnp
from jax import lax
from jax.experimental import pallas as pl
from jax.experimental.pallas import tpu as pltpu
from jax.sharding import Mesh
from jax.sharding import PartitionSpec as P

F32, BF16 = jnp.float32, jnp.bfloat16
LIMIT = pltpu.CompilerParams(vmem_limit_bytes=28 * 1024 * 1024)
SMALL = pltpu.CompilerParams(vmem_limit_bytes=12 * 1024 * 1024)
LARGE = pltpu.CompilerParams(vmem_limit_bytes=60 * 1024 * 1024)
ANY = pl.BlockSpec(memory_space=pl.ANY)
VMEM = pl.BlockSpec(memory_space=pltpu.VMEM)
HBM = pl.BlockSpec(memory_space=pltpu.HBM)
NT = (((1,), (1,)), ((), ()))
OFFSETS = (0, -1, 1, 2)


def like(*arrays):
    return [jax.ShapeDtypeStruct(a.shape, a.dtype) for a in arrays]


def cost(flops, arrays):
    return pl.CostEstimate(
        flops=flops,
        bytes_accessed=sum(a.size * a.dtype.itemsize for a in arrays),
        transcendentals=0,
    )


def ring_place(axis, by):
    return lax.rem(lax.axis_index(axis) + (OFFSETS[by] + 4), 4)


def column_place(k, kind, core):
    return 4 * ring_place("x", k) + 2 * kind + core


def this_core():
    return lax.axis_index("core")


def columns(ref, place, cols):
    return ref.at[:, pl.ds(pl.multiple_of(place * cols, 128), cols)]


def pick(routes, combine, grad_out, cols, slots, most):
    tokens = grad_out.shape[0]

    def kernel(routes_ref, combine_ref, grad, out_ref, target, rows, routes, combine, out, sems):
        small = [
            pltpu.make_async_copy(routes_ref, routes, sems.at[2]),
            pltpu.make_async_copy(combine_ref, combine, sems.at[3]),
        ]
        for c in small:
            c.start()
        copies = [
            pltpu.make_async_copy(
                columns(grad, column_place(0, kind, this_core()), cols), rows.at[kind], sems.at[kind]
            )
            for kind in range(2)
        ]
        for c in copies:
            c.start()
        for c in small:
            c.wait()
        expert = lax.broadcasted_iota(jnp.int32, (8, tokens), 0)
        named = [routes[k : k + 1, :] for k in range(2)]
        hits = [(n == expert).astype(F32) for n in named]
        earlier = lax.broadcasted_iota(jnp.int32, (tokens, tokens), 0)
        later = lax.broadcasted_iota(jnp.int32, (tokens, tokens), 1)
        before = jnp.dot(
            (hits[0] + hits[1]).astype(BF16),
            (earlier < later).astype(F32).astype(BF16),
            preferred_element_type=F32,
        )
        slot = lax.broadcasted_iota(jnp.int32, (slots, tokens), 0).astype(F32)
        picker = None
        for k in range(2):
            rank = jnp.sum(hits[k] * before, axis=0, keepdims=True)
            where = named[k].astype(F32) * float(most) + rank
            target[k : k + 1, :] = where
            term = jnp.where(where == slot, combine[k : k + 1, :].astype(F32), 0.0)
            picker = term if picker is None else picker + term
        picker = picker.astype(BF16)
        stores = []
        for kind in range(2):
            copies[kind].wait()
            found = jnp.dot(picker, rows[kind], preferred_element_type=F32)
            out[kind] = found.astype(BF16)
            to = out_ref.at[:, pl.ds(kind * cols, cols)]
            stores.append(pltpu.make_async_copy(out.at[kind], to, sems.at[4 + kind]))
            stores[-1].start()
        for c in stores:
            c.wait()

    return pl.pallas_call(
        kernel,
        in_specs=[HBM, HBM, HBM],
        out_specs=[HBM, VMEM],
        out_shape=[
            jax.ShapeDtypeStruct((slots, 2 * cols), BF16),
            jax.ShapeDtypeStruct((2, tokens), F32),
        ],
        scratch_shapes=[
            pltpu.VMEM((2, tokens, cols), BF16),
            pltpu.VMEM(routes.shape, routes.dtype),
            pltpu.VMEM(combine.shape, combine.dtype),
            pltpu.VMEM((2, slots, cols), BF16),
            pltpu.SemaphoreType.DMA((6,)),
        ],
        compiler_params=LARGE,
        cost_estimate=pl.CostEstimate(
            flops=4 * tokens * slots * cols, bytes_accessed=8 * slots * cols, transcendentals=0
        ),
    )(routes, combine, grad_out)


def turn(hidden, crossed):
    n_rep, slots, units = hidden.shape

    def kernel(hidden, crossed, turned, held, sems):
        copies = []
        for j in range(4):
            for i, ref in enumerate((hidden, crossed)):
                copies.append(
                    pltpu.make_async_copy(
                        ref.at[ring_place("dp", j)], held.at[j, i], sems.at[2 * j + i]
                    )
                )
                copies[-1].start()
        for j in range(4):
            for i in range(2):
                copies[2 * j + i].wait()
                turned[j, i * units : (i + 1) * units] = held[j, i].astype(F32).T.astype(BF16)

    return pl.pallas_call(
        kernel,
        in_specs=[HBM, HBM],
        out_specs=VMEM,
        out_shape=jax.ShapeDtypeStruct((4, 2 * units, slots), BF16),
        scratch_shapes=[pltpu.VMEM((4, 2, slots, units), BF16), pltpu.SemaphoreType.DMA((8,))],
        compiler_params=SMALL,
        cost_estimate=cost(0, (hidden, hidden, hidden, hidden)),
    )(hidden, crossed)


LAST_KEYS = ((0, 0), (1, 0), (2, 0), (3, 0), (3, 1))


def fetch(weight, sent, hidden, cols):
    units = weight.shape[0]

    def kernel(weight, sent, hidden, own, crossed, held, sems):
        copies = []

        def start(src, dst):
            copies.append(pltpu.make_async_copy(src, dst, sems.at[len(copies)]))
            copies[-1].start()

        for k in range(4):
            for kind in range(2):
                place = column_place(k, kind, this_core())
                for side, ref in enumerate((weight, sent)):
                    to = own.at[2 * k + kind, pl.ds(side * units, units)]
                    start(columns(ref, place, cols), to)
        for i, (k, kind) in enumerate(LAST_KEYS):
            start(columns(weight, column_place(k, kind, 1 - this_core()), cols), crossed.at[i])
        for j in range(4):
            start(hidden.at[ring_place("dp", j)], held.at[j])
        for c in copies:
            c.wait()

    return pl.pallas_call(
        kernel,
        in_specs=[HBM] * 3,
        out_specs=[VMEM] * 3,
        out_shape=[
            jax.ShapeDtypeStruct((8, 2 * units, cols), BF16),
            jax.ShapeDtypeStruct((5, units, cols), BF16),
            jax.ShapeDtypeStruct(hidden.shape, BF16),
        ],
        scratch_shapes=[pltpu.SemaphoreType.DMA((25,))],
        compiler_params=SMALL,
        cost_estimate=cost(0, (weight, weight, hidden)),
    )(weight, sent, hidden)


def fence(*arrays):
    return pl.pallas_call(
        lambda *refs: None,
        out_shape=like(*arrays),
        in_specs=[ANY] * len(arrays),
        out_specs=[ANY] * len(arrays),
        input_output_aliases={i: i for i in range(len(arrays))},
        compiler_params=pltpu.CompilerParams(
            has_side_effects=True, vmem_limit_bytes=1024 * 1024
        ),
    )(*arrays)


def settled(*arrays, place=ANY):
    def kernel(*refs):
        refs[-1][...] = jnp.zeros_like(refs[-1])

    n = len(arrays)
    return pl.pallas_call(
        kernel,
        out_shape=like(*arrays) + [jax.ShapeDtypeStruct((8, 128), F32)],
        in_specs=[place] * n,
        out_specs=[place] * n + [VMEM],
        input_output_aliases={i: i for i in range(n)},
        compiler_params=pltpu.CompilerParams(vmem_limit_bytes=1024 * 1024),
    )(*arrays)


def arrived(*arrays):
    def kernel(*refs):
        refs[-1][...] = jnp.zeros_like(refs[-1])

    return pl.pallas_call(
        kernel,
        out_shape=jax.ShapeDtypeStruct((8, 128), F32),
        in_specs=[ANY] * len(arrays),
        out_specs=VMEM,
        compiler_params=pltpu.CompilerParams(vmem_limit_bytes=1024 * 1024),
    )(*arrays)


def stack(copies, *pairs, after=()):
    rows, cols = pairs[0][0].shape
    ins = [a for pair in pairs for a in pair]
    n = len(pairs)

    def kernel(*refs):
        outs, sems = refs[2 * n + len(after) : -1], refs[-1]
        started = []
        for i in range(n):
            for out in outs[i * copies : (i + 1) * copies]:
                for k in range(2):
                    started.append(
                        pltpu.make_async_copy(refs[2 * i + k], out.at[k], sems.at[len(started)])
                    )
                    started[-1].start()
        for c in started:
            c.wait()

    return pl.pallas_call(
        kernel,
        in_specs=[ANY] * (2 * n + len(after)),
        out_specs=[VMEM] * (n * copies),
        out_shape=[jax.ShapeDtypeStruct((2, rows, cols), BF16)] * (n * copies),
        scratch_shapes=[pltpu.SemaphoreType.DMA((2 * n * copies,))],
        compiler_params=SMALL,
    )(*ins, *after)


def absorb(weight, before, parts, sides=(0, 1), crossed=False, turned=None, downs=(), kinds=(F32, F32), hidden=None, after=None):
    arrays = [p[3] for p in parts]
    used = [i for i, p in enumerate(parts) if p[4]]

    def keys_of(i):
        what, off, pair = parts[i][:3]
        return [(2 * pair, 0), (2 * pair + 1, 0)] if what == 0 else [(off, 1)] * 2

    def block(ref, key):
        if crossed:
            return ref[LAST_KEYS.index(key)]
        return ref[2 * key[0] + key[1], sides[0] * units : (sides[-1] + 1) * units]

    n, s = len(arrays), len(sides)
    rows, cols = arrays[0].shape[1:]
    units = rows
    olds = [a for side in before for a in side]
    n_old = [len(side) for side in before]
    turned = [] if turned is None else [turned]
    last = [] if hidden is None else [hidden]
    extra = [] if after is None else [after]
    operands = arrays + [weight] + turned + olds + last + extra
    n_sum = 2 if last else s
    n_out = n_sum + (2 if downs else 0)

    def kernel(*refs):
        refs = list(refs)

        def take(count):
            taken = refs[:count]
            del refs[:count]
            return taken

        bufs, (w_ref,) = take(n), take(1)
        t, held, hid_ref = take(len(turned)), take(len(olds)), take(len(last))
        take(len(extra))
        outs = take(n_out)
        rounded, sems = take(2) if last else (None, None)
        started = []

        def start(src, dst):
            copy = pltpu.make_async_copy(src, dst, sems.at[len(started)])
            copy.start()
            started.append(copy)
            return copy

        def of(j):
            return [
                (i, k, key)
                for i in used
                for k, key in enumerate(keys_of(i))
                if (parts[i][1] if parts[i][0] == 0 else 2 * parts[i][2] + k) == j
            ]

        stores = []
        for g, off in enumerate(downs):
            down = None
            for i, part in enumerate(parts):
                if part[0] == 1 and part[1] == off:
                    at = 2 * part[2]
                    term = jnp.dot(
                        jnp.concatenate([t[0][at], t[0][at + 1]], axis=1),
                        bufs[i][...].reshape(2 * rows, cols),
                        preferred_element_type=F32,
                    )
                    down = term if down is None else down + term
            for side in range(2):
                outs[n_sum + side][g] = down[side * units : (side + 1) * units].astype(BF16)
        for j in range(4):
            total = None
            for i, k, key in of(j):
                term = lax.dot_general(
                    bufs[i][k], block(w_ref, key), NT, preferred_element_type=F32
                )
                total = term if total is None else total + term
            at = 0
            for where in range(s):
                mine = None if total is None else total[:, where * units : (where + 1) * units]
                for h in held[at : at + (n_old[where] if n_old else 0)]:
                    old = h[j].astype(F32)
                    mine = old if mine is None else mine + old
                at += n_old[where] if n_old else 0
                if last:
                    place = ring_place("dp", j)
                    rounded[j] = mine.astype(BF16)
                    stores.append(start(rounded.at[j], outs[0].at[place]))
                    prod = mine * hid_ref[0][j].astype(F32)
                    folded = sum(prod[:, c : c + 128] for c in range(0, units, 128))
                    row = jnp.sum(folded.T, axis=0, keepdims=True)
                    for q in range(8):
                        piece = row[:, q * (rows // 8) : (q + 1) * (rows // 8)]
                        outs[1][place, q] = jnp.broadcast_to(piece, (8, rows // 8))
                else:
                    outs[where][j] = mine.astype(kinds[where])
        for c in stores:
            c.wait()

    if last:
        out_shape = [
            jax.ShapeDtypeStruct((4, rows, units), BF16),
            jax.ShapeDtypeStruct((4, 8, 8, rows // 8), F32),
        ]
        out_specs = [HBM, VMEM]
    else:
        out_shape = [jax.ShapeDtypeStruct((4, rows, units), kinds[i]) for i in range(s)]
        out_specs = [VMEM] * s
    if downs:
        out_shape += [jax.ShapeDtypeStruct((len(downs), units, cols), BF16)] * 2
        out_specs = out_specs + [VMEM] * 2
    scratch = [pltpu.VMEM((4, rows, units), BF16), pltpu.SemaphoreType.DMA((4,))] if last else []
    flops = 4 * rows * cols * units * (s * len(used) + 2 * 2 * len(downs))
    return pl.pallas_call(
        kernel,
        in_specs=[VMEM] * (len(operands) - len(extra)) + [ANY] * len(extra),
        out_specs=out_specs,
        out_shape=out_shape,
        scratch_shapes=scratch,
        compiler_params=LIMIT,
        cost_estimate=cost(flops, operands),
    )(*operands)


def first_down(pair, turned):
    both, rows = turned.shape[1:]
    units, cols = both // 2, pair[0].shape[2]

    def kernel(first, second, t, own, other):
        total = None
        for j in range(4):
            part = jnp.dot(t[j], (first, second)[j // 2][j % 2], preferred_element_type=F32)
            total = part if total is None else total + part
        own[0] = total[:units].astype(BF16)
        other[0] = total[units:].astype(BF16)

    return pl.pallas_call(
        kernel,
        in_specs=[VMEM] * 3,
        out_specs=[VMEM] * 2,
        out_shape=[jax.ShapeDtypeStruct((1, units, cols), BF16)] * 2,
        compiler_params=SMALL,
        cost_estimate=cost(8 * rows * both * cols, (*pair, turned)),
    )(*pair, turned)


def early_down(groups, turned):
    both, rows = turned.shape[1:]
    cols = groups[0][0].shape[2]
    arrays = [r for g in groups for r in g]

    def kernel(*refs):
        ins, t, sums = refs[:-2], refs[-2], refs[-1]
        for i in range(2):
            total = None
            for j in range(len(groups)):
                both_blocks = jnp.concatenate([ins[2 * j + i][0], ins[2 * j + i][1]], axis=1)
                part = jnp.dot(t[j], both_blocks, preferred_element_type=F32)
                total = part if total is None else total + part
            for k in range(2):
                sums[2 * i + k] = total[:, k * cols : (k + 1) * cols]

    return pl.pallas_call(
        kernel,
        in_specs=[VMEM] * (len(arrays) + 1),
        out_specs=VMEM,
        out_shape=jax.ShapeDtypeStruct((4, both, cols), F32),
        compiler_params=LIMIT,
        cost_estimate=cost(8 * len(groups) * rows * both * cols, (*arrays, turned)),
    )(*arrays, turned)


def last_down(sums, a_pair, b_pair, turned, after):
    both, rows = turned.shape[1:]
    units = both // 2
    cols = a_pair[0].shape[2]

    def kernel(sums, a1, a2, b1, b2, t, _, own, other):
        def put(k, total):
            other[k] = total[units:].astype(BF16)
            own[k] = total[:units].astype(BF16)

        for i, a in enumerate((a1, a2)):
            both_blocks = jnp.concatenate([a[0], a[1]], axis=1)
            part = jnp.dot(t[3], both_blocks, preferred_element_type=F32)
            for k in range(2):
                put(2 * i + k, sums[2 * i + k] + part[:, k * cols : (k + 1) * cols])
        total = None
        for i, b in enumerate((b1, b2)):
            turned_pair = jnp.concatenate([t[2 * i], t[2 * i + 1]], axis=1)
            part = jnp.dot(turned_pair, b[...].reshape(2 * rows, cols), preferred_element_type=F32)
            total = part if total is None else total + part
        put(4, total)

    operands = [sums, *a_pair, *b_pair, turned, after]
    return pl.pallas_call(
        kernel,
        in_specs=[VMEM] * 6 + [ANY],
        out_specs=[VMEM] * 2,
        out_shape=[jax.ShapeDtypeStruct((5, units, cols), BF16)] * 2,
        compiler_params=LIMIT,
        cost_estimate=cost(16 * rows * both * cols, operands),
    )(*operands)


def gather_down(width, pieces):
    blocks = [p[0] for p in pieces]
    count = sum(len(p[2]) for p in pieces)
    units, cols = blocks[0].shape[1:]

    def kernel(*refs):
        ins, out = refs[: len(blocks)], refs[len(blocks)]
        bufs, in_sems, out_sems = refs[len(blocks) + 1 :]
        copies, stores, places = [], [], []
        for ref, (_, crossed, keys) in zip(ins, pieces):
            core = 1 - this_core() if crossed else this_core()
            for k, key in enumerate(keys):
                i = len(copies)
                places.append(column_place(key[0], key[1], core))
                copies.append(pltpu.make_async_copy(ref.at[k], bufs.at[i], in_sems.at[i]))
                copies[-1].start()
        for i in range(count):
            copies[i].wait()
            stores.append(
                pltpu.make_async_copy(bufs.at[i], columns(out, places[i], cols), out_sems.at[i])
            )
            stores[-1].start()
        for c in stores:
            c.wait()

    return pl.pallas_call(
        kernel,
        in_specs=[ANY] * len(blocks),
        out_specs=HBM,
        out_shape=jax.ShapeDtypeStruct((units, width), BF16),
        scratch_shapes=[
            pltpu.VMEM((count, units, cols), BF16),
            pltpu.SemaphoreType.DMA((count,)),
            pltpu.SemaphoreType.DMA((count,)),
        ],
        compiler_params=SMALL,
        cost_estimate=cost(0, (*blocks, *blocks)),
    )(*blocks)


def per_device(grad_out, routes, combine, saved_hidden, down_weight):
    n_expert = lax.axis_size("expert")
    n_rep = lax.axis_size("dp")
    n_x = lax.axis_size("x")
    capacity = saved_hidden.shape[2]
    width = grad_out.shape[1]
    most = capacity // n_expert
    cols = width // (4 * n_x)
    weight, hidden = down_weight[0], saved_hidden[:, 0]

    def along_x(v, by):
        return lax.ppermute(v, "x", [(i, (i + by) % n_x) for i in range(n_x)])

    def along_y(v, by):
        return lax.ppermute(v, "dp", [(p, (p + by) % n_rep) for p in range(n_rep)])

    def to_core(v):
        return lax.ppermute(v, "core", [(0, 1), (1, 0)])

    sent, crossed = to_core(weight), to_core(hidden)
    rows, target = pick(routes.T, combine.T, grad_out, cols, capacity, most)
    got = lax.all_to_all(
        rows.reshape(n_expert, most, 2 * cols), "expert", split_axis=0, concat_axis=0, tiled=True
    ).reshape(capacity, 2 * cols)
    sent, crossed, token = settled(sent, crossed, place=HBM)
    got, _ = fence(got, token)

    a, b = got[:, :cols], got[:, cols:]
    al, ar = along_x(a, 1), along_x(a, -1)
    bd, bu = along_y(b, 1), along_y(b, -1)
    a_far, b_far = along_x(al, 1), along_y(bd, 1)
    met = to_core(arrived(al, bd))
    a1, a1p, b1, b1p = stack(2, (a, al), (b, bd), after=(ar, bu, met))
    u1, r1 = along_y(a1, -1), along_x(b1, -1)
    b_far, a1p = fence(b_far, a1p)
    a_far, b1p = fence(a_far, b1p)
    d1, l1 = along_y(a1p, 1), along_x(b1p, 1)
    a2, a2p, a2m, b2, b2p, b2m = stack(3, (ar, a_far), (bu, b_far))
    turned = turn(hidden, crossed)
    blocks, crossed_blocks, held = fetch(weight, sent, hidden, cols)
    g0, g0c = first_down((b1, b2), turned)
    r1, b2m = fence(r1, b2m)
    u1, a2m = fence(u1, a2m)
    l1, b2p = fence(l1, b2p)
    d1, a2p, g0, g0c, blocks = fence(d1, a2p, g0, g0c, blocks)
    d2, u2, l2, r2 = along_y(a2p, 1), along_y(a2m, -1), along_x(b2p, 1), along_x(b2m, -1)
    own, other = absorb(
        blocks,
        (),
        [
            (0, 0, 0, a1, True),
            (0, 0, 1, a2, True),
            (1, 0, 0, b1, True),
            (1, 0, 1, b2, True),
            (0, 1, 0, d1, True),
            (0, 2, 0, u1, True),
            (1, 1, 0, l1, True),
            (1, 2, 0, r1, True),
        ],
    )
    r1, r2, own = fence(r1, r2, own)
    u1, u2, own = fence(u1, u2, own)
    l1, l2, own = fence(l1, l2, own)
    d1, d2, own, other = fence(d1, d2, own, other)
    o1, o2, q1, q2 = along_y(d1, 1), along_y(u2, -1), along_x(l1, 1), along_x(r2, -1)
    own, other, g1, g1c = absorb(
        blocks,
        ((own,), (other,)),
        [
            (0, 1, 1, d2, True),
            (0, 2, 1, u2, True),
            (1, 1, 1, l2, True),
            (1, 2, 1, r2, True),
            (1, 1, 0, l1, False),
            (1, 2, 0, r1, False),
        ],
        turned=turned,
        downs=(1, 2),
        kinds=(F32, BF16),
    )
    sums = early_down([(a1, a2), (d1, d2), (u1, u2)], turned)
    other, o1, o2, q1, q2, sums, token = settled(other, o1, o2, q1, q2, sums)
    before = to_core(other)
    last = [(0, 3, 0, o1, True), (0, 3, 1, o2, True), (1, 3, 0, q1, True), (1, 3, 1, q2, True)]
    crossing = [(*part[:3], to_core(part[3]), True) for part in last]
    g2, g2c = last_down(sums, (o1, o2), (q1, q2), turned, to_core(token))
    (own,) = absorb(blocks, ((own, before),), last, sides=(0,))
    grad_hidden, partial = absorb(
        crossed_blocks, ((own,),), crossing, sides=(0,), crossed=True, hidden=held, after=g2
    )
    partial, g0c, g1c, g2c = fence(partial, g0c, g1c, g2c)
    returned = lax.all_to_all(
        partial.reshape(-1, 1, most),
        ("dp", "expert", "x", "core"),
        split_axis=0,
        concat_axis=0,
        tiled=True,
    )
    first, later, final = [(0, 1)], [(1, 1), (2, 1)], [(0, 0), (1, 0), (2, 0), (3, 0), (3, 1)]
    grad_down = gather_down(
        width,
        [
            (g0, False, first),
            (g1, False, later),
            (g2, False, final),
            (to_core(g0c), True, first),
            (to_core(g1c), True, later),
            (to_core(g2c), True, final),
        ],
    )
    returned, grad_down = fence(returned, grad_down)
    whole = jnp.sum(returned.reshape(n_rep, n_expert, 2 * n_x, most), axis=(0, 2)).reshape(-1)
    slot = jnp.arange(capacity, dtype=jnp.int32).astype(F32)
    chosen = target[:, None] == slot[None, :, None]
    grad_combine = jnp.sum(jnp.where(chosen, whole[None, :, None], 0.0), axis=1) / combine.T.astype(F32)
    return grad_hidden[:, None], grad_down[None], grad_combine.T


def solution(mesh):
    n_dp, n_expert, n_tensor = mesh.devices.shape
    split = Mesh(
        mesh.devices.reshape(n_dp, n_expert, n_tensor // 2, 2), ("dp", "expert", "x", "core")
    )
    return jax.shard_map(
        per_device,
        mesh=split,
        in_specs=(
            P(("dp", "expert"), None),
            P(("dp", "expert"), None),
            P(("dp", "expert"), None),
            P(None, "expert", None, ("dp", "x", "core")),
            P("expert", ("dp", "x", "core"), None),
        ),
        out_specs=(
            P(None, "expert", None, ("dp", "x", "core")),
            P("expert", ("dp", "x", "core"), None),
            P(("dp", "expert"), None),
        ),
        check_vma=False,
    )
```
